32 devices in a mesh: rows: 16 (over z, y, core), seq: 2 (over x).
Axes of the slice: x: 2, y: 2, z: 4, core: 2. Of those that a mesh axis runs over, the one named last changes fastest.
Arguments:
- patches: bfloat16 [64, 128, 48], P('rows', 'seq'), may hold values from -6 to 6
- seg_lengths: int32 [64, 4], P('rows'), may hold values from 1 to 96, 128 in all within a row
- class_labels: int32 [64, 4], P('rows'), may hold values from 0 to 999
- cotangent: float32 [64, 128, 48], P('rows', 'seq'), may hold values from -6 to 6
- w_in: float32 [2, 48, 768], P(None, None, 'rows'), may hold values from -0.875 to 0.875
- m_in: float32 [2, 48, 768], P(None, None, 'rows'), may hold values from -16 to 16
- v_in: float32 [2, 48, 768], P(None, None, 'rows'), may hold values from 39.3216 to 155.648
- w_table: float32 [2, 1000, 768], P(None, None, 'rows'), may hold values from -6 to 6
- m_table: float32 [2, 1000, 768], P(None, None, 'rows'), may hold values from -4 to 4
- v_table: float32 [2, 1000, 768], P(None, None, 'rows'), may hold values from 0.393216 to 1.55648
- w_qkv: float32 [4, 768, 2304], P(None, 'rows'), may hold values from -0.21875 to 0.21875
- m_qkv: float32 [4, 768, 2304], P(None, 'rows'), may hold values from -4 to 4
- v_qkv: float32 [4, 768, 2304], P(None, 'rows'), may hold values from 4.34176 to 17.2032
- w_o: float32 [4, 768, 768], P(None, 'rows'), may hold values from -0.625 to 0.625
- m_o: float32 [4, 768, 768], P(None, 'rows'), may hold values from -12 to 12
- v_o: float32 [4, 768, 768], P(None, 'rows'), may hold values from 17.2032 to 68.8128
- w_up: float32 [4, 768, 3072], P(None, 'rows'), may hold values from -0.21875 to 0.21875
- m_up: float32 [4, 768, 3072], P(None, 'rows'), may hold values from -12 to 12
- v_up: float32 [4, 768, 3072], P(None, 'rows'), may hold values from 17.2032 to 68.8128
- w_down: float32 [4, 3072, 768], P(None, 'rows'), may hold values from -0.109375 to 0.109375
- m_down: float32 [4, 3072, 768], P(None, 'rows'), may hold values from -4 to 4
- v_down: float32 [4, 3072, 768], P(None, 'rows'), may hold values from 4.34176 to 17.2032
- w_out: float32 [2, 768, 96], P(None, 'rows'), may hold values from -0.0625 to 0.0625
- m_out: float32 [2, 768, 96], P(None, 'rows'), may hold values from -64 to 64
- v_out: float32 [2, 768, 96], P(None, 'rows'), may hold values from 434.176 to 1720.32
- gains: float32 [2, 5, 768], P(None, None, 'rows'), may hold values from 0.5 to 1.5
- m_gains: float32 [2, 5, 768], P(None, None, 'rows'), may hold values from -16 to 16
- v_gains: float32 [2, 5, 768], P(None, None, 'rows'), may hold values from 39.3216 to 155.648
Outputs:
- latents: float32 [64, 128, 48], P('rows', 'seq')
- logdet: float32 [64, 128], P('rows', 'seq')
- patch_grad: float32 [64, 128, 48], P('rows', 'seq')
- new_m_in: float32 [2, 48, 768], P(None, None, 'rows')
- new_v_in: float32 [2, 48, 768], P(None, None, 'rows')
- new_w_in: float32 [2, 48, 768], P(None, None, 'rows')
- new_m_table: float32 [2, 1000, 768], P(None, None, 'rows')
- new_v_table: float32 [2, 1000, 768], P(None, None, 'rows')
- new_w_table: float32 [2, 1000, 768], P(None, None, 'rows')
- new_m_qkv: float32 [4, 768, 2304], P(None, 'rows')
- new_v_qkv: float32 [4, 768, 2304], P(None, 'rows')
- new_w_qkv: float32 [4, 768, 2304], P(None, 'rows')
- new_m_o: float32 [4, 768, 768], P(None, 'rows')
- new_v_o: float32 [4, 768, 768], P(None, 'rows')
- new_w_o: float32 [4, 768, 768], P(None, 'rows')
- new_m_up: float32 [4, 768, 3072], P(None, 'rows')
- new_v_up: float32 [4, 768, 3072], P(None, 'rows')
- new_w_up: float32 [4, 768, 3072], P(None, 'rows')
- new_m_down: float32 [4, 3072, 768], P(None, 'rows')
- new_v_down: float32 [4, 3072, 768], P(None, 'rows')
- new_w_down: float32 [4, 3072, 768], P(None, 'rows')
- new_m_out: float32 [2, 768, 96], P(None, 'rows')
- new_v_out: float32 [2, 768, 96], P(None, 'rows')
- new_w_out: float32 [2, 768, 96], P(None, 'rows')
- new_m_gains: float32 [2, 5, 768], P(None, None, 'rows')
- new_v_gains: float32 [2, 5, 768], P(None, None, 'rows')
- new_w_gains: float32 [2, 5, 768], P(None, None, 'rows')
The draws below stay inside these ranges and needn't reach their ends.
Inputs may be any that keep to these rules, and one draw needn't show every extreme that they name: `seg_lengths`: each row's lengths sum to 128, and one of them is exactly 96.
All inputs are finite; a program needn't handle non-finite values.
Results may differ from the reference program's by a relative error of at most 0.012.
Values may be sent and summed in bfloat16 or wider, within the bound.
A program may use at most 576 MiB of HBM per device.

```python
import math
import jax
import jax.numpy as jnp
import numpy as np
from jax import lax

D = 768
HEADS = 12
HEAD_DIM = 64
FF = 3072
CH = 48
CLASSES = 1000
LAYERS = 2
SEGS = 4
STEP = 10
GROUP = 64
OUT = 96
NL = 4
NG = 5
ROW_LEN = 128
ROWS_TOT = 64
TOKENS = 8192


def with_ends(result, own_key, smallest, top_value):
    dims = result.shape
    place = [jax.random.randint(jax.random.fold_in(own_key, axis), (), 0, dims[axis]) for axis in range(len(dims))]
    result = result.at[tuple(place)].set(smallest)
    longest = dims.index(max(dims))
    place[longest] = (place[longest] + 1) % dims[longest]
    return result.at[tuple(place)].set(top_value)


def shard_levels(rng, dims, cuts, low, top_value):
    def one(position, shards_of):
        steps = jax.random.uniform(jax.random.fold_in(jax.random.fold_in(rng, 6), position), (shards_of,), jnp.float32, low / len(cuts), top_value / len(cuts))
        return jnp.repeat(jnp.exp(steps), dims[position] // shards_of).reshape((-1,) + (1,) * (len(dims) - position - 1))

    gain = one(*cuts[0])
    for cut in cuts[1:]:
        gain = gain * one(*cut)
    return gain


def split_up(number_of, total, limit, lean):
    weights = [(1 << 20) // math.isqrt(standing ** lean) + 1 for standing in range(2, number_of + 1)]
    spare, counts = total - limit - (number_of - 1), [1] * (number_of - 1)
    while spare > 0:
        free = [i for i in range(number_of - 1) if counts[i] < limit]
        mass, left = sum([weights[i] for i in free]), spare
        for i in free:
            more = min(limit - counts[i], max(1, left * weights[i] // mass), spare)
            counts[i] = counts[i] + more
            spare = spare - more
    return np.array([limit] + counts)


def ragged_sizes(stream_key, count, total, limit, lean):
    if count == 2:
        one = jax.random.randint(stream_key, (), max(1, total - limit), min(limit, total - 1) + 1)
        return jnp.stack([one, total - one])
    sizes = jnp.asarray(split_up(count, total, limit, lean), jnp.int32)
    twos = (count - 1) // 2
    donor, receiver = sizes[1:1 + 2 * twos:2], sizes[2:2 + 2 * twos:2]
    margin = jnp.minimum(donor - 1, limit - receiver)
    shifted = jax.random.randint(jax.random.fold_in(stream_key, 1), (twos,), 0, 1 << 20) % (margin + 1)
    sizes = sizes.at[1:1 + 2 * twos:2].set(donor - shifted).at[2:2 + 2 * twos:2].set(receiver + shifted)
    return sizes[jax.random.permutation(jax.random.fold_in(stream_key, 2), count)]


def centred(own_key, shape, scale, reach, shards=(), kind=jnp.bfloat16):
    array = jax.random.normal(own_key, shape, jnp.float32) * scale
    if len(shards) > 0:
        array = shard_levels(own_key, shape, shards, -0.22, 0.18) * array
    return jnp.clip(array, min=-reach, max=reach).astype(kind)


def setup_inputs(seed: int = 0) -> dict:
    streams_of = jax.random.split(jax.random.key(seed), 29)
    return {
        "patches": centred(streams_of[0], (ROWS_TOT, ROW_LEN, CH), 1.0, 6.0, ((0, 16), (1, 2))),
        "seg_lengths": jax.vmap(lambda own: ragged_sizes(own, SEGS, ROW_LEN, ROW_LEN - GROUP // 2, 2))(jax.random.split(streams_of[1], ROWS_TOT)).reshape((ROWS_TOT, SEGS)).astype(jnp.int32),
        "class_labels": with_ends(jax.random.randint(streams_of[2], (ROWS_TOT, SEGS), 0, CLASSES), jax.random.fold_in(streams_of[2], 1), 0, CLASSES - 1).astype(jnp.int32),
        "cotangent": centred(streams_of[3], (ROWS_TOT, ROW_LEN, CH), 1.0, 6.0, ((0, 16), (1, 2)), jnp.float32),
        "w_in": centred(streams_of[4], (2, CH, D), CH ** -0.5, 0.875, ((2, 16),), jnp.float32),
        "m_in": centred(streams_of[5], (2, CH, D), (0.033 * TOKENS ** 0.5), 16.0, ((2, 16),), jnp.float32),
        "v_in": jnp.clip(jnp.exp(math.log(155.648) - 1.375823 * jax.random.uniform(streams_of[6], (2, CH, D), jnp.float32) ** shard_levels(streams_of[6], (2, CH, D), ((2, 16),), -0.2, 0.2)), 39.3216, 155.648),
        "w_table": centred(streams_of[7], (2, CLASSES, D), 1.0, 6.0, ((2, 16),), jnp.float32),
        "m_table": centred(streams_of[8], (2, CLASSES, D), (0.0033 * TOKENS ** 0.5), 4.0, ((2, 16),), jnp.float32),
        "v_table": jnp.clip(jnp.exp(math.log(1.55648) - 1.375823 * jax.random.uniform(streams_of[9], (2, CLASSES, D), jnp.float32) ** shard_levels(streams_of[9], (2, CLASSES, D), ((2, 16),), -0.2, 0.2)), 0.393216, 1.55648),
        "w_qkv": centred(streams_of[10], (NL, D, 3 * D), D ** -0.5, 0.21875, ((1, 16),), jnp.float32),
        "m_qkv": centred(streams_of[11], (NL, D, 3 * D), (0.011 * TOKENS ** 0.5), 4.0, ((1, 16),), jnp.float32),
        "v_qkv": jnp.clip(jnp.exp(math.log(17.2032) - 1.3768155 * jax.random.uniform(streams_of[12], (NL, D, 3 * D), jnp.float32) ** shard_levels(streams_of[12], (NL, D, 3 * D), ((1, 16),), -0.2, 0.2)), 4.34176, 17.2032),
        "w_o": centred(streams_of[13], (NL, D, D), (D // 8) ** -0.5, 0.625, ((1, 16),), jnp.float32),
        "m_o": centred(streams_of[14], (NL, D, D), (0.022 * TOKENS ** 0.5), 12.0, ((1, 16),), jnp.float32),
        "v_o": jnp.clip(jnp.exp(math.log(68.8128) - 1.3862944 * jax.random.uniform(streams_of[15], (NL, D, D), jnp.float32) ** shard_levels(streams_of[15], (NL, D, D), ((1, 16),), -0.2, 0.2)), 17.2032, 68.8128),
        "w_up": centred(streams_of[16], (NL, D, FF), D ** -0.5, 0.21875, ((1, 16),), jnp.float32),
        "m_up": centred(streams_of[17], (NL, D, FF), (0.022 * TOKENS ** 0.5), 12.0, ((1, 16),), jnp.float32),
        "v_up": jnp.clip(jnp.exp(math.log(68.8128) - 1.3862944 * jax.random.uniform(streams_of[18], (NL, D, FF), jnp.float32) ** shard_levels(streams_of[18], (NL, D, FF), ((1, 16),), -0.2, 0.2)), 17.2032, 68.8128),
        "w_down": centred(streams_of[19], (NL, FF, D), FF ** -0.5, 0.109375, ((1, 16),), jnp.float32),
        "m_down": centred(streams_of[20], (NL, FF, D), (0.011 * TOKENS ** 0.5), 4.0, ((1, 16),), jnp.float32),
        "v_down": jnp.clip(jnp.exp(math.log(17.2032) - 1.3768155 * jax.random.uniform(streams_of[21], (NL, FF, D), jnp.float32) ** shard_levels(streams_of[21], (NL, FF, D), ((1, 16),), -0.2, 0.2)), 4.34176, 17.2032),
        "w_out": centred(streams_of[22], (2, D, OUT), (10 * D) ** -0.5, 0.0625, ((1, 16),), jnp.float32),
        "m_out": centred(streams_of[23], (2, D, OUT), (0.11 * TOKENS ** 0.5), 64.0, ((1, 16),), jnp.float32),
        "v_out": jnp.clip(jnp.exp(math.log(1720.32) - 1.3768156 * jax.random.uniform(streams_of[24], (2, D, OUT), jnp.float32) ** shard_levels(streams_of[24], (2, D, OUT), ((1, 16),), -0.2, 0.2)), 434.176, 1720.32),
        "gains": jnp.clip(1.0 + 0.1 * jax.random.normal(streams_of[25], (2, NG, D), jnp.float32), 0.5, 1.5),
        "m_gains": centred(streams_of[26], (2, NG, D), (0.033 * TOKENS ** 0.5), 16.0, ((2, 16),), jnp.float32),
        "v_gains": jnp.clip(jnp.exp(math.log(155.648) - 1.375823 * jax.random.uniform(streams_of[27], (2, NG, D), jnp.float32) ** shard_levels(streams_of[27], (2, NG, D), ((2, 16),), -0.2, 0.2)), 39.3216, 155.648),
    }


@jax.custom_vjp
def low(v):
    return lax.optimization_barrier(v.astype(jnp.bfloat16)).astype(jnp.float32)

@jax.custom_vjp
def low_back(v):
    return v

def low_keep(v):
    return (low(v), None)

def low_pass(kept, grad):
    return (grad,)

def back_keep(v):
    return (v, None)

def back_low(kept, grad):
    return (low(grad),)
low.defvjp(low_keep, low_pass)
low_back.defvjp(back_keep, back_low)
EPS_NORM = 1e-05
MASKED = -1000000000.0
BETA_ONE = 0.9
BETA_TWO = 0.95
EPS_ADAM = 1e-08
DECAY = 0.1
RATES = (0.05, 0.3, 0.02, 0.05, 0.02, 0.01, 0.01, 0.3)
HIGHEST = lax.Precision.HIGHEST

def matmul(left, right):
    return jnp.dot(left, right, precision=HIGHEST, preferred_element_type=jnp.float32)

def normalize(hidden):
    center = hidden - lax.optimization_barrier(jnp.mean(hidden, -1, keepdims=True))
    return center * lax.rsqrt(lax.optimization_barrier(jnp.mean(center * center, -1, keepdims=True)) + EPS_NORM)

def segment_of(places, seg_ends):
    return lax.optimization_barrier(jnp.sum((places[:, None] >= seg_ends[None, :]).astype(jnp.int32), -1)).astype(jnp.int32)

def block_weights(weights, block_index):
    w_in, w_table, w_qkv, w_o, w_up, w_down, w_out, gains = weights
    layer_list = []
    for layer_index in range(LAYERS):
        where_at = block_index * LAYERS + layer_index
        layer_list.append((w_qkv[where_at], w_o[where_at], w_up[where_at], w_down[where_at]))
    return (w_in[block_index], w_table[block_index], layer_list, w_out[block_index], gains[block_index])

def flow_block(inputs, seg_ids, labels_row, weights):
    w_in, w_table, layer_list, w_out, gains = weights
    length = inputs.shape[0]
    width = w_in.shape[1]
    channels = inputs.shape[1]
    factor = HEAD_DIM ** (-0.5)
    places = jnp.arange(length, dtype=jnp.int32)
    attend = (seg_ids[:, None] == seg_ids[None, :]) & (places[:, None] >= places[None, :])
    classes_tok = labels_row[seg_ids]
    hidden = low_back(matmul(low(inputs), w_in) + w_table[classes_tok])
    for layer_index, (w_qkv, w_o, w_up, w_down) in enumerate(layer_list):
        act_a = low(normalize(hidden) * gains[2 * layer_index])
        qkv = low(low_back(matmul(act_a, w_qkv)))
        query = qkv[:, :width].reshape(length, HEADS, HEAD_DIM)
        key_rows = qkv[:, width:2 * width].reshape(length, HEADS, HEAD_DIM)
        value_rows = qkv[:, 2 * width:].reshape(length, HEADS, HEAD_DIM)
        scores = low_back(jnp.einsum('qhd,khd->hqk', query, key_rows, precision=HIGHEST) * factor)
        scores = jnp.where(attend[None], scores, MASKED)
        expo_rows = jnp.exp(scores - lax.optimization_barrier(jnp.max(scores, -1, keepdims=True)))
        weights_soft = expo_rows / lax.optimization_barrier(jnp.sum(expo_rows, -1, keepdims=True))
        context = jnp.einsum('hqk,khd->qhd', low(weights_soft), value_rows, precision=HIGHEST).reshape(length, width)
        context = low(low_back(context))
        hidden = hidden + low_back(matmul(context, w_o))
        act_m = low(normalize(hidden) * gains[2 * layer_index + 1])
        upper_rows = low_back(matmul(act_m, w_up))
        hidden = hidden + low_back(matmul(low(jax.nn.gelu(upper_rows, approximate=True)), w_down))
    prediction = low_back(matmul(low(normalize(hidden) * gains[2 * LAYERS]), w_out))
    previous = jnp.concatenate([jnp.zeros((1, prediction.shape[1]), jnp.float32), prediction[:-1]], 0)
    same_seg = jnp.concatenate([jnp.zeros((1,), bool), seg_ids[1:] == seg_ids[:-1]], 0)[:, None]
    shift_mu = jnp.where(same_seg, previous[:, :channels], 0.0)
    shift_alpha = jnp.where(same_seg, previous[:, channels:], 0.0)
    latent = (inputs - shift_mu) * jnp.exp(-shift_alpha)
    return (latent, -lax.optimization_barrier(jnp.sum(shift_alpha, -1)))

def row_objective(weights, pieces):
    inputs, lengths_row, labels_row, cot_row = pieces
    length = inputs.shape[0]
    seg_ids = segment_of(jnp.arange(length, dtype=jnp.int32), jnp.cumsum(lengths_row).astype(jnp.int32))
    latent_one, det_one = flow_block(inputs, seg_ids, labels_row, block_weights(weights, 0))
    latent_two, det_two = flow_block(latent_one[::-1], seg_ids[::-1], labels_row, block_weights(weights, 1))
    det_total = det_two + det_one[::-1]
    return (jnp.sum(cot_row * latent_two) - jnp.sum(det_total), latent_two, det_total)

def adam_step(weight, first, second, grad, rate):
    first_new = BETA_ONE * first + (1.0 - BETA_ONE) * grad
    second_new = BETA_TWO * second + (1.0 - BETA_TWO) * grad * grad
    first_hat = first_new / (1.0 - BETA_ONE ** STEP)
    second_hat = second_new / (1.0 - BETA_TWO ** STEP)
    weight_new = weight - rate * (first_hat / (jnp.sqrt(second_hat) + EPS_ADAM) + DECAY * weight)
    return (first_new, second_new, weight_new)

def reference(patches, seg_lengths, class_labels, cotangent, w_in, m_in, v_in, w_table, m_table, v_table, w_qkv, m_qkv, v_qkv, w_o, m_o, v_o, w_up, m_up, v_up, w_down, m_down, v_down, w_out, m_out, v_out, gains, m_gains, v_gains):
    masters = (w_in, w_table, w_qkv, w_o, w_up, w_down, w_out, gains)
    inputs = patches.astype(jnp.float32)

    def objective(weights, inputs_all):
        lowered = tuple((low(weight) for weight in weights))

        def one_row(pieces):
            return row_objective(lowered, pieces)
        values, latents_all, dets_all = lax.map(jax.checkpoint(one_row), (inputs_all, seg_lengths, class_labels, cotangent))
        return (jnp.sum(values), (latents_all, dets_all))
    value_out, pullback, extras = jax.vjp(objective, masters, inputs, has_aux=True)
    grads, grad_patches = pullback(jnp.ones((), value_out.dtype))
    firsts = (m_in, m_table, m_qkv, m_o, m_up, m_down, m_out, m_gains)
    seconds = (v_in, v_table, v_qkv, v_o, v_up, v_down, v_out, v_gains)
    updates = [adam_step(masters[where_at], firsts[where_at], seconds[where_at], grads[where_at], RATES[where_at]) for where_at in range(8)]
    return (extras[0], extras[1], grad_patches, updates[0][0], updates[0][1], updates[0][2], updates[1][0], updates[1][1], updates[1][2], updates[2][0], updates[2][1], updates[2][2], updates[3][0], updates[3][1], updates[3][2], updates[4][0], updates[4][1], updates[4][2], updates[5][0], updates[5][1], updates[5][2], updates[6][0], updates[6][1], updates[6][2], updates[7][0], updates[7][1], updates[7][2])
```

```python
import functools
from functools import partial

import jax
import jax.numpy as jnp
from jax import lax
from jax.experimental import pallas as pl
from jax.experimental.pallas import tpu as pltpu
from jax.sharding import PartitionSpec as P

HEADS = 12
HEAD_DIM = 64
LAYERS = 2
SEGS = 4
STEP = 10

EPS_NORM = 1e-05
MASKED = -1000000000.0
BETA_ONE = 0.9
BETA_TWO = 0.95
EPS_ADAM = 1e-08
DECAY = 0.1
RATES = (0.05, 0.3, 0.02, 0.05, 0.02, 0.01, 0.01, 0.3)

MESH_ID = pl.DeviceIdType.MESH
LANES = 128

def place():
    r = lax.axis_index("rows")
    x = lax.axis_index("seq")
    c = lax.rem(r, 2)
    y = lax.rem(r // 2, 2)
    z = r // 4
    return r, x, y, z, c

def units_of(shards, d1_share):
    units = []
    order = sorted(range(len(shards)), key=lambda a: shards[a].shape[0])
    layers = max(s.shape[0] // 2 for s in shards)
    todo = [(a, 0) for a in order if shards[a].shape[0] == 2]
    for l in range(layers):
        todo += [(a, l) for a in order if shards[a].shape[0] > 2]
    for a, l in todo:
        n, rows, cols = shards[a].shape
        half = cols // 2
        if rows >= 64:
            first = max(16, round(rows * d1_share / 16) * 16)
            split = (0, first)
        else:
            first = max(LANES, round(half * d1_share / LANES) * LANES)
            split = (1, first)
        units.append((a, l, n // 2, rows, half, split))
    return units

def wait_all_of(cell, sem):
    pltpu.make_async_copy(cell, cell, sem).wait()

def gather_kernel(units, n_arrays, *refs):
    srcs, outs = refs[:n_arrays], refs[n_arrays : 2 * n_arrays]
    send, recv, local = refs[2 * n_arrays :]
    r, x, y, z, c = place()
    stage = z // 2
    other = 1 - stage
    zi = lax.rem(z, 2)
    dev_x = (r, 1 - x)
    dev_y = (r + 2 - 4 * y, x)
    dev_s = (r + 1 - 2 * c, x)
    z_near = z + 1 - 2 * zi
    z_src = (z_near, other * 2, other * 2 + 1)
    dev_z = tuple((zz * 4 + y * 2 + c, x) for zz in z_src)
    barrier = pltpu.get_barrier_semaphore()
    partners = (dev_x, dev_y, dev_s) + dev_z
    for dev in partners:
        pl.semaphore_signal(barrier, 1, device_id=dev, device_id_type=MESH_ID)
    pl.semaphore_wait(barrier, len(partners))

    started = []

    def cell(u, zz, yy, cc, h=None, part=None):
        a, l, _, rows, half, (dim, first) = units[u]
        row0, nrow = (zz * 4 + yy * 2 + cc) * rows, rows
        col0, ncol = (0, 2 * half) if h is None else (h * half, half)
        if part is not None:
            if dim == 0:
                row0, nrow = (row0, first) if part == 0 else (row0 + first, rows - first)
            else:
                col0, ncol = (col0, first) if part == 0 else (col0 + first, half - first)
        if h is not None:
            col0 = pl.multiple_of(col0, LANES)
        return outs[a].at[l, pl.ds(pl.multiple_of(row0, 16), nrow), pl.ds(col0, ncol)]

    def own(u, b, h=None):
        a, l, layers, rows, half, _ = units[u]
        if h is None:
            return srcs[a].at[layers * b + l]
        return srcs[a].at[layers * b + l, :, pl.ds(pl.multiple_of(h * half, LANES), half)]

    def push(u, src, dst, idx, dev, slot=None):
        cp = pltpu.make_async_remote_copy(
            src_ref=src,
            dst_ref=dst,
            send_sem=send.at[u, idx if slot is None else slot],
            recv_sem=recv.at[u, idx],
            device_id=dev,
            device_id_type=MESH_ID,
        )
        cp.start()
        started.append(cp)

    def arrived(u, dst, idx):
        wait_all_of(dst, recv.at[u, idx])

    def begin(u):
        mine = cell(u, z, y, c, x)
        for i in range(2):
            push(u, own(u, other, x), mine, 1 + zi, dev_z[1 + i], slot=1 + i)
        push(u, own(u, stage, x), mine, 0, dev_z[0])
        push(u, own(u, stage, x), mine, 10, dev_y)
        push(u, own(u, stage), cell(u, z, y, c), 17, dev_s)
        pltpu.make_async_copy(own(u, stage), cell(u, z, y, c), local.at[u]).start()

    def spread(u):
        arrived(u, cell(u, z, 1 - y, c, x), 10)
        push(u, cell(u, z, 1 - y, c, x), cell(u, z, 1 - y, c, x), 6, dev_x)
        for j in range(3):
            piece = cell(u, z_src[j], y, c, x)
            arrived(u, piece, j)
            push(u, piece, piece, 3 + j, dev_x)
            push(u, piece, piece, 7 + j, dev_y)

    def corner(u):
        for j in range(3):
            arrived(u, cell(u, z_src[j], y, c, 1 - x), 3 + j)
            part = cell(u, z_src[j], y, c, 1 - x, 0)
            push(u, part, part, 11 + j, dev_y)
            arrived(u, cell(u, z_src[j], 1 - y, c, x), 7 + j)
            part = cell(u, z_src[j], 1 - y, c, x, 1)
            push(u, part, part, 14 + j, dev_x)
            slab = cell(u, z_src[j], y, c)
            push(u, slab, slab, 19 + j, dev_s)

    def finish(u):
        arrived(u, cell(u, z, 1 - y, c, 1 - x), 6)
        slab = cell(u, z, 1 - y, c)
        push(u, slab, slab, 18, dev_s)
        for j in range(3):
            arrived(u, cell(u, z_src[j], 1 - y, c, 1 - x, 0), 11 + j)
            arrived(u, cell(u, z_src[j], 1 - y, c, 1 - x, 1), 14 + j)
            slab = cell(u, z_src[j], 1 - y, c)
            push(u, slab, slab, 22 + j, dev_s)

    n = len(units)
    for u in range(n):
        begin(u)
    for t in range(n + 2):
        if t < n:
            spread(t)
        if 0 <= t - 1 < n:
            corner(t - 1)
        if 0 <= t - 2 < n:
            finish(t - 2)
    for u in range(n):
        arrived(u, cell(u, z, y, 1 - c), 17)
        arrived(u, cell(u, z, 1 - y, 1 - c), 18)
        for j in range(3):
            arrived(u, cell(u, z_src[j], y, 1 - c), 19 + j)
            arrived(u, cell(u, z_src[j], 1 - y, 1 - c), 22 + j)
        pltpu.make_async_copy(own(u, stage), cell(u, z, y, c), local.at[u]).wait()
    for cp in started:
        cp.wait_send()

def gather_blocks(shards, collective_id):
    units = units_of(shards, 0.5)
    out = [
        jax.ShapeDtypeStruct((s.shape[0] // 2, 16 * s.shape[1], s.shape[2]), s.dtype)
        for s in shards
    ]
    n = len(units)
    return pl.pallas_call(
        functools.partial(gather_kernel, units, len(shards)),
        out_shape=out,
        in_specs=[pl.BlockSpec(memory_space=pl.ANY)] * len(shards),
        out_specs=[pl.BlockSpec(memory_space=pl.ANY)] * len(shards),
        scratch_shapes=[
            pltpu.SemaphoreType.DMA((n, 25)),
            pltpu.SemaphoreType.DMA((n, 25)),
            pltpu.SemaphoreType.DMA((n,)),
        ],
        compiler_params=pltpu.CompilerParams(collective_id=collective_id, has_side_effects=True),
        name="gather_blocks",
    )(*shards)

def scatter_kernel(units, n_arrays, *refs):
    grads, outs = refs[:n_arrays], refs[n_arrays : 2 * n_arrays]
    n = len(units)
    rest = refs[2 * n_arrays :]
    acc, sib, in_x, in_y, in_d, in_z, fin = [rest[i * n : (i + 1) * n] for i in range(7)]
    send, recv, local, local_out = rest[7 * n :]
    r, x, y, z, c = place()
    stage = z // 2
    other = 1 - stage
    zi = lax.rem(z, 2)
    dev_x = (r, 1 - x)
    dev_y = (r + 2 - 4 * y, x)
    dev_s = (r + 1 - 2 * c, x)
    z_near = z + 1 - 2 * zi
    z_dst = (z_near, other * 2, other * 2 + 1)
    dev_z = tuple((zz * 4 + y * 2 + c, x) for zz in z_dst)
    barrier = pltpu.get_barrier_semaphore()
    partners = (dev_x, dev_y, dev_s) + dev_z
    for dev in partners:
        pl.semaphore_signal(barrier, 1, device_id=dev, device_id_type=MESH_ID)
    pl.semaphore_wait(barrier, len(partners))
    started = []

    def part_of(u, part):
        _, _, _, rows, half, (dim, first) = units[u]
        if dim == 0:
            return (pl.ds(0, first), pl.ds(0, half)) if part == 0 else (pl.ds(first, rows - first), pl.ds(0, half))
        return (pl.ds(0, rows), pl.ds(0, first)) if part == 0 else (pl.ds(0, rows), pl.ds(first, half - first))

    def push(u, src, dst, slot, dev, idx=None):
        cp = pltpu.make_async_remote_copy(
            src_ref=src,
            dst_ref=dst,
            send_sem=send.at[u, slot],
            recv_sem=recv.at[u, slot if idx is None else idx],
            device_id=dev,
            device_id_type=MESH_ID,
        )
        cp.start()
        started.append(cp)

    def arrived(u, dst, idx):
        wait_all_of(dst, recv.at[u, idx])

    def pieces(u, cc):
        a, l, _, rows, half, _ = units[u]
        for s in range(8):
            for h in range(2):
                row0 = pl.multiple_of((s * 2 + cc) * rows, 16)
                yield s, h, grads[a].at[l, pl.ds(row0, rows), pl.ds(h * half, half)]

    def begin(u):
        for s, h, src in pieces(u, 1 - c):
            push(u, src, sib[u].at[s, h], 18 + 2 * s + h, dev_s)
        for s, h, src in pieces(u, c):
            pltpu.make_async_copy(src, acc[u].at[s, h], local.at[u]).start()

    def chip_sum(u):
        wait_all_of(acc[u], local.at[u])
        for s in range(8):
            for h in range(2):
                arrived(u, sib[u].at[s, h], 18 + 2 * s + h)

        @pl.loop(0, 8)
        def _(s):
            for h in range(2):
                acc[u][s, h] = acc[u][s, h] + sib[u][s, h]

        for zz in range(4):
            slab = zz * 2 + 1 - y
            rs, cs = part_of(u, 0)
            push(u, acc[u].at[slab, 1 - x, rs, cs], in_d[u].at[zz, rs, cs], zz, dev_y)
            rs, cs = part_of(u, 1)
            push(u, acc[u].at[slab, 1 - x, rs, cs], in_d[u].at[zz, rs, cs], 4 + zz, dev_x)

    def side_sum(u):
        for zz in range(4):
            rs, cs = part_of(u, 0)
            arrived(u, in_d[u].at[zz, rs, cs], zz)
            acc[u][zz * 2 + y, 1 - x, rs, cs] = acc[u][zz * 2 + y, 1 - x, rs, cs] + in_d[u][zz, rs, cs]
            push(u, acc[u].at[zz * 2 + y, 1 - x], in_x[u].at[zz], 8 + zz, dev_x)
            rs, cs = part_of(u, 1)
            arrived(u, in_d[u].at[zz, rs, cs], 4 + zz)
            acc[u][zz * 2 + 1 - y, x, rs, cs] = acc[u][zz * 2 + 1 - y, x, rs, cs] + in_d[u][zz, rs, cs]
            push(u, acc[u].at[zz * 2 + 1 - y, x], in_y[u].at[zz], 12 + zz, dev_y)

    def plane_sum(u):
        for zz in range(4):
            arrived(u, in_x[u].at[zz], 8 + zz)
            arrived(u, in_y[u].at[zz], 12 + zz)
            acc[u][zz * 2 + y, x] = (
                acc[u][zz * 2 + y, x].astype(jnp.float32)
                + in_x[u][zz].astype(jnp.float32)
                + in_y[u][zz].astype(jnp.float32)
            ).astype(jnp.bfloat16)
        for i in range(2):
            push(u, acc[u].at[z_dst[1 + i] * 2 + y, x], in_z[u].at[1 + zi], 35 + i, dev_z[1 + i], idx=35 + zi)
        push(u, acc[u].at[z_near * 2 + y, x], in_z[u].at[0], 34, dev_z[0])

    def total(u):
        a, l, layers, rows, half, _ = units[u]
        for j in range(3):
            arrived(u, in_z[u].at[j], 34 + j)
        fin[u][0] = acc[u][z * 2 + y, x] + in_z[u][0]
        fin[u][1] = in_z[u][1] + in_z[u][2]
        for k, b in ((0, stage), (1, other)):
            dst = outs[a].at[layers * b + l, :, pl.ds(pl.multiple_of(x * half, LANES), half)]
            push(u, fin[u].at[k], dst, 16 + k, dev_x)
            pltpu.make_async_copy(fin[u].at[k], dst, local_out.at[u, k]).start()

    for u in range(n):
        begin(u)
    for t in range(n + 3):
        if t < n:
            chip_sum(t)
        if 0 <= t - 1 < n:
            side_sum(t - 1)
        if 0 <= t - 2 < n:
            plane_sum(t - 2)
        if 0 <= t - 3 < n:
            total(t - 3)
    for u in range(n):
        a, l, layers, rows, half, _ = units[u]
        for k, b in ((0, stage), (1, other)):
            there = outs[a].at[layers * b + l, :, pl.ds(pl.multiple_of((1 - x) * half, LANES), half)]
            arrived(u, there, 16 + k)
            dst = outs[a].at[layers * b + l, :, pl.ds(pl.multiple_of(x * half, LANES), half)]
            pltpu.make_async_copy(fin[u].at[k], dst, local_out.at[u, k]).wait()
    for cp in started:
        cp.wait_send()

def scatter_blocks(grads, collective_id):
    out = [
        jax.ShapeDtypeStruct((g.shape[0] * 2, g.shape[1] // 16, g.shape[2]), g.dtype) for g in grads
    ]
    units = units_of(out, 0.75)
    n = len(units)

    def bufs(lead):
        return [pltpu.VMEM(lead + (u[3], u[4]), jnp.bfloat16) for u in units]

    return pl.pallas_call(
        functools.partial(scatter_kernel, units, len(grads)),
        out_shape=out,
        in_specs=[pl.BlockSpec(memory_space=pl.ANY)] * len(grads),
        out_specs=[pl.BlockSpec(memory_space=pl.ANY)] * len(grads),
        scratch_shapes=bufs((8, 2))
        + bufs((8, 2))
        + bufs((4,))
        + bufs((4,))
        + bufs((4,))
        + bufs((3,))
        + bufs((2,))
        + [
            pltpu.SemaphoreType.DMA((n, 37)),
            pltpu.SemaphoreType.DMA((n, 37)),
            pltpu.SemaphoreType.DMA((n,)),
            pltpu.SemaphoreType.DMA((n, 2)),
        ],
        compiler_params=pltpu.CompilerParams(
            collective_id=collective_id, has_side_effects=True, vmem_limit_bytes=60 * 2**20
        ),
        name="scatter_blocks",
    )(*grads)


def dot(left, right, dims=((1,), (0,))):
    return lax.dot_general(left, right, (dims, ((), ())), preferred_element_type=jnp.float32)


def normalize(hidden):
    center = hidden - jnp.mean(hidden, -1, keepdims=True)
    inverse = lax.rsqrt(jnp.mean(center * center, -1, keepdims=True) + EPS_NORM)
    return (center * inverse, inverse)


def normalize_back(normed, inverse, grad_normed):
    mean_grad = jnp.mean(grad_normed, -1, keepdims=True)
    mean_proj = jnp.mean(grad_normed * normed, -1, keepdims=True)
    return inverse * (grad_normed - mean_grad - normed * mean_proj)


def padded(count, unit=256):
    return -(-count // unit) * unit


def side_columns(classes, channels, out, gains):
    table = padded(classes, 128)
    ends = [table, table + channels, table + channels + out, table + channels + out + gains]
    return ends, padded(ends[-1])


def pack_side(w_table, w_in, w_out, gains):
    blocks, classes, shard = w_table.shape
    ends, total = side_columns(classes, w_in.shape[1], w_out.shape[2], gains.shape[1])

    def gap(count):
        return jnp.zeros((blocks, shard, count), w_table.dtype)

    return jnp.concatenate(
        [
            jnp.swapaxes(w_table, 1, 2),
            gap(ends[0] - classes),
            jnp.swapaxes(w_in, 1, 2),
            w_out,
            jnp.swapaxes(gains, 1, 2),
            gap(total - ends[3]),
        ],
        2,
    )


def split_side(side, classes, channels, out, gains):
    ends, _ = side_columns(classes, channels, out, gains)
    return (
        jnp.swapaxes(side[..., :classes], -1, -2),
        jnp.swapaxes(side[..., ends[0] : ends[1]], -1, -2),
        side[..., ends[1] : ends[2]],
        jnp.swapaxes(side[..., ends[2] : ends[3]], -1, -2),
    )


def heads_of(flat, rows):
    return flat.reshape(rows, -1, HEADS, HEAD_DIM)


def attention_scores(query, key_rows, attend):
    scores = jnp.einsum(
        "rqhd,rkhd->rhqk", query, key_rows, preferred_element_type=jnp.float32
    ) * HEAD_DIM ** (-0.5)
    return jnp.where(attend[:, None], scores, MASKED)


def forward_block(inputs, seg_ids, labels, weights, sizes):
    w_qkv, w_o, w_up, w_down, side = weights
    classes, channels, out, gain_count = sizes
    ends, side_total = side_columns(*sizes)
    rows, length, _ = inputs.shape
    tokens = rows * length
    width = side.shape[0]
    places = jnp.arange(length, dtype=jnp.int32)
    attend = (seg_ids[:, :, None] == seg_ids[:, None, :]) & (
        places[None, :, None] >= places[None, None, :]
    )
    same_seg = jnp.concatenate(
        [jnp.zeros((rows, 1), bool), seg_ids[:, 1:] == seg_ids[:, :-1]], 1
    )[..., None]
    onehot = labels.reshape(tokens, 1) == jnp.arange(ends[0])[None, :]
    start = jnp.concatenate(
        [
            onehot.astype(jnp.bfloat16),
            inputs.reshape(tokens, channels).astype(jnp.bfloat16),
            jnp.zeros((tokens, side_total - ends[1]), jnp.bfloat16),
        ],
        1,
    )
    gain_rows = side[:, ends[2] : ends[3]].astype(jnp.float32).T
    hidden = dot(start, side, ((1,), (1,)))
    kept = []
    for layer in range(w_qkv.shape[0]):
        normed_a, inverse_a = normalize(hidden)
        act_a = (normed_a * gain_rows[2 * layer]).astype(jnp.bfloat16)
        qkv = dot(act_a, w_qkv[layer]).astype(jnp.bfloat16)
        query, key_rows, value_rows = [
            heads_of(qkv[:, i * width : (i + 1) * width], rows) for i in range(3)
        ]
        scores = attention_scores(query, key_rows, attend)
        row_top = jnp.max(scores, -1, keepdims=True)
        expo_rows = jnp.exp(scores - row_top)
        row_total = jnp.sum(expo_rows, -1, keepdims=True)
        soft_low = (expo_rows / row_total).astype(jnp.bfloat16)
        log_total = row_top + jnp.log(row_total)
        context = jnp.einsum(
            "rhqk,rkhd->rqhd", soft_low, value_rows, preferred_element_type=jnp.float32
        )
        context = context.reshape(tokens, width).astype(jnp.bfloat16)
        middle = hidden + dot(context, w_o[layer])
        normed_m, inverse_m = normalize(middle)
        act_m = (normed_m * gain_rows[2 * layer + 1]).astype(jnp.bfloat16)
        upper = dot(act_m, w_up[layer])
        gelu_low = jax.nn.gelu(upper, approximate=True).astype(jnp.bfloat16)
        hidden = middle + dot(gelu_low, w_down[layer])
        kept.append(
            (
                normed_a,
                inverse_a,
                act_a,
                qkv,
                log_total,
                context,
                normed_m,
                inverse_m,
                act_m,
                upper,
                gelu_low,
            )
        )
    normed_f, inverse_f = normalize(hidden)
    act_f = (normed_f * gain_rows[gain_count - 1]).astype(jnp.bfloat16)
    prediction = dot(act_f, side[:, ends[1] : ends[2]]).reshape(rows, length, out)
    previous = jnp.concatenate([jnp.zeros((rows, 1, out), jnp.float32), prediction[:, :-1]], 1)
    shift = jnp.where(same_seg, previous, 0.0)
    shift_alpha = shift[..., channels:]
    latent = (inputs - shift[..., :channels]) * jnp.exp(-shift_alpha)
    saved = (attend, same_seg, start, kept, normed_f, inverse_f, act_f, shift_alpha, latent)
    return (latent, -jnp.sum(shift_alpha, -1), saved)


def backward_block(grad_latent, saved, weights, sizes):
    w_qkv, w_o, w_up, w_down, side = weights
    classes, channels, out, gain_count = sizes
    ends, _ = side_columns(*sizes)
    attend, same_seg, start, kept, normed_f, inverse_f, act_f, shift_alpha, latent = saved
    rows, length, _ = latent.shape
    tokens = rows * length
    width = side.shape[0]
    factor = HEAD_DIM ** (-0.5)
    gain_rows = side[:, ends[2] : ends[3]].astype(jnp.float32).T
    scale_back = jnp.exp(-shift_alpha)
    grad_inputs = grad_latent * scale_back
    grad_prev = jnp.where(
        same_seg, jnp.concatenate([-grad_inputs, 1.0 - grad_latent * latent], 2), 0.0
    )
    grad_pred = jnp.concatenate([grad_prev[:, 1:], jnp.zeros((rows, 1, out), jnp.float32)], 1)
    grad_pred = grad_pred.reshape(tokens, out).astype(jnp.bfloat16)
    grad_act = dot(grad_pred, side[:, ends[1] : ends[2]], ((1,), (1,)))
    gain_grads = [None] * gain_count
    gain_grads[-1] = jnp.sum(grad_act * normed_f, 0)
    grad_hidden = normalize_back(normed_f, inverse_f, grad_act * gain_rows[gain_count - 1])
    pairs = [None] * w_qkv.shape[0]
    for layer in reversed(range(w_qkv.shape[0])):
        (
            normed_a,
            inverse_a,
            act_a,
            qkv,
            log_total,
            context,
            normed_m,
            inverse_m,
            act_m,
            upper,
            gelu_low,
        ) = kept[layer]
        grad_branch = grad_hidden.astype(jnp.bfloat16)
        grad_gelu = dot(grad_branch, w_down[layer], ((1,), (1,)))
        gelu_pull = jax.vjp(partial(jax.nn.gelu, approximate=True), upper)[1]
        grad_upper = gelu_pull(grad_gelu)[0].astype(jnp.bfloat16)
        grad_act_m = dot(grad_upper, w_up[layer], ((1,), (1,)))
        gain_grads[2 * layer + 1] = jnp.sum(grad_act_m * normed_m, 0)
        grad_middle = grad_hidden + normalize_back(
            normed_m, inverse_m, grad_act_m * gain_rows[2 * layer + 1]
        )
        grad_mid_low = grad_middle.astype(jnp.bfloat16)
        grad_context = heads_of(
            dot(grad_mid_low, w_o[layer], ((1,), (1,))).astype(jnp.bfloat16), rows
        )
        query, key_rows, value_rows = [
            heads_of(qkv[:, i * width : (i + 1) * width], rows) for i in range(3)
        ]
        soft_rows = jnp.exp(attention_scores(query, key_rows, attend) - log_total)
        soft_low = soft_rows.astype(jnp.bfloat16)
        grad_soft = jnp.einsum(
            "rqhd,rkhd->rhqk", grad_context, value_rows, preferred_element_type=jnp.float32
        )
        row_delta = jnp.sum(soft_rows * grad_soft, -1, keepdims=True)
        grad_scores = (soft_rows * (grad_soft - row_delta)).astype(jnp.bfloat16)
        grad_query = factor * jnp.einsum(
            "rhqk,rkhd->rqhd", grad_scores, key_rows, preferred_element_type=jnp.float32
        )
        grad_keys = factor * jnp.einsum(
            "rhqk,rqhd->rkhd", grad_scores, query, preferred_element_type=jnp.float32
        )
        grad_values = jnp.einsum(
            "rhqk,rqhd->rkhd", soft_low, grad_context, preferred_element_type=jnp.float32
        )
        grad_qkv = jnp.concatenate(
            [part.reshape(tokens, width) for part in (grad_query, grad_keys, grad_values)], 1
        ).astype(jnp.bfloat16)
        grad_act_a = dot(grad_qkv, w_qkv[layer], ((1,), (1,)))
        gain_grads[2 * layer] = jnp.sum(grad_act_a * normed_a, 0)
        grad_hidden = grad_middle + normalize_back(
            normed_a, inverse_a, grad_act_a * gain_rows[2 * layer]
        )
        pairs[layer] = (
            (act_a, grad_qkv),
            (context, grad_mid_low),
            (act_m, grad_upper),
            (gelu_low, grad_branch),
        )
    grad_start = grad_hidden.astype(jnp.bfloat16)
    grad_inputs = grad_inputs + dot(grad_start, side[:, ends[0] : ends[1]]).reshape(
        rows, length, channels
    )
    return grad_inputs, (
        pairs,
        (start[:, : ends[1]], grad_start),
        (act_f, grad_pred),
        jnp.stack(gain_grads, 1),
    )


def weight_grads(parts, side_total):
    pairs, (start, grad_start), (act_f, grad_pred), gain_grads = parts
    arrays = [
        jnp.stack([dot(*layer[i], ((0,), (0,))).astype(jnp.bfloat16) for layer in pairs], 0)
        for i in range(4)
    ]
    side = [
        dot(grad_start, start, ((0,), (0,))),
        dot(act_f, grad_pred, ((0,), (0,))),
        gain_grads,
    ]
    count = sum(part.shape[1] for part in side)
    side.append(jnp.zeros((gain_grads.shape[0], side_total - count), jnp.float32))
    side = jnp.concatenate(side, 1).astype(jnp.bfloat16)
    return arrays + [side[None]]


def adam_step(weight, first, second, grad, rate):
    first_new = BETA_ONE * first + (1.0 - BETA_ONE) * grad
    second_new = BETA_TWO * second + (1.0 - BETA_TWO) * grad * grad
    first_hat = first_new / (1.0 - BETA_ONE**STEP)
    second_hat = second_new / (1.0 - BETA_TWO**STEP)
    weight_new = weight - rate * (first_hat / (jnp.sqrt(second_hat) + EPS_ADAM) + DECAY * weight)
    return (first_new, second_new, weight_new)


def segment_of(places, seg_ends):
    return jnp.sum((places[None, :, None] >= seg_ends[:, None, :]).astype(jnp.int32), -1)


def row_facts(seg_lengths, class_labels, length):
    seg_ids = segment_of(jnp.arange(length, dtype=jnp.int32), jnp.cumsum(seg_lengths, 1))
    picked = seg_ids[:, :, None] == jnp.arange(SEGS)[None, None, :]
    return seg_ids, jnp.sum(jnp.where(picked, class_labels[:, None, :], 0), -1)


def staged(mine, low, sizes):
    half = lax.axis_size("rows") // 2
    second = lax.axis_index("rows") >= half
    swap = [(i, (i + half) % (2 * half)) for i in range(2 * half)]
    up = [(i, i + half) for i in range(half)]
    down = [(i + half, i) for i in range(half)]
    theirs = [lax.ppermute(part, "rows", swap) for part in mine]
    batch = [
        [jnp.where(second, b, a) for a, b in zip(mine, theirs)],
        [jnp.where(second, a, b) for a, b in zip(mine, theirs)],
    ]
    weights = list(gather_blocks(low, 1))
    weights[4] = weights[4][0]

    def facts(index):
        ahead, behind = batch[min(index, 1)], batch[max(index - 1, 0)]
        return [jnp.where(second, behind[i][:, ::-1], ahead[i]) for i in (2, 3)]

    steps = []
    arrived = None
    for index in range(3):
        inputs = batch[min(index, 1)][0]
        if arrived is None:
            inputs = jnp.where(second, 0.0, inputs)
        else:
            inputs = jnp.where(second, arrived[..., :-1], inputs)
        latent, logdet, saved = forward_block(inputs, *facts(index), weights, sizes)
        if arrived is not None:
            logdet = logdet + arrived[..., -1]
        steps.append((latent, logdet, saved))
        if index < 2:
            arrived = lax.ppermute(
                jnp.concatenate([latent, logdet[..., None]], 2)[:, ::-1], "rows", up
            )
    parts = []
    grad_inputs = []
    returned = jnp.zeros_like(batch[0][1])
    for index in range(3):
        grad_latent = jnp.where(second, batch[max(1 - index, 0)][1], returned)
        grad, part = backward_block(grad_latent, steps[2 - index][2], weights, sizes)
        parts.append(part)
        grad_inputs.append(grad)
        if index < 2:
            returned = lax.ppermute(grad[:, ::-1], "rows", down)
    chosen = jax.tree.map(lambda a, b: jnp.where(second, a, b), parts[0], parts[2])
    gain_grads = parts[1][3] + chosen[3]
    both = jax.tree.map(lambda a, b: jnp.concatenate([a, b], 0), parts[1], chosen)
    grads = weight_grads(both[:3] + (gain_grads,), low[4].shape[2])
    sums = scatter_blocks(grads, 2)

    def result(index):
        return jnp.concatenate([steps[index][0], steps[index][1][..., None]], 2)

    sent = jnp.where(second, result(1), jnp.pad(grad_inputs[1], ((0, 0), (0, 0), (0, 1))))
    received = lax.ppermute(sent, "rows", swap)
    outcome = jnp.where(second, result(2), received)
    patch_grad = jnp.where(second, received[..., :-1], grad_inputs[2])
    return outcome, patch_grad, sums


def unstaged(mine, low, sizes):
    inputs, cotangent, seg_ids, labels = mine
    whole = [lax.all_gather(part, "rows", axis=1, tiled=True) for part in low]

    def block(index):
        picked = [part[index * LAYERS : (index + 1) * LAYERS] for part in whole[:4]]
        return picked + [whole[4][index]]

    back = seg_ids[:, ::-1], labels[:, ::-1]
    latent_one, det_one, saved_one = forward_block(inputs, seg_ids, labels, block(0), sizes)
    latent_two, det_two, saved_two = forward_block(latent_one[:, ::-1], *back, block(1), sizes)
    outcome = jnp.concatenate([latent_two, (det_two + det_one[:, ::-1])[..., None]], 2)
    grad_mid, parts_two = backward_block(cotangent, saved_two, block(1), sizes)
    patch_grad, parts_one = backward_block(grad_mid[:, ::-1], saved_one, block(0), sizes)
    grads = [
        jnp.concatenate(pair, 0)
        for pair in zip(
            weight_grads(parts_one, low[4].shape[2]), weight_grads(parts_two, low[4].shape[2])
        )
    ]
    sums = [
        lax.psum(
            lax.psum_scatter(grad, "rows", scatter_dimension=1, tiled=True).astype(jnp.float32),
            "seq",
        )
        for grad in grads
    ]
    return outcome, patch_grad, sums


def body(
    patches,
    seg_lengths,
    class_labels,
    cotangent,
    w_in,
    m_in,
    v_in,
    w_table,
    m_table,
    v_table,
    w_qkv,
    m_qkv,
    v_qkv,
    w_o,
    m_o,
    v_o,
    w_up,
    m_up,
    v_up,
    w_down,
    m_down,
    v_down,
    w_out,
    m_out,
    v_out,
    gains,
    m_gains,
    v_gains,
):
    masters = (w_in, w_table, w_qkv, w_o, w_up, w_down, w_out, gains)
    low = [weight.astype(jnp.bfloat16) for weight in masters]
    sizes = (w_table.shape[1], w_in.shape[1], w_out.shape[2], gains.shape[1])
    shards = low[2:6] + [pack_side(low[1], low[0], low[6], low[7])]
    held, group, channels = patches.shape
    seq_count = lax.axis_size("seq")
    length = group * seq_count
    share = max(1, held // seq_count)
    copies = seq_count * share // held
    first_row = (lax.axis_index("seq") // copies) * share
    pieces = jnp.concatenate([patches.astype(jnp.float32), cotangent], 2)
    pieces = lax.all_gather(pieces, "seq", axis=1, tiled=True)
    pieces = lax.dynamic_slice_in_dim(pieces, first_row, share, 0)
    seg_ids, labels = row_facts(
        lax.dynamic_slice_in_dim(seg_lengths, first_row, share, 0),
        lax.dynamic_slice_in_dim(class_labels, first_row, share, 0),
        length,
    )
    mine = (pieces[..., :channels], pieces[..., channels:], seg_ids, labels)
    two_stages = seq_count == 2 and lax.axis_size("rows") == 16 and copies == 1
    outcome, patch_grad, sums = (staged if two_stages else unstaged)(mine, shards, sizes)
    results = lax.all_gather(jnp.concatenate([outcome, patch_grad], 2), "seq", axis=0)
    results = results[::copies].reshape((held,) + results.shape[2:])
    results = lax.dynamic_slice_in_dim(results, lax.axis_index("seq") * group, group, 1)
    sums = [total.astype(jnp.float32) / copies for total in sums]
    table, first, last, gain = split_side(sums[4], *sizes)
    grads = (first, table, sums[0], sums[1], sums[2], sums[3], last, gain)
    firsts = (m_in, m_table, m_qkv, m_o, m_up, m_down, m_out, m_gains)
    seconds = (v_in, v_table, v_qkv, v_o, v_up, v_down, v_out, v_gains)
    updates = [adam_step(*item) for item in zip(masters, firsts, seconds, grads, RATES)]
    return (
        results[..., :channels],
        results[..., channels],
        results[..., channels + 1 :],
    ) + tuple(part for update in updates for part in update)


def solution(mesh):
    tokens = P("rows", "seq", None)
    row = P("rows", None)
    last, middle = P(None, None, "rows"), P(None, "rows", None)
    weights = (last,) * 6 + (middle,) * 15 + (last,) * 3
    return jax.shard_map(
        body,
        mesh=mesh,
        in_specs=(tokens, row, row, tokens) + weights,
        out_specs=(tokens, P("rows", "seq"), tokens) + weights,
        check_vma=False,
    )
```

```python
import functools
from functools import partial

import jax
import jax.numpy as jnp
from jax import lax
from jax.experimental import pallas as pl
from jax.experimental.pallas import tpu as pltpu
from jax.sharding import PartitionSpec as P

HEADS = 12
HEAD_DIM = 64
LAYERS = 2
SEGS = 4
STEP = 10

EPS_NORM = 1e-05
MASKED = -1000000000.0
BETA_ONE = 0.9
BETA_TWO = 0.95
EPS_ADAM = 1e-08
DECAY = 0.1
RATES = (0.05, 0.3, 0.02, 0.05, 0.02, 0.01, 0.01, 0.3)

MESH_ID = pl.DeviceIdType.MESH
LANES = 128


def place():
    r = lax.axis_index("rows")
    x = lax.axis_index("seq")
    c = lax.rem(r, 2)
    y = lax.rem(r // 2, 2)
    z = r // 4
    return r, x, y, z, c


def units_of(shards, d1_share):
    units = []
    order = sorted(range(len(shards)), key=lambda a: shards[a].shape[0])
    layers = max(s.shape[0] // 2 for s in shards)
    todo = [(a, 0) for a in order if shards[a].shape[0] == 2]
    for l in range(layers):
        todo += [(a, l) for a in order if shards[a].shape[0] > 2]
    for a, l in todo:
        n, rows, cols = shards[a].shape
        half = cols // 2
        if rows >= 64:
            first = max(16, round(rows * d1_share / 16) * 16)
            split = (0, first)
        else:
            first = max(LANES, round(half * d1_share / LANES) * LANES)
            split = (1, first)
        units.append((a, l, n // 2, rows, half, split))
    return units


def wait_all_of(cell, sem):
    pltpu.make_async_copy(cell, cell, sem).wait()


def gather_kernel(units, n_arrays, *refs):
    srcs, outs = refs[:n_arrays], refs[n_arrays : 2 * n_arrays]
    send, recv, local = refs[2 * n_arrays :]
    r, x, y, z, c = place()
    stage = z // 2
    other = 1 - stage
    zi = lax.rem(z, 2)
    dev_x = (r, 1 - x)
    dev_y = (r + 2 - 4 * y, x)
    dev_s = (r + 1 - 2 * c, x)
    z_near = z + 1 - 2 * zi
    z_src = (z_near, other * 2, other * 2 + 1)
    dev_z = tuple((zz * 4 + y * 2 + c, x) for zz in z_src)
    barrier = pltpu.get_barrier_semaphore()
    partners = (dev_x, dev_y, dev_s) + dev_z
    for dev in partners:
        pl.semaphore_signal(barrier, 1, device_id=dev, device_id_type=MESH_ID)
    pl.semaphore_wait(barrier, len(partners))

    inner = stage != zi
    dev_inner = ((1 + other) * 4 + y * 2 + c, x)
    started = []

    def cell(u, zz, yy, cc, h=None, part=None):
        a, l, _, rows, half, (dim, first) = units[u]
        row0, nrow = (zz * 4 + yy * 2 + cc) * rows, rows
        col0, ncol = (0, 2 * half) if h is None else (h * half, half)
        if part is not None:
            if dim == 0:
                row0, nrow = (row0, first) if part == 0 else (row0 + first, rows - first)
            else:
                col0, ncol = (col0, first) if part == 0 else (col0 + first, half - first)
        if h is not None:
            col0 = pl.multiple_of(col0, LANES)
        return outs[a].at[l, pl.ds(pl.multiple_of(row0, 16), nrow), pl.ds(col0, ncol)]

    def own(u, b, h=None):
        a, l, layers, rows, half, _ = units[u]
        if h is None:
            return srcs[a].at[layers * b + l]
        return srcs[a].at[layers * b + l, :, pl.ds(pl.multiple_of(h * half, LANES), half)]

    def push(u, src, dst, idx, dev, slot=None):
        cp = pltpu.make_async_remote_copy(
            src_ref=src,
            dst_ref=dst,
            send_sem=send.at[u, idx if slot is None else slot],
            recv_sem=recv.at[u, idx],
            device_id=dev,
            device_id_type=MESH_ID,
        )
        cp.start()
        started.append(cp)

    def arrived(u, dst, idx):
        wait_all_of(dst, recv.at[u, idx])

    def relay_copy(u, piece, j):
        return pltpu.make_async_remote_copy(
            src_ref=piece,
            dst_ref=piece,
            send_sem=send.at[u, 24 + j],
            recv_sem=recv.at[u, j],
            device_id=dev_z[0],
            device_id_type=MESH_ID,
        )

    def relay(u, piece, j):
        @pl.when(inner)
        def _():
            relay_copy(u, piece, j).start()

    def begin(u):
        mine = cell(u, z, y, c, x)
        push(u, own(u, other, x), mine, 1 + zi, dev_inner, slot=1)
        push(u, own(u, stage, x), mine, 0, dev_z[0])
        push(u, own(u, stage, x), mine, 10, dev_y)
        push(u, own(u, stage), cell(u, z, y, c), 17, dev_s)
        pltpu.make_async_copy(own(u, stage), cell(u, z, y, c), local.at[u]).start()

    def spread(u):
        arrived(u, cell(u, z, 1 - y, c, x), 10)
        push(u, cell(u, z, 1 - y, c, x), cell(u, z, 1 - y, c, x), 6, dev_x)
        for j in range(3):
            piece = cell(u, z_src[j], y, c, x)
            arrived(u, piece, j)
            if j > 0:
                relay(u, piece, j)
            push(u, piece, piece, 3 + j, dev_x)
            push(u, piece, piece, 7 + j, dev_y)

    def corner(u):
        for j in range(3):
            arrived(u, cell(u, z_src[j], y, c, 1 - x), 3 + j)
            part = cell(u, z_src[j], y, c, 1 - x, 0)
            push(u, part, part, 11 + j, dev_y)
            arrived(u, cell(u, z_src[j], 1 - y, c, x), 7 + j)
            part = cell(u, z_src[j], 1 - y, c, x, 1)
            push(u, part, part, 14 + j, dev_x)
            slab = cell(u, z_src[j], y, c)
            push(u, slab, slab, 19 + j, dev_s)

    def finish(u):
        arrived(u, cell(u, z, 1 - y, c, 1 - x), 6)
        slab = cell(u, z, 1 - y, c)
        push(u, slab, slab, 18, dev_s)
        for j in range(3):
            arrived(u, cell(u, z_src[j], 1 - y, c, 1 - x, 0), 11 + j)
            arrived(u, cell(u, z_src[j], 1 - y, c, 1 - x, 1), 14 + j)
            slab = cell(u, z_src[j], 1 - y, c)
            push(u, slab, slab, 22 + j, dev_s)

    n = len(units)
    for u in range(n):
        begin(u)
    for t in range(n + 2):
        if t < n:
            spread(t)
        if 0 <= t - 1 < n:
            corner(t - 1)
        if 0 <= t - 2 < n:
            finish(t - 2)
    for u in range(n):
        arrived(u, cell(u, z, y, 1 - c), 17)
        arrived(u, cell(u, z, 1 - y, 1 - c), 18)
        for j in range(3):
            arrived(u, cell(u, z_src[j], y, 1 - c), 19 + j)
            arrived(u, cell(u, z_src[j], 1 - y, 1 - c), 22 + j)
        pltpu.make_async_copy(own(u, stage), cell(u, z, y, c), local.at[u]).wait()
        for j in (1, 2):

            @pl.when(inner)
            def _():
                relay_copy(u, cell(u, z_src[j], y, c, x), j).wait_send()

    for cp in started:
        cp.wait_send()


def gather_blocks(shards, collective_id):
    units = units_of(shards, 0.5)
    out = [
        jax.ShapeDtypeStruct((s.shape[0] // 2, 16 * s.shape[1], s.shape[2]), s.dtype)
        for s in shards
    ]
    n = len(units)
    return pl.pallas_call(
        functools.partial(gather_kernel, units, len(shards)),
        out_shape=out,
        in_specs=[pl.BlockSpec(memory_space=pl.ANY)] * len(shards),
        out_specs=[pl.BlockSpec(memory_space=pl.ANY)] * len(shards),
        scratch_shapes=[
            pltpu.SemaphoreType.DMA((n, 27)),
            pltpu.SemaphoreType.DMA((n, 25)),
            pltpu.SemaphoreType.DMA((n,)),
        ],
        compiler_params=pltpu.CompilerParams(collective_id=collective_id, has_side_effects=True),
        name="gather_blocks",
    )(*shards)


TOKENS = 256
HALF_LANES = 64
FORWARD_VMEM = 58 * 2**20


def lane_of(shape):
    return lax.broadcasted_iota(jnp.int32, shape, len(shape) - 1)


def norm_rows(hidden):
    center = hidden - jnp.mean(hidden, -1, keepdims=True)
    inverse = lax.rsqrt(jnp.mean(center * center, -1, keepdims=True) + EPS_NORM)
    return center * inverse, inverse


def gelu_and_slope(v):
    root = 0.7978845608028654
    square = v * v
    wave = jnp.tanh(root * (v + 0.044715 * (square * v)))
    near = 0.5 * (1.0 + wave)
    slope = near + (0.5 * root) * v * (1.0 - wave * wave) * (1.0 + (3 * 0.044715) * square)
    return v * near, slope


def both_heads(pair, first):
    zero = jnp.zeros_like(pair)
    return jnp.concatenate([jnp.where(first, pair, zero), jnp.where(first, zero, pair)], 0)


def step_forward_kernel(
    sizes,
    inputs,
    labels,
    seg_col,
    seg_row,
    same,
    hbm_qkv,
    hbm_o,
    hbm_up,
    hbm_down,
    hbm_side,
    gain_rows,
    out_latent,
    out_na,
    out_aa,
    out_qkv,
    out_p,
    out_ctx,
    out_nm,
    out_am,
    out_slope,
    out_gelu,
    out_stat,
    out_nf,
    out_af,
    out_tail,
    out_start,
    w_qkv,
    w_o,
    w_up,
    w_down,
    w_side,
    na,
    aa,
    qkv,
    prob,
    ctx,
    nm,
    am,
    slope,
    gelu,
    stat,
    nf,
    af,
    tail,
    start,
    hidden,
    w_sem,
    out_sem,
    last_sem,
):
    rows, length, classes, channels = sizes
    layers, width = w_qkv.shape[0], w_qkv.shape[1]
    loads = [(hbm_side, w_side, 0)]
    for layer in range(layers):
        for i, (src, dst) in enumerate(
            ((hbm_qkv, w_qkv), (hbm_o, w_o), (hbm_up, w_up), (hbm_down, w_down))
        ):
            loads.append((src.at[layer], dst.at[layer], 1 + 4 * layer + i))
    for src, dst, i in loads:
        pltpu.make_async_copy(src, dst, w_sem.at[i]).start()

    def ready(layer, i, dst):
        pltpu.make_async_copy(dst.at[layer], dst.at[layer], w_sem.at[1 + 4 * layer + i]).wait()

    def save(layer, i, src, dst):
        pltpu.make_async_copy(src, dst.at[layer], out_sem.at[layer, i]).start()

    table = classes
    start[:, :table] = (labels[...] == lane_of((TOKENS, table))).astype(jnp.bfloat16)
    start[:, table:] = inputs[...].astype(jnp.bfloat16)
    pltpu.make_async_copy(w_side, w_side, w_sem.at[0]).wait()
    hidden[...] = lax.dot_general(
        start[...],
        w_side[:, : table + LANES],
        (((1,), (1,)), ((), ())),
        preferred_element_type=jnp.float32,
    )

    def saves(layer):
        return (
            (na.at[layer], out_na),
            (aa.at[layer], out_aa),
            (qkv.at[layer], out_qkv),
            (prob.at[layer], out_p),
            (ctx.at[layer], out_ctx),
            (nm.at[layer], out_nm),
            (am.at[layer], out_am),
            (slope, out_slope),
            (gelu.at[layer], out_gelu),
            (stat.at[layer], out_stat),
        )

    for layer in range(layers):
        out = saves(layer)
        normed, inverse_a = norm_rows(hidden[...])
        na[layer] = normed
        save(layer, 0, *out[0])
        aa[layer] = (normed * gain_rows[2 * layer : 2 * layer + 1, :]).astype(jnp.bfloat16)
        save(layer, 1, *out[1])
        ready(layer, 0, w_qkv)

        @pl.loop(0, 3)
        def _(i):
            cols = pl.ds(pl.multiple_of(i * width, LANES), width)
            qkv[layer, :, cols] = jnp.dot(
                aa[layer], w_qkv[layer, :, cols], preferred_element_type=jnp.float32
            ).astype(jnp.bfloat16)

        save(layer, 2, *out[2])
        pairs = width // LANES
        for row in range(rows):
            toks = pl.ds(row * length, length)
            causal = lax.broadcasted_iota(jnp.int32, (length, length), 0) >= lane_of(
                (length, length)
            )
            attend = (seg_col[toks, :] == seg_row[row : row + 1, :]) & causal
            attend = jnp.concatenate([attend.astype(jnp.float32)] * 2, 0) > 0.5
            first = lane_of((length, LANES)) < HALF_LANES

            def each_pair(pair):
                def part(i):
                    return qkv[
                        layer, toks, pl.ds(i * width + pair * LANES, LANES)
                    ]

                query = both_heads(part(0), first)
                scores = (
                    lax.dot_general(
                        query, part(1), (((1,), (1,)), ((), ())), preferred_element_type=jnp.float32
                    )
                    * HEAD_DIM ** (-0.5)
                )
                scores = jnp.where(attend, scores, MASKED)
                expo = jnp.exp(scores - jnp.max(scores, -1, keepdims=True))
                soft = expo / jnp.sum(expo, -1, keepdims=True)
                prob[layer, row * pairs + pair] = soft
                mixed = jnp.dot(
                    soft.astype(jnp.bfloat16), part(2), preferred_element_type=jnp.float32
                )
                ctx[layer, toks, pl.ds(pair * LANES, LANES)] = jnp.where(
                    first, mixed[:length], mixed[length:]
                ).astype(jnp.bfloat16)

            for pair in range(pairs):
                each_pair(pair)

        save(layer, 3, *out[3])
        save(layer, 4, *out[4])
        ready(layer, 1, w_o)
        hidden[...] = hidden[...] + jnp.dot(
            ctx[layer], w_o[layer], preferred_element_type=jnp.float32
        )
        normed, inverse_m = norm_rows(hidden[...])
        nm[layer] = normed
        save(layer, 5, *out[5])
        am[layer] = (normed * gain_rows[2 * layer + 1 : 2 * layer + 2, :]).astype(jnp.bfloat16)
        save(layer, 6, *out[6])
        stat[layer] = jnp.where(lane_of((TOKENS, LANES)) == 0, inverse_a, inverse_m)
        save(layer, 9, *out[9])
        ready(layer, 2, w_up)
        if layer > 0:
            pltpu.make_async_copy(slope, slope, out_sem.at[layer - 1, 7]).wait()

        @pl.loop(0, w_up.shape[2] // width)
        def _(i):
            cols = pl.ds(pl.multiple_of(i * width, LANES), width)
            upper = jnp.dot(am[layer], w_up[layer, :, cols], preferred_element_type=jnp.float32)
            value, rate = gelu_and_slope(upper)
            gelu[layer, :, cols] = value.astype(jnp.bfloat16)
            slope[:, cols] = rate

        save(layer, 7, *out[7])
        save(layer, 8, *out[8])
        ready(layer, 3, w_down)
        half = width // 2

        @pl.loop(0, 2)
        def _(i):
            cols = pl.ds(pl.multiple_of(i * half, LANES), half)
            hidden[:, cols] = hidden[:, cols] + jnp.dot(
                gelu[layer], w_down[layer, :, cols], preferred_element_type=jnp.float32
            )

    normed, inverse_f = norm_rows(hidden[...])
    nf[...] = normed
    af[...] = (normed * gain_rows[2 * layers : 2 * layers + 1, :]).astype(jnp.bfloat16)
    prediction = jnp.dot(
        af[...], w_side[:, table + LANES :], preferred_element_type=jnp.float32
    )
    previous = pltpu.roll(prediction, 1, 0)
    lane = lane_of((TOKENS, LANES))
    shown = (same[...] > 0) & (lane < channels)
    shift_alpha = jnp.where(shown, pltpu.roll(previous, LANES - channels, 1), 0.0)
    shift_mu = jnp.where(shown, previous, 0.0)
    latent = (inputs[...] - shift_mu) * jnp.exp(-shift_alpha)
    logdet = -jnp.sum(shift_alpha, -1, keepdims=True)
    out_latent[...] = jnp.where(lane == channels, logdet + inputs[...], latent)
    tail[0] = latent
    tail[1] = shift_alpha
    tail[2] = jnp.broadcast_to(inverse_f, (TOKENS, LANES))
    final = ((nf, out_nf), (af, out_af), (tail, out_tail), (start, out_start))
    for i, (src, dst) in enumerate(final):
        pltpu.make_async_copy(src, dst, last_sem.at[i]).start()
    for layer in range(layers):
        for i, (src, dst) in enumerate(saves(layer)):
            if i != 7 or layer == layers - 1:
                pltpu.make_async_copy(src, dst.at[layer], out_sem.at[layer, i]).wait()
    for i, (src, dst) in enumerate(final):
        pltpu.make_async_copy(src, dst, last_sem.at[i]).wait()


def step_forward(inputs, labels, seg_ids, same, weights, gain_rows, table, channels):
    w_qkv, w_o, w_up, w_down, side = weights
    rows, length = seg_ids.shape
    layers, width, hidden = w_up.shape
    pairs = rows * width // LANES
    low, full = jnp.bfloat16, jnp.float32
    kept = [
        ((layers, TOKENS, width), full),
        ((layers, TOKENS, width), low),
        ((layers, TOKENS, 3 * width), low),
        ((layers, pairs, 2 * length, length), full),
        ((layers, TOKENS, width), low),
        ((layers, TOKENS, width), full),
        ((layers, TOKENS, width), low),
        ((layers, TOKENS, hidden), full),
        ((layers, TOKENS, hidden), low),
        ((layers, TOKENS, LANES), full),
        ((TOKENS, width), full),
        ((TOKENS, width), low),
        ((3, TOKENS, LANES), full),
        ((TOKENS, table + LANES), low),
    ]
    scratch = [pltpu.VMEM(w.shape, low) for w in weights]
    for i, (shape, kind) in enumerate(kept):
        scratch.append(pltpu.VMEM(shape[1:] if i == 7 else shape, kind))
    scratch += [
        pltpu.VMEM((TOKENS, width), full),
        pltpu.SemaphoreType.DMA((1 + 4 * layers,)),
        pltpu.SemaphoreType.DMA((layers, 10)),
        pltpu.SemaphoreType.DMA((4,)),
    ]
    vmem, hbm = pl.BlockSpec(memory_space=pltpu.VMEM), pl.BlockSpec(memory_space=pl.ANY)
    flops = 2 * TOKENS * (sum(w.size for w in weights))
    return pl.pallas_call(
        functools.partial(step_forward_kernel, (rows, length, table, channels)),
        out_shape=[jax.ShapeDtypeStruct((TOKENS, LANES), full)]
        + [jax.ShapeDtypeStruct(shape, kind) for shape, kind in kept],
        in_specs=[vmem] * 5 + [hbm] * 5 + [vmem],
        out_specs=[vmem] + [hbm] * len(kept),
        scratch_shapes=scratch,
        cost_estimate=pl.CostEstimate(flops=flops, bytes_accessed=50 * 2**20, transcendentals=0),
        compiler_params=pltpu.CompilerParams(vmem_limit_bytes=FORWARD_VMEM),
        name="step_forward",
    )(
        inputs,
        labels,
        seg_ids.reshape(TOKENS, 1),
        seg_ids,
        same,
        w_qkv,
        w_o,
        w_up,
        w_down,
        side,
        gain_rows,
    )


def norm_rows_back(normed, inverse, grad_normed):
    mean_grad = jnp.mean(grad_normed, -1, keepdims=True)
    mean_proj = jnp.mean(grad_normed * normed, -1, keepdims=True)
    return inverse * (grad_normed - mean_grad - normed * mean_proj)


def by_rows(left, right):
    return lax.dot_general(
        left, right, (((1,), (1,)), ((), ())), preferred_element_type=jnp.float32
    )


def down_columns(left, right):
    return lax.dot_general(
        left, right, (((0,), (0,)), ((), ())), preferred_element_type=jnp.float32
    )


def step_backward_kernel(
    sizes,
    grad_latent,
    same,
    hbm_qkv,
    hbm_o,
    hbm_up,
    hbm_down,
    hbm_side,
    gain_rows,
    in_na,
    in_qkv,
    in_p,
    in_nm,
    in_slope,
    in_stat,
    in_nf,
    in_tail,
    out_grad,
    out_gains,
    out_gqkv,
    out_gmid,
    out_gup,
    out_gbr,
    out_gstart,
    out_gpred,
    w_qkv,
    w_o,
    w_up,
    w_down,
    w_side,
    na,
    qkv,
    prob,
    nm,
    slope,
    stat,
    nf,
    tail,
    gqkv,
    gmid,
    gup,
    gbr,
    gstart,
    gpred,
    ghid,
    gact,
    gctx,
    w_sem,
    in_sem,
    out_sem,
    last_sem,
):
    rows, length, table, channels = sizes
    layers, width = w_qkv.shape[0], w_qkv.shape[1]
    pairs = width // LANES
    order = list(reversed(range(layers)))
    weights = ((hbm_down, w_down), (hbm_up, w_up), (hbm_o, w_o), (hbm_qkv, w_qkv))
    layered = ((in_slope, slope), (in_nm, nm), (in_p, prob), (in_qkv, qkv), (in_na, na))

    def load(src, dst, sem):
        return pltpu.make_async_copy(src, dst, sem)

    def layer_load(layer, i):
        src, dst = layered[i]
        return load(src.at[layer], dst if i == 0 else dst.at[layer], in_sem.at[layer, i])

    def weight_load(layer, i):
        src, dst = weights[i]
        return load(src.at[layer], dst.at[layer], w_sem.at[1 + 4 * layer + i])

    single = ((in_tail, tail), (in_nf, nf), (in_stat, stat))
    for i, (src, dst) in enumerate(single):
        load(src, dst, last_sem.at[i]).start()
    load(hbm_side, w_side, w_sem.at[0]).start()
    for layer in order:
        for i in range(4):
            weight_load(layer, i).start()
            if i > 0 or layer == order[0]:
                layer_load(layer, i).start()
        layer_load(layer, 4).start()

    def save(layer, i, src, dst):
        pltpu.make_async_copy(src, dst.at[layer], out_sem.at[layer, i]).start()

    lane = lane_of((TOKENS, LANES))
    load(in_tail, tail, last_sem.at[0]).wait()
    out_gains[...] = jnp.zeros_like(out_gains)
    scaled = grad_latent[...] * jnp.exp(-tail[1])
    grad_alpha = 1.0 - grad_latent[...] * tail[0]
    grad_prev = jnp.where(lane < channels, -scaled, pltpu.roll(grad_alpha, channels, 1))
    grad_prev = jnp.where((same[...] > 0) & (lane < 2 * channels), grad_prev, 0.0)
    gpred[...] = pltpu.roll(grad_prev, TOKENS - 1, 0).astype(jnp.bfloat16)
    out_gpred[...] = gpred[...]
    load(hbm_side, w_side, w_sem.at[0]).wait()
    gact[...] = by_rows(gpred[...], w_side[:, table + LANES :])
    load(in_nf, nf, last_sem.at[1]).wait()
    load(in_stat, stat, last_sem.at[2]).wait()

    def through_norm(normed, inverse, index):
        grad = gact[...]
        out_gains[index : index + 1, :] = jnp.sum(grad * normed, 0, keepdims=True)
        return norm_rows_back(normed, inverse, grad * gain_rows[index : index + 1, :])

    ghid[...] = through_norm(nf[...], tail[2][:, :1], 2 * layers)
    for layer in order:
        gbr[layer] = ghid[...].astype(jnp.bfloat16)
        save(layer, 3, gbr.at[layer], out_gbr)
        weight_load(layer, 0).wait()
        layer_load(layer, 0).wait()
        if layer != order[0]:
            pltpu.make_async_copy(gup, out_gup.at[layer + 1], out_sem.at[layer + 1, 2]).wait()

        @pl.loop(0, w_up.shape[2] // width)
        def _(i):
            cols = pl.ds(pl.multiple_of(i * width, LANES), width)
            gup[:, cols] = (by_rows(gbr[layer], w_down[layer, cols, :]) * slope[:, cols]).astype(
                jnp.bfloat16
            )

        save(layer, 2, gup, out_gup)
        if layer > 0:
            layer_load(layer - 1, 0).start()
        weight_load(layer, 1).wait()

        half = width // 2

        @pl.loop(0, 2)
        def _(i):
            cols = pl.ds(pl.multiple_of(i * half, LANES), half)
            gact[:, cols] = by_rows(gup[...], w_up[layer, cols, :])

        layer_load(layer, 1).wait()
        ghid[...] = ghid[...] + through_norm(nm[layer], stat[layer][:, 1:2], 2 * layer + 1)
        gmid[layer] = ghid[...].astype(jnp.bfloat16)
        save(layer, 1, gmid.at[layer], out_gmid)
        weight_load(layer, 2).wait()
        gctx[...] = by_rows(gmid[layer], w_o[layer]).astype(jnp.bfloat16)
        layer_load(layer, 2).wait()
        layer_load(layer, 3).wait()
        for row in range(rows):
            toks = pl.ds(row * length, length)
            first = lane_of((length, LANES)) < HALF_LANES

            def each_pair(pair):
                def at(i):
                    return pl.ds(i * width + pair * LANES, LANES)

                query = both_heads(qkv[layer, toks, at(0)], first)
                key = qkv[layer, toks, at(1)]
                value = qkv[layer, toks, at(2)]
                grad = both_heads(gctx[toks, at(0)], first)
                soft = prob[layer, row * pairs + pair]
                grad_soft = by_rows(grad, value)
                delta = jnp.sum(soft * grad_soft, -1, keepdims=True)
                grad_scores = (soft * (grad_soft - delta)).astype(jnp.bfloat16)
                factor = HEAD_DIM ** (-0.5)
                mixed = jnp.dot(grad_scores, key, preferred_element_type=jnp.float32) * factor
                gqkv[layer, toks, at(0)] = jnp.where(
                    first, mixed[:length], mixed[length:]
                ).astype(jnp.bfloat16)
                gqkv[layer, toks, at(1)] = (down_columns(grad_scores, query) * factor).astype(
                    jnp.bfloat16
                )
                gqkv[layer, toks, at(2)] = down_columns(soft.astype(jnp.bfloat16), grad).astype(
                    jnp.bfloat16
                )

            for pair in range(pairs):
                each_pair(pair)

        save(layer, 0, gqkv.at[layer], out_gqkv)
        weight_load(layer, 3).wait()

        @pl.loop(0, 2)
        def _(i):
            cols = pl.ds(pl.multiple_of(i * half, LANES), half)
            gact[:, cols] = by_rows(gqkv[layer], w_qkv[layer, cols, :])

        layer_load(layer, 4).wait()
        ghid[...] = ghid[...] + through_norm(na[layer], stat[layer][:, :1], 2 * layer)
    gstart[...] = ghid[...].astype(jnp.bfloat16)
    pltpu.make_async_copy(gstart, out_gstart, last_sem.at[3]).start()
    grad_inputs = scaled + jnp.dot(
        gstart[...], w_side[:, table : table + LANES], preferred_element_type=jnp.float32
    )
    out_grad[...] = jnp.where(lane < channels, grad_inputs, 0.0)
    pltpu.make_async_copy(gstart, out_gstart, last_sem.at[3]).wait()
    for layer in range(layers):
        done = ((gqkv.at[layer], out_gqkv), (gmid.at[layer], out_gmid), (gup, out_gup))
        done = done + ((gbr.at[layer], out_gbr),)
        for i, (src, dst) in enumerate(done):
            if i != 2 or layer == 0:
                pltpu.make_async_copy(src, dst.at[layer], out_sem.at[layer, i]).wait()


def step_backward(grad_latent, same, weights, gain_rows, kept, rows, length, table, channels):
    w_qkv, w_o, w_up, w_down, side = weights
    layers, width, hidden = w_up.shape
    na, aa, qkv, prob, ctx, nm, am, slope, gelu, stat, nf, af, tail, start = kept
    used = [na, qkv, prob, nm, slope, stat, nf, tail]
    low, full = jnp.bfloat16, jnp.float32
    made = [
        (layers, TOKENS, 3 * width),
        (layers, TOKENS, width),
        (layers, TOKENS, hidden),
        (layers, TOKENS, width),
        (TOKENS, width),
        (TOKENS, LANES),
    ]
    scratch = [pltpu.VMEM(w.shape, low) for w in weights]
    scratch += [
        pltpu.VMEM(part.shape[1:] if i == 4 else part.shape, part.dtype)
        for i, part in enumerate(used)
    ]
    scratch += [pltpu.VMEM(s[1:] if i == 2 else s, low) for i, s in enumerate(made)]
    scratch += [
        pltpu.VMEM((TOKENS, width), full),
        pltpu.VMEM((TOKENS, width), full),
        pltpu.VMEM((TOKENS, width), low),
        pltpu.SemaphoreType.DMA((1 + 4 * layers,)),
        pltpu.SemaphoreType.DMA((layers, 5)),
        pltpu.SemaphoreType.DMA((layers, 4)),
        pltpu.SemaphoreType.DMA((4,)),
    ]
    vmem, hbm = pl.BlockSpec(memory_space=pltpu.VMEM), pl.BlockSpec(memory_space=pl.ANY)
    flops = 2 * TOKENS * (sum(w.size for w in weights))
    return pl.pallas_call(
        functools.partial(step_backward_kernel, (rows, length, table, channels)),
        out_shape=[
            jax.ShapeDtypeStruct((TOKENS, LANES), full),
            jax.ShapeDtypeStruct((8, width), full),
        ]
        + [jax.ShapeDtypeStruct(shape, low) for shape in made],
        in_specs=[vmem] * 2 + [hbm] * 5 + [vmem] + [hbm] * len(used),
        out_specs=[vmem] * 2 + [hbm] * 5 + [vmem],
        scratch_shapes=scratch,
        cost_estimate=pl.CostEstimate(flops=flops, bytes_accessed=50 * 2**20, transcendentals=0),
        compiler_params=pltpu.CompilerParams(vmem_limit_bytes=FORWARD_VMEM),
        name="step_backward",
    )(grad_latent, same, w_qkv, w_o, w_up, w_down, side, gain_rows, *used)


def products_kernel(units, n_pairs, *refs):
    per = 2 * n_pairs
    first, middle, final = refs[:per], refs[per : 2 * per], refs[2 * per : 3 * per]
    gain_cols = refs[3 * per]
    outs = refs[3 * per + 1 : 3 * per + 6]
    rest = refs[3 * per + 6 :]
    bufs, made, turned = rest[:per], rest[per : per + 5], rest[per + 5]
    rest = rest[per + 6 :]
    n = len(units)
    acc, in_x, in_y, in_d, in_z = [rest[i * n : (i + 1) * n] for i in range(5)]
    in_sem, send, recv, local_out = rest[5 * n :]
    r, x, y, z, c = place()
    stage = z // 2
    other = 1 - stage
    zi = lax.rem(z, 2)
    dev_x = (r, 1 - x)
    dev_y = (r + 2 - 4 * y, x)
    dev_s = (r + 1 - 2 * c, x)
    z_dst = (z + 1 - 2 * zi, other * 2, other * 2 + 1)
    dev_z = tuple((zz * 4 + y * 2 + c, x) for zz in z_dst)
    barrier = pltpu.get_barrier_semaphore()
    partners = (dev_x, dev_y, dev_s) + dev_z
    for dev in partners:
        pl.semaphore_signal(barrier, 1, device_id=dev, device_id_type=MESH_ID)

    def loads(i, layer):
        def view(ref):
            return ref.at[layer] if len(ref.shape) == 3 else ref

        lower, upper = bufs[i].at[pl.ds(0, TOKENS)], bufs[i].at[pl.ds(TOKENS, TOKENS)]
        return view(first[i]), view(middle[i]), view(final[i]), lower, upper

    def fetch(i, layer):
        a, b, c, lower, upper = loads(i, layer)
        pltpu.make_async_copy(b, lower, in_sem.at[layer, 2 * i]).start()

        @pl.when(stage == 1)
        def _():
            pltpu.make_async_copy(c, upper, in_sem.at[layer, 2 * i + 1]).start()

        @pl.when(stage == 0)
        def _():
            pltpu.make_async_copy(a, upper, in_sem.at[layer, 2 * i + 1]).start()

    def fetched(i, layer):
        a, b, c, lower, upper = loads(i, layer)
        pltpu.make_async_copy(b, lower, in_sem.at[layer, 2 * i]).wait()
        pltpu.make_async_copy(a, upper, in_sem.at[layer, 2 * i + 1]).wait()

    for i in (8, 9, 10, 11):
        fetch(i, 0)
    for i in range(8):
        fetch(i, 0)
    pl.semaphore_wait(barrier, len(partners))
    started = {}

    def push(u, src, dst, slot, dev, idx=None):
        cp = pltpu.make_async_remote_copy(
            src_ref=src,
            dst_ref=dst,
            send_sem=send.at[u, slot],
            recv_sem=recv.at[u, slot if idx is None else idx],
            device_id=dev,
            device_id_type=MESH_ID,
        )
        cp.start()
        started[u, slot] = cp

    def arrived(u, dst, idx):
        wait_all_of(dst, recv.at[u, idx])

    def part_of(u, part):
        _, _, _, rows, half, (dim, cut) = units[u]
        if dim == 0:
            return (pl.ds(0, cut), pl.ds(0, half)) if part == 0 else (pl.ds(cut, rows - cut), pl.ds(0, half))
        return (pl.ds(0, rows), pl.ds(0, cut)) if part == 0 else (pl.ds(0, rows), pl.ds(cut, half - cut))

    block, strip = turned.shape[0], 3 * LANES

    def multiply(out, rows, right, m, begin, count, wide, extra=None):
        def one(cols, out_cols):
            product = jnp.dot(turned[...], right[:, cols], preferred_element_type=jnp.float32)
            if extra is not None:
                product = product + extra[...]
            product = product.astype(jnp.bfloat16)
            for k in range(block // rows):
                s = m * (block // rows) + k
                out[s // 4, (s // 2) % 2, s % 2, :, out_cols] = product[k * rows : (k + 1) * rows]

        if count == 1:
            one(slice(0, wide), slice(begin, begin + wide))
        else:

            @pl.loop(0, count)
            def _(i):
                cols = pl.ds(pl.multiple_of(i * wide, LANES), wide)
                one(cols, cols)

    def product(u):
        a, layer, _, rows, half, _ = units[u]
        if a == 4:
            for i in (8, 9, 10, 11):
                fetched(i, 0)
            turned[...] = bufs[9][...].T
            multiply(made[4], rows, bufs[8], 0, 0, bufs[8].shape[1] // strip, strip)
            turned[...] = bufs[10][...].T
            multiply(made[4], rows, bufs[11], 0, bufs[8].shape[1], 1, LANES, gain_cols)
        else:
            fetched(2 * a, layer)
            fetched(2 * a + 1, layer)
            if layer > 0:
                for h in range(2):
                    started.pop((u - 4, h)).wait_send()
            for m in range(bufs[2 * a].shape[1] // block):
                turned[...] = bufs[2 * a][:, m * block : (m + 1) * block].T
                multiply(made[a], rows, bufs[2 * a + 1], m, 0, 2 * half // strip, strip)
            if layer + 1 < units[-1][1] + 1:
                fetch(2 * a, layer + 1)
                fetch(2 * a + 1, layer + 1)
        for h in range(2):
            cols = pl.ds(h * half, half)
            push(u, made[a].at[:, :, 1 - c, :, cols], acc[u].at[:, :, h], h, dev_s)

    def chip_sum(u):
        a, layer, _, rows, half, _ = units[u]
        for h in range(2):
            arrived(u, acc[u].at[:, :, h], h)

        @pl.loop(0, 4)
        def _(zz):
            for yy in range(2):
                for h in range(2):
                    mine = made[a][zz, yy, c, :, h * half : (h + 1) * half]
                    acc[u][zz, yy, h] = acc[u][zz, yy, h] + mine

        for part, dev in ((0, dev_y), (1, dev_x)):
            rs, cs = part_of(u, part)
            push(u, acc[u].at[:, 1 - y, 1 - x, rs, cs], in_d[u].at[:, rs, cs], 2 + part, dev)

    def side_sum(u):
        for part, yy, h, dev, into in ((0, y, 1 - x, dev_x, in_x), (1, 1 - y, x, dev_y, in_y)):
            rs, cs = part_of(u, part)
            arrived(u, in_d[u].at[:, rs, cs], 2 + part)

            @pl.loop(0, 4)
            def _(zz):
                acc[u][zz, yy, h, rs, cs] = acc[u][zz, yy, h, rs, cs] + in_d[u][zz, rs, cs]

            push(u, acc[u].at[:, yy, h], into[u], 4 + part, dev)

    def plane_sum(u):
        arrived(u, in_x[u], 4)
        arrived(u, in_y[u], 5)

        @pl.loop(0, 4)
        def _(zz):
            acc[u][zz, y, x] = (
                acc[u][zz, y, x].astype(jnp.float32)
                + in_x[u][zz].astype(jnp.float32)
                + in_y[u][zz].astype(jnp.float32)
            ).astype(jnp.bfloat16)

        for i in range(2):
            push(u, acc[u].at[z_dst[1 + i], y, x], in_z[u].at[1 + zi], 7 + i, dev_z[1 + i], idx=7 + zi)
        push(u, acc[u].at[z_dst[0], y, x], in_z[u].at[0], 6, dev_z[0])

    def owned(u, b, h):
        a, layer, layers, _, half, _ = units[u]
        return outs[a].at[layers * b + layer, :, pl.ds(pl.multiple_of(h * half, LANES), half)]

    def totals(u):
        return ((acc[u].at[z, y, x], stage), (in_z[u].at[1], other))

    def total(u):
        for j in range(3):
            arrived(u, in_z[u].at[j], 6 + j)
        acc[u][z, y, x] = acc[u][z, y, x] + in_z[u][0]
        in_z[u][1] = in_z[u][1] + in_z[u][2]
        for k, (src, b) in enumerate(totals(u)):
            push(u, src, owned(u, b, x), 9 + k, dev_x)
            pltpu.make_async_copy(src, owned(u, b, x), local_out.at[u, k]).start()

    lags = (0, 1, 3, 5, 7)
    for t in range(n + lags[-1]):
        for lag, part in zip(lags, (product, chip_sum, side_sum, plane_sum, total)):
            if 0 <= t - lag < n:
                part(t - lag)
    for u in range(n):
        for k, (src, b) in enumerate(totals(u)):
            arrived(u, owned(u, b, 1 - x), 9 + k)
            pltpu.make_async_copy(src, owned(u, b, x), local_out.at[u, k]).wait()
    for cp in started.values():
        cp.wait_send()


def summed_products(operands, gain_cols, shards, collective_id):
    low = jnp.bfloat16
    out = [jax.ShapeDtypeStruct(s.shape, low) for s in shards]
    units = units_of(out, 0.75)
    n = len(units)
    layers = max(u[1] for u in units) + 1
    n_pairs = len(operands[0]) // 2
    width = operands[0][0].shape[-1]
    hbm, vmem = pl.BlockSpec(memory_space=pl.ANY), pl.BlockSpec(memory_space=pltpu.VMEM)

    def slots(lead):
        return [pltpu.VMEM(lead + (u[3], u[4]), low) for u in units]

    return pl.pallas_call(
        functools.partial(products_kernel, units, n_pairs),
        out_shape=out,
        in_specs=[hbm] * (6 * n_pairs) + [vmem],
        out_specs=[hbm] * 5,
        scratch_shapes=[
            pltpu.VMEM((2 * TOKENS, part.shape[-1]), low) for part in operands[0]
        ]
        + [pltpu.VMEM((4, 2, 2) + s.shape[1:], low) for s in shards]
        + [pltpu.VMEM((width, 2 * TOKENS), low)]
        + slots((4, 2, 2))
        + slots((4,))
        + slots((4,))
        + slots((4,))
        + slots((3,))
        + [
            pltpu.SemaphoreType.DMA((layers, 4 * n_pairs)),
            pltpu.SemaphoreType.DMA((n, 11)),
            pltpu.SemaphoreType.DMA((n, 11)),
            pltpu.SemaphoreType.DMA((n, 2)),
        ],
        compiler_params=pltpu.CompilerParams(
            collective_id=collective_id, has_side_effects=True, vmem_limit_bytes=62 * 2**20
        ),
        name="summed_products",
    )(*[part for step in operands for part in step], gain_cols)


def dot(left, right, dims=((1,), (0,))):
    return lax.dot_general(left, right, (dims, ((), ())), preferred_element_type=jnp.float32)


def normalize(hidden):
    center = hidden - jnp.mean(hidden, -1, keepdims=True)
    inverse = lax.rsqrt(jnp.mean(center * center, -1, keepdims=True) + EPS_NORM)
    return (center * inverse, inverse)


def normalize_back(normed, inverse, grad_normed):
    mean_grad = jnp.mean(grad_normed, -1, keepdims=True)
    mean_proj = jnp.mean(grad_normed * normed, -1, keepdims=True)
    return inverse * (grad_normed - mean_grad - normed * mean_proj)


def padded(count, unit):
    return -(-count // unit) * unit


def side_columns(classes, channels, out, gains):
    table = padded(classes, LANES)
    last = table + padded(channels, LANES)
    return table, last, padded(last + out + gains, 2 * LANES)


def pack_side(w_table, w_in, w_out, gains):
    blocks, classes, shard = w_table.shape
    channels, out, gain_count = w_in.shape[1], w_out.shape[2], gains.shape[1]
    table, last, total = side_columns(classes, channels, out, gain_count)

    def gap(count):
        return jnp.zeros((blocks, shard, count), w_table.dtype)

    return jnp.concatenate(
        [
            jnp.swapaxes(w_table, 1, 2),
            gap(table - classes),
            jnp.swapaxes(w_in, 1, 2),
            gap(last - table - channels),
            w_out,
            jnp.swapaxes(gains, 1, 2),
            gap(total - last - out - gain_count),
        ],
        2,
    )


def split_side(side, classes, channels, out, gains):
    table, last, _ = side_columns(classes, channels, out, gains)
    return (
        jnp.swapaxes(side[..., :classes], -1, -2),
        jnp.swapaxes(side[..., table : table + channels], -1, -2),
        side[..., last : last + out],
        jnp.swapaxes(side[..., last + out : last + out + gains], -1, -2),
    )


def heads_of(flat, rows):
    return flat.reshape(rows, -1, HEADS, HEAD_DIM)


def attention_scores(query, key_rows, attend):
    scores = jnp.einsum(
        "rqhd,rkhd->rhqk", query, key_rows, preferred_element_type=jnp.float32
    ) * HEAD_DIM ** (-0.5)
    return jnp.where(attend[:, None], scores, MASKED)


def forward_block(inputs, seg_ids, labels, weights, sizes):
    w_qkv, w_o, w_up, w_down, side = weights
    classes, channels, out, gain_count = sizes
    table, last, _ = side_columns(*sizes)
    rows, length, _ = inputs.shape
    tokens = rows * length
    width = side.shape[0]
    places = jnp.arange(length, dtype=jnp.int32)
    attend = (seg_ids[:, :, None] == seg_ids[:, None, :]) & (
        places[None, :, None] >= places[None, None, :]
    )
    same_seg = jnp.concatenate(
        [jnp.zeros((rows, 1), bool), seg_ids[:, 1:] == seg_ids[:, :-1]], 1
    )[..., None]
    onehot = labels.reshape(tokens, 1) == jnp.arange(table)[None, :]
    start = jnp.concatenate(
        [
            onehot.astype(jnp.bfloat16),
            inputs.reshape(tokens, channels).astype(jnp.bfloat16),
            jnp.zeros((tokens, last - table - channels), jnp.bfloat16),
        ],
        1,
    )
    gain_rows = side[:, last + out : last + out + gain_count].astype(jnp.float32).T
    hidden = dot(start, side[:, :last], ((1,), (1,)))
    kept = []
    for layer in range(w_qkv.shape[0]):
        normed_a, inverse_a = normalize(hidden)
        act_a = (normed_a * gain_rows[2 * layer]).astype(jnp.bfloat16)
        qkv = dot(act_a, w_qkv[layer]).astype(jnp.bfloat16)
        query, key_rows, value_rows = [
            heads_of(qkv[:, i * width : (i + 1) * width], rows) for i in range(3)
        ]
        scores = attention_scores(query, key_rows, attend)
        row_top = jnp.max(scores, -1, keepdims=True)
        expo_rows = jnp.exp(scores - row_top)
        row_total = jnp.sum(expo_rows, -1, keepdims=True)
        soft_low = (expo_rows / row_total).astype(jnp.bfloat16)
        log_total = row_top + jnp.log(row_total)
        context = jnp.einsum(
            "rhqk,rkhd->rqhd", soft_low, value_rows, preferred_element_type=jnp.float32
        )
        context = context.reshape(tokens, width).astype(jnp.bfloat16)
        middle = hidden + dot(context, w_o[layer])
        normed_m, inverse_m = normalize(middle)
        act_m = (normed_m * gain_rows[2 * layer + 1]).astype(jnp.bfloat16)
        upper = dot(act_m, w_up[layer])
        gelu_low = jax.nn.gelu(upper, approximate=True).astype(jnp.bfloat16)
        hidden = middle + dot(gelu_low, w_down[layer])
        kept.append(
            (
                normed_a,
                inverse_a,
                act_a,
                qkv,
                log_total,
                context,
                normed_m,
                inverse_m,
                act_m,
                upper,
                gelu_low,
            )
        )
    normed_f, inverse_f = normalize(hidden)
    act_f = (normed_f * gain_rows[gain_count - 1]).astype(jnp.bfloat16)
    prediction = dot(act_f, side[:, last : last + out]).reshape(rows, length, out)
    previous = jnp.concatenate([jnp.zeros((rows, 1, out), jnp.float32), prediction[:, :-1]], 1)
    shift = jnp.where(same_seg, previous, 0.0)
    shift_alpha = shift[..., channels:]
    latent = (inputs - shift[..., :channels]) * jnp.exp(-shift_alpha)
    saved = (attend, same_seg, start, kept, normed_f, inverse_f, act_f, shift_alpha, latent)
    return (latent, -jnp.sum(shift_alpha, -1), saved)


def backward_block(grad_latent, saved, weights, sizes):
    w_qkv, w_o, w_up, w_down, side = weights
    classes, channels, out, gain_count = sizes
    table, last, _ = side_columns(*sizes)
    attend, same_seg, start, kept, normed_f, inverse_f, act_f, shift_alpha, latent = saved
    rows, length, _ = latent.shape
    tokens = rows * length
    width = side.shape[0]
    factor = HEAD_DIM ** (-0.5)
    gain_rows = side[:, last + out : last + out + gain_count].astype(jnp.float32).T
    scale_back = jnp.exp(-shift_alpha)
    grad_inputs = grad_latent * scale_back
    grad_prev = jnp.where(
        same_seg, jnp.concatenate([-grad_inputs, 1.0 - grad_latent * latent], 2), 0.0
    )
    grad_pred = jnp.concatenate([grad_prev[:, 1:], jnp.zeros((rows, 1, out), jnp.float32)], 1)
    grad_pred = grad_pred.reshape(tokens, out).astype(jnp.bfloat16)
    grad_act = dot(grad_pred, side[:, last : last + out], ((1,), (1,)))
    gain_grads = [None] * gain_count
    gain_grads[-1] = jnp.sum(grad_act * normed_f, 0)
    grad_hidden = normalize_back(normed_f, inverse_f, grad_act * gain_rows[gain_count - 1])
    pairs = [None] * w_qkv.shape[0]
    for layer in reversed(range(w_qkv.shape[0])):
        (
            normed_a,
            inverse_a,
            act_a,
            qkv,
            log_total,
            context,
            normed_m,
            inverse_m,
            act_m,
            upper,
            gelu_low,
        ) = kept[layer]
        grad_branch = grad_hidden.astype(jnp.bfloat16)
        grad_gelu = dot(grad_branch, w_down[layer], ((1,), (1,)))
        gelu_pull = jax.vjp(partial(jax.nn.gelu, approximate=True), upper)[1]
        grad_upper = gelu_pull(grad_gelu)[0].astype(jnp.bfloat16)
        grad_act_m = dot(grad_upper, w_up[layer], ((1,), (1,)))
        gain_grads[2 * layer + 1] = jnp.sum(grad_act_m * normed_m, 0)
        grad_middle = grad_hidden + normalize_back(
            normed_m, inverse_m, grad_act_m * gain_rows[2 * layer + 1]
        )
        grad_mid_low = grad_middle.astype(jnp.bfloat16)
        grad_context = heads_of(
            dot(grad_mid_low, w_o[layer], ((1,), (1,))).astype(jnp.bfloat16), rows
        )
        query, key_rows, value_rows = [
            heads_of(qkv[:, i * width : (i + 1) * width], rows) for i in range(3)
        ]
        soft_rows = jnp.exp(attention_scores(query, key_rows, attend) - log_total)
        soft_low = soft_rows.astype(jnp.bfloat16)
        grad_soft = jnp.einsum(
            "rqhd,rkhd->rhqk", grad_context, value_rows, preferred_element_type=jnp.float32
        )
        row_delta = jnp.sum(soft_rows * grad_soft, -1, keepdims=True)
        grad_scores = (soft_rows * (grad_soft - row_delta)).astype(jnp.bfloat16)
        grad_query = factor * jnp.einsum(
            "rhqk,rkhd->rqhd", grad_scores, key_rows, preferred_element_type=jnp.float32
        )
        grad_keys = factor * jnp.einsum(
            "rhqk,rqhd->rkhd", grad_scores, query, preferred_element_type=jnp.float32
        )
        grad_values = jnp.einsum(
            "rhqk,rqhd->rkhd", soft_low, grad_context, preferred_element_type=jnp.float32
        )
        grad_qkv = jnp.concatenate(
            [part.reshape(tokens, width) for part in (grad_query, grad_keys, grad_values)], 1
        ).astype(jnp.bfloat16)
        grad_act_a = dot(grad_qkv, w_qkv[layer], ((1,), (1,)))
        gain_grads[2 * layer] = jnp.sum(grad_act_a * normed_a, 0)
        grad_hidden = grad_middle + normalize_back(
            normed_a, inverse_a, grad_act_a * gain_rows[2 * layer]
        )
        pairs[layer] = (
            (act_a, grad_qkv),
            (context, grad_mid_low),
            (act_m, grad_upper),
            (gelu_low, grad_branch),
        )
    grad_start = grad_hidden.astype(jnp.bfloat16)
    grad_inputs = grad_inputs + dot(grad_start, side[:, table : table + channels]).reshape(
        rows, length, channels
    )
    return grad_inputs, (
        pairs,
        (start, grad_start),
        (act_f, grad_pred),
        jnp.stack(gain_grads, 1),
    )


def weight_grads(parts, side_total):
    pairs, (start, grad_start), (act_f, grad_pred), gain_grads = parts
    arrays = [
        jnp.stack([dot(*layer[i], ((0,), (0,))).astype(jnp.bfloat16) for layer in pairs], 0)
        for i in range(4)
    ]
    side = [
        dot(grad_start, start, ((0,), (0,))),
        dot(act_f, grad_pred, ((0,), (0,))),
        gain_grads,
    ]
    count = sum(part.shape[1] for part in side)
    side.append(jnp.zeros((gain_grads.shape[0], side_total - count), jnp.float32))
    side = jnp.concatenate(side, 1).astype(jnp.bfloat16)
    return arrays + [side[None]]


def adam_step(weight, first, second, grad, rate):
    first_new = BETA_ONE * first + (1.0 - BETA_ONE) * grad
    second_new = BETA_TWO * second + (1.0 - BETA_TWO) * grad * grad
    first_hat = first_new / (1.0 - BETA_ONE**STEP)
    second_hat = second_new / (1.0 - BETA_TWO**STEP)
    weight_new = weight - rate * (first_hat / (jnp.sqrt(second_hat) + EPS_ADAM) + DECAY * weight)
    return (first_new, second_new, weight_new)


def segment_of(places, seg_ends):
    return jnp.sum((places[None, :, None] >= seg_ends[:, None, :]).astype(jnp.int32), -1)


def row_facts(seg_lengths, class_labels, length):
    seg_ids = segment_of(jnp.arange(length, dtype=jnp.int32), jnp.cumsum(seg_lengths, 1))
    picked = seg_ids[:, :, None] == jnp.arange(SEGS)[None, None, :]
    return seg_ids, jnp.sum(jnp.where(picked, class_labels[:, None, :], 0), -1)


def staged(mine, low, sizes):
    half = lax.axis_size("rows") // 2
    second = lax.axis_index("rows") >= half
    swap = [(i, (i + half) % (2 * half)) for i in range(2 * half)]
    up = [(i, i + half) for i in range(half)]
    down = [(i + half, i) for i in range(half)]
    classes, channels, out, gain_count = sizes
    table, last, _ = side_columns(*sizes)
    rows, length, _ = mine[0].shape

    def wide(part):
        return jnp.pad(part, ((0, 0), (0, 0), (0, LANES - part.shape[2])))

    def back(part):
        return part.reshape(rows, length, LANES)[:, ::-1].reshape(TOKENS, LANES)

    mine = (wide(mine[0]), wide(mine[1])) + mine[2:]
    theirs = [lax.ppermute(part, "rows", swap) for part in mine]
    batch = [
        [jnp.where(second, b, a) for a, b in zip(mine, theirs)],
        [jnp.where(second, a, b) for a, b in zip(mine, theirs)],
    ]
    for part in batch:
        part[0] = part[0].reshape(TOKENS, LANES)
        part[1] = part[1].reshape(TOKENS, LANES)
    facts = []
    for index in range(3):
        ahead, behind = batch[min(index, 1)], batch[max(index - 1, 0)]
        seg_ids, labels = [jnp.where(second, behind[i][:, ::-1], ahead[i]) for i in (2, 3)]
        same = seg_ids[:, 1:] == seg_ids[:, :-1]
        same = jnp.pad(same.astype(jnp.int32), ((0, 0), (1, 0))).reshape(TOKENS, 1)
        facts.append((labels.reshape(TOKENS, 1), seg_ids, same))
    weights = list(gather_blocks(low, 1))
    weights[4] = weights[4][0]
    gain_rows = weights[4][:, last + out : last + out + gain_count].astype(jnp.float32).T
    gain_rows = jnp.pad(gain_rows, ((0, 8 - gain_count), (0, 0)))
    steps = []
    arrived = jnp.zeros((TOKENS, LANES), jnp.float32)
    for index in range(3):
        inputs = jnp.where(second, arrived, batch[min(index, 1)][0])
        steps.append(step_forward(inputs, *facts[index], weights, gain_rows, table, channels))
        if index < 2:
            arrived = back(lax.ppermute(steps[-1][0], "rows", up))
    made = []
    returned = jnp.zeros((TOKENS, LANES), jnp.float32)
    for index in range(3):
        grad_latent = jnp.where(second, batch[max(1 - index, 0)][1], returned)
        made.append(
            step_backward(
                grad_latent,
                facts[2 - index][2],
                weights,
                gain_rows,
                steps[2 - index][1:],
                rows,
                length,
                table,
                channels,
            )
        )
        if index < 2:
            returned = back(lax.ppermute(made[-1][0], "rows", down))
    gain_grads = made[1][1] + jnp.where(second, made[0][1], made[2][1])
    gain_cols = jnp.pad(gain_grads[:gain_count].T, ((0, 0), (out, LANES - out - gain_count)))

    def operands(step, grads):
        _, na, aa, qkv, prob, ctx, nm, am, slope, gelu, stat, nf, af, tail, start = step
        _, _, gqkv, gmid, gup, gbr, gstart, gpred = grads
        return (aa, gqkv, ctx, gmid, am, gup, gelu, gbr, start, gstart, af, gpred)

    sums = summed_products(
        [operands(steps[i], made[2 - i]) for i in range(3)], gain_cols, low, 2
    )
    sent = jnp.where(second, steps[1][0], made[1][0])
    received = lax.ppermute(sent, "rows", swap)
    outcome = jnp.where(second, steps[2][0], received).reshape(rows, length, LANES)
    patch_grad = jnp.where(second, received, made[2][0]).reshape(rows, length, LANES)
    return outcome[..., : channels + 1], patch_grad[..., :channels], sums


def unstaged(mine, low, sizes):
    inputs, cotangent, seg_ids, labels = mine
    whole = [lax.all_gather(part, "rows", axis=1, tiled=True) for part in low]

    def block(index):
        picked = [part[index * LAYERS : (index + 1) * LAYERS] for part in whole[:4]]
        return picked + [whole[4][index]]

    back = seg_ids[:, ::-1], labels[:, ::-1]
    latent_one, det_one, saved_one = forward_block(inputs, seg_ids, labels, block(0), sizes)
    latent_two, det_two, saved_two = forward_block(latent_one[:, ::-1], *back, block(1), sizes)
    outcome = jnp.concatenate([latent_two, (det_two + det_one[:, ::-1])[..., None]], 2)
    grad_mid, parts_two = backward_block(cotangent, saved_two, block(1), sizes)
    patch_grad, parts_one = backward_block(grad_mid[:, ::-1], saved_one, block(0), sizes)
    grads = [
        jnp.concatenate(pair, 0)
        for pair in zip(
            weight_grads(parts_one, low[4].shape[2]), weight_grads(parts_two, low[4].shape[2])
        )
    ]
    sums = [
        lax.psum(
            lax.psum_scatter(grad, "rows", scatter_dimension=1, tiled=True).astype(jnp.float32),
            "seq",
        )
        for grad in grads
    ]
    return outcome, patch_grad, sums


def body(
    patches,
    seg_lengths,
    class_labels,
    cotangent,
    w_in,
    m_in,
    v_in,
    w_table,
    m_table,
    v_table,
    w_qkv,
    m_qkv,
    v_qkv,
    w_o,
    m_o,
    v_o,
    w_up,
    m_up,
    v_up,
    w_down,
    m_down,
    v_down,
    w_out,
    m_out,
    v_out,
    gains,
    m_gains,
    v_gains,
):
    masters = (w_in, w_table, w_qkv, w_o, w_up, w_down, w_out, gains)
    low = [weight.astype(jnp.bfloat16) for weight in masters]
    sizes = (w_table.shape[1], w_in.shape[1], w_out.shape[2], gains.shape[1])
    shards = low[2:6] + [pack_side(low[1], low[0], low[6], low[7])]
    held, group, channels = patches.shape
    seq_count = lax.axis_size("seq")
    length = group * seq_count
    share = max(1, held // seq_count)
    copies = seq_count * share // held
    first_row = (lax.axis_index("seq") // copies) * share
    pieces = jnp.concatenate([patches.astype(jnp.float32), cotangent], 2)
    pieces = lax.all_gather(pieces, "seq", axis=1, tiled=True)
    pieces = lax.dynamic_slice_in_dim(pieces, first_row, share, 0)
    seg_ids, labels = row_facts(
        lax.dynamic_slice_in_dim(seg_lengths, first_row, share, 0),
        lax.dynamic_slice_in_dim(class_labels, first_row, share, 0),
        length,
    )
    mine = (pieces[..., :channels], pieces[..., channels:], seg_ids, labels)
    two_stages = seq_count == 2 and lax.axis_size("rows") == 16 and copies == 1
    outcome, patch_grad, sums = (staged if two_stages else unstaged)(mine, shards, sizes)
    results = lax.all_gather(jnp.concatenate([outcome, patch_grad], 2), "seq", axis=0)
    results = results[::copies].reshape((held,) + results.shape[2:])
    results = lax.dynamic_slice_in_dim(results, lax.axis_index("seq") * group, group, 1)
    sums = [total.astype(jnp.float32) / copies for total in sums]
    table, first, last, gain = split_side(sums[4], *sizes)
    grads = (first, table, sums[0], sums[1], sums[2], sums[3], last, gain)
    firsts = (m_in, m_table, m_qkv, m_o, m_up, m_down, m_out, m_gains)
    seconds = (v_in, v_table, v_qkv, v_o, v_up, v_down, v_out, v_gains)
    updates = [adam_step(*item) for item in zip(masters, firsts, seconds, grads, RATES)]
    return (
        results[..., :channels],
        results[..., channels],
        results[..., channels + 1 :],
    ) + tuple(part for update in updates for part in update)


def solution(mesh):
    tokens = P("rows", "seq", None)
    row = P("rows", None)
    last, middle = P(None, None, "rows"), P(None, "rows", None)
    weights = (last,) * 6 + (middle,) * 15 + (last,) * 3
    return jax.shard_map(
        body,
        mesh=mesh,
        in_specs=(tokens, row, row, tokens) + weights,
        out_specs=(tokens, P("rows", "seq"), tokens) + weights,
        check_vma=False,
    )
```

```python
import functools
from functools import partial

import jax
import jax.numpy as jnp
from jax import lax
from jax.experimental import pallas as pl
from jax.experimental.pallas import tpu as pltpu
from jax.sharding import PartitionSpec as P

HEADS = 12
HEAD_DIM = 64
LAYERS = 2
SEGS = 4
STEP = 10

EPS_NORM = 1e-05
MASKED = -1000000000.0
BETA_ONE = 0.9
BETA_TWO = 0.95
EPS_ADAM = 1e-08
DECAY = 0.1
RATES = (0.05, 0.3, 0.02, 0.05, 0.02, 0.01, 0.01, 0.3)

MESH_ID = pl.DeviceIdType.MESH
LANES = 128
LATE = (0, 1, 2)
GATHER_LAGS = (1.5, 3.5, 5.5, 8.5, 0.0, 1.0, 1.7, 3.0)


def place():
    r = lax.axis_index("rows")
    x = lax.axis_index("seq")
    c = lax.rem(r, 2)
    y = lax.rem(r // 2, 2)
    z = r // 4
    return r, x, y, z, c


def units_of(shards, d1_share):
    units = []
    order = sorted(range(len(shards)), key=lambda a: shards[a].shape[0])
    layers = max(s.shape[0] // 2 for s in shards)
    todo = [(a, 0) for a in order if shards[a].shape[0] == 2]
    for l in range(layers):
        todo += [(a, l) for a in order if shards[a].shape[0] > 2]
    for a, l in todo:
        n, rows, cols = shards[a].shape
        half = cols // 2
        if rows >= 64:
            first = max(16, round(rows * d1_share / 16) * 16)
            split = (0, first)
        else:
            first = max(LANES, round(half * d1_share / LANES) * LANES)
            split = (1, first)
        units.append((a, l, n // 2, rows, half, split))
    return units


def wait_all_of(cell, sem):
    pltpu.make_async_copy(cell, cell, sem).wait()


def gather_kernel(units, late, lags, n_arrays, *refs):
    srcs, outs = refs[:n_arrays], refs[n_arrays : 2 * n_arrays]
    send, recv, local = refs[2 * n_arrays :]
    r, x, y, z, c = place()
    stage = z // 2
    other = 1 - stage
    zi = lax.rem(z, 2)
    dev_x = (r, 1 - x)
    dev_y = (r + 2 - 4 * y, x)
    dev_s = (r + 1 - 2 * c, x)
    z_near = z + 1 - 2 * zi
    z_src = (z_near, other * 2, other * 2 + 1)
    dev_z = tuple((zz * 4 + y * 2 + c, x) for zz in z_src)
    barrier = pltpu.get_barrier_semaphore()
    partners = (dev_x, dev_y, dev_s) + dev_z
    for dev in partners:
        pl.semaphore_signal(barrier, 1, device_id=dev, device_id_type=MESH_ID)
    pl.semaphore_wait(barrier, len(partners))

    inner = stage != zi
    dev_inner = ((1 + other) * 4 + y * 2 + c, x)
    side_of = jnp.where(inner, other, stage)
    z_mine, z_theirs = 2 * side_of, 2 - 2 * side_of
    started = []

    def cell(u, zz, yy, cc, h=None, part=None):
        a, l, _, rows, half, (dim, first) = units[u]
        row0, nrow = (zz * 4 + yy * 2 + cc) * rows, rows
        col0, ncol = (0, 2 * half) if h is None else (h * half, half)
        if part is not None:
            if dim == 0:
                row0, nrow = (row0, first) if part == 0 else (row0 + first, rows - first)
            else:
                col0, ncol = (col0, first) if part == 0 else (col0 + first, half - first)
        if h is not None:
            col0 = pl.multiple_of(col0, LANES)
        return outs[a].at[l, pl.ds(pl.multiple_of(row0, 16), nrow), pl.ds(col0, ncol)]

    def own(u, b, h=None):
        a, l, layers, rows, half, _ = units[u]
        if h is None:
            return srcs[a].at[layers * b + l]
        return srcs[a].at[layers * b + l, :, pl.ds(pl.multiple_of(h * half, LANES), half)]

    def push(u, src, dst, idx, dev, slot=None):
        cp = pltpu.make_async_remote_copy(
            src_ref=src,
            dst_ref=dst,
            send_sem=send.at[u, idx if slot is None else slot],
            recv_sem=recv.at[u, idx],
            device_id=dev,
            device_id_type=MESH_ID,
        )
        cp.start()
        started.append(cp)

    def arrived(u, dst, idx):
        wait_all_of(dst, recv.at[u, idx])

    def relay_copy(u, piece, j):
        return pltpu.make_async_remote_copy(
            src_ref=piece,
            dst_ref=piece,
            send_sem=send.at[u, 24 + j],
            recv_sem=recv.at[u, j],
            device_id=dev_z[0],
            device_id_type=MESH_ID,
        )

    def relay(u, piece, j):
        @pl.when(inner)
        def _():
            relay_copy(u, piece, j).start()

    def begin(u):
        mine = cell(u, z, y, c, x)
        push(u, own(u, other, x), mine, 1 + zi, dev_inner, slot=1)
        if u in late:

            @pl.when(inner)
            def _():
                near_copy(u).start()

            @pl.when(jnp.logical_not(inner))
            def _():
                own_copy(u).start()

            return
        push(u, own(u, stage, x), mine, 0, dev_z[0])
        push(u, own(u, stage, x), mine, 10, dev_y)
        push(u, own(u, stage), cell(u, z, y, c), 17, dev_s)
        pltpu.make_async_copy(own(u, stage), cell(u, z, y, c), local.at[u]).start()

    def near_copy(u):
        return pltpu.make_async_remote_copy(
            src_ref=own(u, stage, x),
            dst_ref=cell(u, z, y, c, x),
            send_sem=send.at[u, 0],
            recv_sem=recv.at[u, 1 + zi],
            device_id=dev_z[0],
            device_id_type=MESH_ID,
        )

    def own_copy(u):
        return pltpu.make_async_copy(own(u, stage, x), cell(u, z, y, c, x), recv.at[u, 1 + zi])

    def near(u):
        if u in late:
            return
        arrived(u, cell(u, z, 1 - y, c, x), 10)
        push(u, cell(u, z, 1 - y, c, x), cell(u, z, 1 - y, c, x), 6, dev_x)
        side(u, 0, z_src[0], 0)

    def side(u, j, zz, idx):
        piece = cell(u, zz, y, c, x)
        arrived(u, piece, idx)
        if u not in late and j > 0:
            relay(u, piece, j)
        push(u, piece, piece, 3 + j, dev_x)
        push(u, piece, piece, 7 + j, dev_y)

    def spread(u):
        if u in late:
            for j in range(2):
                side(u, j, z_mine + j, 1 + j)
        else:
            for j in (1, 2):
                side(u, j, z_src[j], j)

    def turn(u, j, zz):
        arrived(u, cell(u, zz, y, c, 1 - x), 3 + j)
        part = cell(u, zz, y, c, 1 - x, 0)
        push(u, part, part, 11 + j, dev_y)
        arrived(u, cell(u, zz, 1 - y, c, x), 7 + j)
        part = cell(u, zz, 1 - y, c, x, 1)
        push(u, part, part, 14 + j, dev_x)

    def near_corner(u):
        if u not in late:
            turn(u, 0, z_src[0])
            slab = cell(u, z_src[0], y, c)
            push(u, slab, slab, 19, dev_s)

    def corner(u):
        if u in late:
            for j in range(2):
                turn(u, j, z_mine + j)
        else:
            for j in (1, 2):
                turn(u, j, z_src[j])
                slab = cell(u, z_src[j], y, c)
                push(u, slab, slab, 19 + j, dev_s)

    def corners_in(u, j, zz):
        arrived(u, cell(u, zz, 1 - y, c, 1 - x, 0), 11 + j)
        arrived(u, cell(u, zz, 1 - y, c, 1 - x, 1), 14 + j)

    def finish(u):
        if u in late:
            for j in range(2):
                corners_in(u, j, z_mine + j)
                for yy in range(2):
                    slab = cell(u, z_mine + j, yy, c)
                    push(u, slab, slab, (0, 5, 6, 9)[2 * j + yy], dev_z[0], slot=(2, 5, 6, 9)[2 * j + yy])
                    push(u, slab, slab, 17 + 2 * j + yy, dev_s)
            return
        arrived(u, cell(u, z, 1 - y, c, 1 - x), 6)
        slab = cell(u, z, 1 - y, c)
        push(u, slab, slab, 18, dev_s)
        for j in range(3):
            corners_in(u, j, z_src[j])
            slab = cell(u, z_src[j], 1 - y, c)
            push(u, slab, slab, 22 + j, dev_s)

    def last(u):
        if u in late:
            for j in range(2):
                for yy in range(2):
                    slab = cell(u, z_theirs + j, yy, c)
                    arrived(u, slab, (0, 5, 6, 9)[2 * j + yy])
                    push(u, slab, slab, 21 + 2 * j + yy, dev_s)

    n = len(units)
    order = sorted(range(n), key=lambda u: u not in late)
    events = [(1.0 * i - lags[7], begin, u) for i, u in enumerate(order)]
    events += [(lags[0] + 1.0 * i, spread, u) for i, u in enumerate(order)]
    events += [(lags[1] + 1.0 * i, corner, u) for i, u in enumerate(order)]
    events += [(lags[2] + 1.0 * i, finish, u) for i, u in enumerate(order)]
    events += [(lags[3] + 1.0 * i, last, u) for i, u in enumerate(order)]
    events += [(lags[4] + lags[5] * i, near, u) for i, u in enumerate(order)]
    events += [(lags[6] + 1.0 * i, near_corner, u) for i, u in enumerate(order)]
    for _, act, u in sorted(events, key=lambda e: e[0]):
        act(u)
    for u in range(n):
        if u in late:
            for j in range(2):
                for yy in range(2):
                    arrived(u, cell(u, z_mine + j, yy, 1 - c), 17 + 2 * j + yy)
                    arrived(u, cell(u, z_theirs + j, yy, 1 - c), 21 + 2 * j + yy)

            @pl.when(inner)
            def _():
                near_copy(u).wait_send()

            continue
        arrived(u, cell(u, z, y, 1 - c), 17)
        arrived(u, cell(u, z, 1 - y, 1 - c), 18)
        for j in range(3):
            arrived(u, cell(u, z_src[j], y, 1 - c), 19 + j)
            arrived(u, cell(u, z_src[j], 1 - y, 1 - c), 22 + j)
        pltpu.make_async_copy(own(u, stage), cell(u, z, y, c), local.at[u]).wait()
        for j in (1, 2):

            @pl.when(inner)
            def _():
                relay_copy(u, cell(u, z_src[j], y, c, x), j).wait_send()

    for cp in started:
        cp.wait_send()


def gather_blocks(shards, collective_id):
    units = units_of(shards, 0.5)
    out = [
        jax.ShapeDtypeStruct((s.shape[0] // 2, 16 * s.shape[1], s.shape[2]), s.dtype)
        for s in shards
    ]
    n = len(units)
    return pl.pallas_call(
        functools.partial(gather_kernel, units, LATE, GATHER_LAGS, len(shards)),
        out_shape=out,
        in_specs=[pl.BlockSpec(memory_space=pl.ANY)] * len(shards),
        out_specs=[pl.BlockSpec(memory_space=pl.ANY)] * len(shards),
        scratch_shapes=[
            pltpu.SemaphoreType.DMA((n, 27)),
            pltpu.SemaphoreType.DMA((n, 25)),
            pltpu.SemaphoreType.DMA((n,)),
        ],
        compiler_params=pltpu.CompilerParams(collective_id=collective_id, has_side_effects=True),
        name="gather_blocks",
    )(*shards)


TOKENS = 256
HALF_LANES = 64
FORWARD_VMEM = 58 * 2**20


def lane_of(shape):
    return lax.broadcasted_iota(jnp.int32, shape, len(shape) - 1)


def norm_rows(hidden):
    center = hidden - jnp.mean(hidden, -1, keepdims=True)
    inverse = lax.rsqrt(jnp.mean(center * center, -1, keepdims=True) + EPS_NORM)
    return center * inverse, inverse


def gelu_and_slope(v):
    root = 0.7978845608028654
    square = v * v
    wave = jnp.tanh(root * (v + 0.044715 * (square * v)))
    near = 0.5 * (1.0 + wave)
    slope = near + (0.5 * root) * v * (1.0 - wave * wave) * (1.0 + (3 * 0.044715) * square)
    return v * near, slope


def turned_round(part):
    length = part.shape[0]
    down = lax.broadcasted_iota(jnp.int32, (length, length), 0)
    flip = (down + lane_of((length, length)) == length - 1).astype(jnp.bfloat16)
    total = None
    for _ in range(3):
        high = part.astype(jnp.bfloat16)
        part = part - high.astype(jnp.float32)
        moved = jnp.dot(flip, high, preferred_element_type=jnp.float32)
        total = moved if total is None else total + moved
    return total


def packed_pair(part, length):
    lane = lane_of((length, LANES))
    return jnp.where(lane < HALF_LANES, part[:length], pltpu.roll(part[length:], HALF_LANES, 1))


def unpacked(part, row):
    lane = lane_of(part.shape)
    part = part if row == 0 else pltpu.roll(part, HALF_LANES, 1)
    return jnp.where(lane < HALF_LANES, part, 0.0)


def facts_of(facts, batch, second, row, places):
    at = jnp.where(second, facts[batch, row, 8] - 1 - places, places)
    segment = jnp.zeros(places.shape, jnp.int32)
    for k in range(SEGS):
        segment = segment + (at >= facts[batch, row, k]).astype(jnp.int32)
    label = jnp.zeros(places.shape, jnp.int32)
    for k in range(SEGS):
        label = jnp.where(segment == k, facts[batch, row, SEGS + k], label)
    return segment, label


def columns_of(facts, batch, second, rows, length):
    parts = []
    for row in range(rows):
        places = lax.broadcasted_iota(jnp.int32, (length, LANES), 0)
        segment, label = facts_of(facts, batch, second, row, places)
        before, _ = facts_of(facts, batch, second, row, places - 1)
        parts.append((segment, label, (places >= 1) & (segment == before)))
    return [
        jnp.concatenate([part[i].astype(jnp.int32) for part in parts], 0)[:, :1] for i in range(3)
    ]


def gain_rows_of(w_side, last, out, count):
    return w_side[:, last:].astype(jnp.float32).T[out : out + count]


def both_heads(pair, first):
    zero = jnp.zeros_like(pair)
    return jnp.concatenate([jnp.where(first, pair, zero), jnp.where(first, zero, pair)], 0)


def norm_rows_back(normed, inverse, grad_normed):
    mean_grad = jnp.mean(grad_normed, -1, keepdims=True)
    mean_proj = jnp.mean(grad_normed * normed, -1, keepdims=True)
    return inverse * (grad_normed - mean_grad - normed * mean_proj)


def by_rows(left, right):
    return lax.dot_general(
        left, right, (((1,), (1,)), ((), ())), preferred_element_type=jnp.float32
    )


def down_columns(left, right):
    return lax.dot_general(
        left, right, (((0,), (0,)), ((), ())), preferred_element_type=jnp.float32
    )


def blocks_kernel(
    sizes,
    facts,
    patches,
    cotangent,
    hbm_qkv,
    hbm_o,
    hbm_up,
    hbm_down,
    hbm_side,
    out_latent,
    out_grad,
    out_gains,
    hbm_na,
    hbm_aa,
    hbm_q,
    hbm_p,
    hbm_ctx,
    hbm_nm,
    hbm_am,
    hbm_slope,
    hbm_gelu,
    hbm_stat,
    hbm_nf,
    hbm_af,
    hbm_tail,
    hbm_start,
    hbm_gqkv,
    hbm_gmid,
    hbm_gup,
    hbm_gbr,
    hbm_gstart,
    hbm_gpred,
    w_qkv,
    w_o,
    w_up,
    w_down,
    w_side,
    na,
    aa,
    qkv,
    prob,
    ctx,
    nm,
    am,
    slope,
    gelu,
    stat,
    nf,
    af,
    tail,
    start,
    gqkv,
    gmid,
    gup,
    gbr,
    gstart,
    gpred,
    hidden,
    inputs,
    gain_rows,
    gact,
    gctx,
    sent,
    received,
    w_sem,
    save_sem,
    last_sem,
    load_sem,
    once_sem,
    grad_sem,
    end_sem,
    send_sem,
    recv_sem,
):
    rows, length, table, channels = sizes
    layers, width = w_qkv.shape[0], w_qkv.shape[1]
    pairs = width // LANES
    half = lax.axis_size("rows") // 2
    me = lax.axis_index("rows")
    second = me >= half
    partner = (jnp.where(second, me - half, me + half), lax.axis_index("seq"))
    barrier = pltpu.get_barrier_semaphore()
    pl.semaphore_signal(barrier, 1, device_id=partner, device_id_type=MESH_ID)

    def hop(slot):
        return pltpu.make_async_remote_copy(
            src_ref=sent.at[slot],
            dst_ref=received.at[slot],
            send_sem=send_sem.at[slot],
            recv_sem=recv_sem.at[slot],
            device_id=partner,
            device_id_type=MESH_ID,
        )

    loads = [(hbm_side.at[0], w_side, 0)]
    for layer in range(layers):
        for i, (src, dst) in enumerate(
            ((hbm_qkv, w_qkv), (hbm_o, w_o), (hbm_up, w_up), (hbm_down, w_down))
        ):
            loads.append((src.at[layer], dst.at[layer], 1 + 4 * layer + i))
    for src, dst, i in loads:
        pltpu.make_async_copy(src, dst, w_sem.at[i]).start()
    pl.semaphore_wait(barrier, 1)
    pltpu.make_async_copy(hbm_side.at[0], w_side, w_sem.at[0]).wait()
    gain_rows[...] = gain_rows_of(w_side, table + LANES, 2 * channels, 8)
    lane = lane_of((TOKENS, LANES))

    layered = (
        (na, hbm_na),
        (aa, hbm_aa),
        (qkv, hbm_q),
        (prob, hbm_p),
        (ctx, hbm_ctx),
        (nm, hbm_nm),
        (am, hbm_am),
        (slope, hbm_slope),
        (gelu, hbm_gelu),
        (stat, hbm_stat),
    )
    single = ((nf, hbm_nf), (af, hbm_af), (tail, hbm_tail), (start, hbm_start))

    @pl.loop(0, 3)
    def _(step):
        batch = jnp.where(second, jnp.maximum(step - 1, 0), jnp.minimum(step, 1))

        def saving(layer, i):
            src, dst = layered[i]
            src = src if i == 7 else src.at[layer]
            return pltpu.make_async_copy(src, dst.at[step, layer], save_sem.at[layer, i])

        def ready(layer, i, dst):
            @pl.when(step == 0)
            def _():
                view = dst.at[layer]
                pltpu.make_async_copy(view, view, w_sem.at[1 + 4 * layer + i]).wait()

        for slot in range(2):

            @pl.when(step == slot + 1)
            def _():
                hop(slot).wait_recv()

        for row in range(rows):
            toks = pl.ds(row * length, length)

            @pl.when(jnp.logical_not(second))
            def _():
                inputs[toks, :] = patches[batch, toks, :]

            @pl.when(second & (step > 0))
            def _():
                before = received[jnp.maximum(step - 1, 0)]
                inputs[toks, :] = turned_round(unpacked(before, row))

            @pl.when(second & (step == 0))
            def _():
                inputs[toks, :] = jnp.zeros((length, LANES), jnp.float32)

        seg_col, labels, same = columns_of(facts, batch, second, rows, length)
        start[:, :table] = (labels == lane_of((TOKENS, table))).astype(jnp.bfloat16)
        start[:, table:] = inputs[...].astype(jnp.bfloat16)
        hidden[...] = by_rows(start[...], w_side[:, : table + LANES])
        for layer in range(layers):
            normed, inverse_a = norm_rows(hidden[...])
            na[layer] = normed
            saving(layer, 0).start()
            aa[layer] = (normed * gain_rows[2 * layer : 2 * layer + 1, :]).astype(jnp.bfloat16)
            saving(layer, 1).start()
            ready(layer, 0, w_qkv)

            @pl.loop(0, 3)
            def _(i):
                cols = pl.ds(pl.multiple_of(i * width, LANES), width)
                qkv[layer, :, cols] = jnp.dot(
                    aa[layer], w_qkv[layer, :, cols], preferred_element_type=jnp.float32
                ).astype(jnp.bfloat16)

            saving(layer, 2).start()
            for row in range(rows):
                toks = pl.ds(row * length, length)
                causal = lax.broadcasted_iota(jnp.int32, (length, length), 0) >= lane_of(
                    (length, length)
                )
                places = lax.broadcasted_iota(jnp.int32, (8, length), 1)
                seg_row = facts_of(facts, batch, second, row, places)[0][:1]
                attend = (seg_col[row * length : (row + 1) * length] == seg_row) & causal
                attend = jnp.concatenate([attend.astype(jnp.float32)] * 2, 0) > 0.5
                first = lane_of((length, LANES)) < HALF_LANES
                for pair in range(pairs):

                    def part(i):
                        return qkv[layer, toks, pl.ds(i * width + pair * LANES, LANES)]

                    scores = by_rows(both_heads(part(0), first), part(1)) * HEAD_DIM ** (-0.5)
                    scores = jnp.where(attend, scores, MASKED)
                    expo = jnp.exp(scores - jnp.max(scores, -1, keepdims=True))
                    soft = expo / jnp.sum(expo, -1, keepdims=True)
                    prob[layer, row * pairs + pair] = soft
                    mixed = jnp.dot(
                        soft.astype(jnp.bfloat16), part(2), preferred_element_type=jnp.float32
                    )
                    ctx[layer, toks, pl.ds(pair * LANES, LANES)] = jnp.where(
                        first, mixed[:length], mixed[length:]
                    ).astype(jnp.bfloat16)

            saving(layer, 3).start()
            saving(layer, 4).start()
            ready(layer, 1, w_o)
            hidden[...] = hidden[...] + jnp.dot(
                ctx[layer], w_o[layer], preferred_element_type=jnp.float32
            )
            normed, inverse_m = norm_rows(hidden[...])
            nm[layer] = normed
            saving(layer, 5).start()
            am[layer] = (normed * gain_rows[2 * layer + 1 : 2 * layer + 2, :]).astype(jnp.bfloat16)
            saving(layer, 6).start()
            stat[layer] = jnp.where(lane == 0, inverse_a, inverse_m)
            saving(layer, 9).start()
            ready(layer, 2, w_up)
            if layer > 0:
                saving(layer - 1, 7).wait()

            @pl.loop(0, w_up.shape[2] // width)
            def _(i):
                cols = pl.ds(pl.multiple_of(i * width, LANES), width)
                upper = jnp.dot(am[layer], w_up[layer, :, cols], preferred_element_type=jnp.float32)
                value, rate = gelu_and_slope(upper)
                gelu[layer, :, cols] = value.astype(jnp.bfloat16)
                slope[:, cols] = rate

            saving(layer, 7).start()
            saving(layer, 8).start()
            ready(layer, 3, w_down)
            hidden[...] = hidden[...] + jnp.dot(
                gelu[layer], w_down[layer], preferred_element_type=jnp.float32
            )

        normed, inverse_f = norm_rows(hidden[...])
        nf[...] = normed
        af[...] = (normed * gain_rows[2 * layers : 2 * layers + 1, :]).astype(jnp.bfloat16)
        prediction = jnp.dot(
            af[...], w_side[:, table + LANES :], preferred_element_type=jnp.float32
        )
        previous = pltpu.roll(prediction, 1, 0)
        shown = (same > 0) & (lane < channels)
        shift_alpha = jnp.where(shown, pltpu.roll(previous, LANES - channels, 1), 0.0)
        shift_mu = jnp.where(shown, previous, 0.0)
        latent = (inputs[...] - shift_mu) * jnp.exp(-shift_alpha)
        logdet = -jnp.sum(shift_alpha, -1, keepdims=True)
        result = jnp.where(lane == channels, logdet + inputs[...], latent)
        out_latent[step] = result
        for slot in range(2):

            @pl.when(step == slot)
            def _():
                sent[slot] = packed_pair(result, length)
                hop(slot).start()

        tail[0] = latent
        tail[1] = shift_alpha
        tail[2] = jnp.broadcast_to(inverse_f, (TOKENS, LANES))
        for i, (src, dst) in enumerate(single):
            pltpu.make_async_copy(src, dst.at[step], last_sem.at[i]).start()
        for layer in range(layers):
            for i in range(len(layered)):
                if i != 7 or layer == layers - 1:
                    saving(layer, i).wait()
        for i, (src, dst) in enumerate(single):
            pltpu.make_async_copy(src, dst.at[step], last_sem.at[i]).wait()

    back = ((nm, hbm_nm), (prob, hbm_p), (qkv, hbm_q), (na, hbm_na), (stat, hbm_stat))
    once = ((tail, hbm_tail), (nf, hbm_nf))
    order = list(reversed(range(layers)))

    @pl.loop(0, 3)
    def _(turn):
        batch = jnp.where(second, jnp.maximum(1 - turn, 0), jnp.minimum(2 - turn, 1))
        slot_of = 2 - turn

        def fetch(layer, i, step):
            src, dst = back[i][1], back[i][0]
            return pltpu.make_async_copy(src.at[step, layer], dst.at[layer], load_sem.at[layer, i])

        def fetch_slope(layer, step):
            return pltpu.make_async_copy(hbm_slope.at[step, layer], slope, load_sem.at[layer, 5])

        def fetch_once(i, step):
            return pltpu.make_async_copy(once[i][1].at[step], once[i][0], once_sem.at[i])

        def refill(copy_of):
            @pl.when(turn < 2)
            def _():
                copy_of(jnp.maximum(slot_of - 1, 0)).start()

        def await_load(copy_of):
            @pl.when(turn > 0)
            def _():
                copy_of(slot_of).wait()

        def saving(layer, i):
            src, dst = ((gqkv, hbm_gqkv), (gmid, hbm_gmid), (gup, hbm_gup), (gbr, hbm_gbr))[i]
            src = src if i == 2 else src.at[layer]
            return pltpu.make_async_copy(src, dst.at[slot_of, layer], grad_sem.at[layer, i])

        for slot in (2, 3):

            @pl.when(turn == slot - 1)
            def _():
                hop(slot).wait_recv()

        for row in range(rows):
            toks = pl.ds(row * length, length)

            @pl.when(second)
            def _():
                inputs[toks, :] = cotangent[batch, toks, :]

            @pl.when(jnp.logical_not(second) & (turn > 0))
            def _():
                before = received[jnp.maximum(turn, 1) + 1]
                inputs[toks, :] = turned_round(unpacked(before, row))

            @pl.when(jnp.logical_not(second) & (turn == 0))
            def _():
                inputs[toks, :] = jnp.zeros((length, LANES), jnp.float32)

        same = columns_of(facts, batch, second, rows, length)[2]
        await_load(functools.partial(fetch_once, 0))
        await_load(functools.partial(fetch_once, 1))
        scaled = inputs[...] * jnp.exp(-tail[1])
        grad_alpha = 1.0 - inputs[...] * tail[0]
        grad_prev = jnp.where(lane < channels, -scaled, pltpu.roll(grad_alpha, channels, 1))
        grad_prev = jnp.where((same > 0) & (lane < 2 * channels), grad_prev, 0.0)
        gpred[...] = pltpu.roll(grad_prev, TOKENS - 1, 0).astype(jnp.bfloat16)
        gact[...] = by_rows(gpred[...], w_side[:, table + LANES :])
        out_gains[turn] = jnp.zeros((8, width), jnp.float32)

        def through_norm(normed, inverse, index):
            grad = gact[...]
            out_gains[turn, index : index + 1, :] = jnp.sum(grad * normed, 0, keepdims=True)
            return norm_rows_back(normed, inverse, grad * gain_rows[index : index + 1, :])

        hidden[...] = through_norm(nf[...], tail[2][:, :1], 2 * layers)
        refill(functools.partial(fetch_once, 0))
        refill(functools.partial(fetch_once, 1))
        for layer in order:
            gbr[layer] = hidden[...].astype(jnp.bfloat16)
            saving(layer, 3).start()
            if layer == order[0]:
                await_load(functools.partial(fetch_slope, layer))
            else:
                fetch_slope(layer, slot_of).wait()
                saving(layer + 1, 2).wait()

            @pl.loop(0, w_up.shape[2] // width)
            def _(i):
                cols = pl.ds(pl.multiple_of(i * width, LANES), width)
                gup[:, cols] = (
                    by_rows(gbr[layer], w_down[layer, cols, :]) * slope[:, cols]
                ).astype(jnp.bfloat16)

            saving(layer, 2).start()
            if layer > 0:
                fetch_slope(layer - 1, slot_of).start()
            else:
                refill(functools.partial(fetch_slope, order[0]))
            gact[...] = by_rows(gup[...], w_up[layer])
            await_load(functools.partial(fetch, layer, 0))
            await_load(functools.partial(fetch, layer, 4))
            hidden[...] = hidden[...] + through_norm(
                nm[layer], stat[layer][:, 1:2], 2 * layer + 1
            )
            refill(functools.partial(fetch, layer, 0))
            gmid[layer] = hidden[...].astype(jnp.bfloat16)
            saving(layer, 1).start()
            gctx[...] = by_rows(gmid[layer], w_o[layer]).astype(jnp.bfloat16)
            await_load(functools.partial(fetch, layer, 1))
            await_load(functools.partial(fetch, layer, 2))
            for row in range(rows):
                toks = pl.ds(row * length, length)
                first = lane_of((length, LANES)) < HALF_LANES
                for pair in range(pairs):

                    def at(i):
                        return pl.ds(i * width + pair * LANES, LANES)

                    query = both_heads(qkv[layer, toks, at(0)], first)
                    key = qkv[layer, toks, at(1)]
                    value = qkv[layer, toks, at(2)]
                    grad = both_heads(gctx[toks, at(0)], first)
                    soft = prob[layer, row * pairs + pair]
                    grad_soft = by_rows(grad, value)
                    delta = jnp.sum(soft * grad_soft, -1, keepdims=True)
                    grad_scores = (soft * (grad_soft - delta)).astype(jnp.bfloat16)
                    factor = HEAD_DIM ** (-0.5)
                    mixed = jnp.dot(grad_scores, key, preferred_element_type=jnp.float32) * factor
                    gqkv[layer, toks, at(0)] = jnp.where(
                        first, mixed[:length], mixed[length:]
                    ).astype(jnp.bfloat16)
                    gqkv[layer, toks, at(1)] = (
                        down_columns(grad_scores, query) * factor
                    ).astype(jnp.bfloat16)
                    gqkv[layer, toks, at(2)] = down_columns(
                        soft.astype(jnp.bfloat16), grad
                    ).astype(jnp.bfloat16)

            refill(functools.partial(fetch, layer, 1))
            refill(functools.partial(fetch, layer, 2))
            saving(layer, 0).start()
            gact[...] = by_rows(gqkv[layer], w_qkv[layer])
            await_load(functools.partial(fetch, layer, 3))
            hidden[...] = hidden[...] + through_norm(na[layer], stat[layer][:, :1], 2 * layer)
            refill(functools.partial(fetch, layer, 3))
            refill(functools.partial(fetch, layer, 4))
        gstart[...] = hidden[...].astype(jnp.bfloat16)
        grad_inputs = scaled + jnp.dot(
            gstart[...], w_side[:, table : table + LANES], preferred_element_type=jnp.float32
        )
        grad_inputs = jnp.where(lane < channels, grad_inputs, 0.0)
        out_grad[turn] = grad_inputs
        for slot in (2, 3):

            @pl.when(turn == slot - 2)
            def _():
                sent[slot] = packed_pair(grad_inputs, length)
                hop(slot).start()

        ends = ((gstart, hbm_gstart), (gpred, hbm_gpred))
        for i, (src, dst) in enumerate(ends):
            pltpu.make_async_copy(src, dst.at[slot_of], end_sem.at[i]).start()
        for layer in range(layers):
            for i in range(4):
                if i != 2 or layer == 0:
                    saving(layer, i).wait()
        for i, (src, dst) in enumerate(ends):
            pltpu.make_async_copy(src, dst.at[slot_of], end_sem.at[i]).wait()

    for slot in range(4):
        hop(slot).wait_send()


def two_blocks(facts, patches, cotangent, weights, table, channels, collective_id):
    w_qkv, w_o, w_up, w_down, side = weights
    rows = facts.shape[1]
    length = TOKENS // rows
    layers, width, hidden = w_up.shape
    pairs = rows * width // LANES
    low, full = jnp.bfloat16, jnp.float32
    kept = [
        ((layers, TOKENS, width), full),
        ((layers, TOKENS, width), low),
        ((layers, TOKENS, 3 * width), low),
        ((layers, pairs, 2 * length, length), full),
        ((layers, TOKENS, width), low),
        ((layers, TOKENS, width), full),
        ((layers, TOKENS, width), low),
        ((layers, TOKENS, hidden), full),
        ((layers, TOKENS, hidden), low),
        ((layers, TOKENS, LANES), full),
        ((TOKENS, width), full),
        ((TOKENS, width), low),
        ((3, TOKENS, LANES), full),
        ((TOKENS, table + LANES), low),
        ((layers, TOKENS, 3 * width), low),
        ((layers, TOKENS, width), low),
        ((layers, TOKENS, hidden), low),
        ((layers, TOKENS, width), low),
        ((TOKENS, width), low),
        ((TOKENS, LANES), low),
    ]
    scratch = [pltpu.VMEM(w.shape, low) for w in weights[:4]] + [pltpu.VMEM(side.shape[1:], low)]
    for i, (shape, kind) in enumerate(kept):
        scratch.append(pltpu.VMEM(shape[1:] if i in (7, 16) else shape, kind))
    dma = pltpu.SemaphoreType.DMA
    scratch += [
        pltpu.VMEM((TOKENS, width), full),
        pltpu.VMEM((TOKENS, LANES), full),
        pltpu.VMEM((8, width), full),
        pltpu.VMEM((TOKENS, width), full),
        pltpu.VMEM((TOKENS, width), low),
        pltpu.VMEM((4, length, LANES), full),
        pltpu.VMEM((4, length, LANES), full),
        dma((1 + 4 * layers,)),
        dma((layers, 10)),
        dma((4,)),
        dma((layers, 6)),
        dma((2,)),
        dma((layers, 4)),
        dma((2,)),
        dma((4,)),
        dma((4,)),
    ]
    vmem, hbm = pl.BlockSpec(memory_space=pltpu.VMEM), pl.BlockSpec(memory_space=pl.ANY)
    smem = pl.BlockSpec(memory_space=pltpu.SMEM)
    results = pl.pallas_call(
        functools.partial(blocks_kernel, (rows, length, table, channels)),
        out_shape=[jax.ShapeDtypeStruct((3, TOKENS, LANES), full)] * 2
        + [jax.ShapeDtypeStruct((3, 8, width), full)]
        + [jax.ShapeDtypeStruct((3,) + shape, kind) for shape, kind in kept],
        in_specs=[smem] + [vmem] * 2 + [hbm] * 5,
        out_specs=[vmem] * 3 + [hbm] * len(kept),
        scratch_shapes=scratch,
        compiler_params=pltpu.CompilerParams(
            collective_id=collective_id, has_side_effects=True, vmem_limit_bytes=61 * 2**20
        ),
        name="two_blocks",
    )(facts, patches, cotangent, w_qkv, w_o, w_up, w_down, side)
    _, aa, _, _, ctx, _, am, _, gelu, _, _, af, _, start = results[3:17]
    gqkv, gmid, gup, gbr, gstart, gpred = results[17:]
    pairs = (aa, gqkv, ctx, gmid, am, gup, gelu, gbr, start, gstart, af, gpred)
    return results[:3], pairs


def products_kernel(units, n_pairs, out_count, *refs):
    per = 2 * n_pairs
    steps, gain_grads = refs[:per], refs[per]
    outs = refs[per + 1 : per + 6]
    rest = refs[per + 6 :]
    bufs, made, turned = rest[:per], rest[per : per + 5], rest[per + 5]
    rest = rest[per + 6 :]
    n = len(units)
    acc, in_x, in_y, in_d, in_z = [rest[i * n : (i + 1) * n] for i in range(5)]
    gain_cols, in_sem, send, recv, local_out = rest[5 * n :]
    r, x, y, z, c = place()
    stage = z // 2
    other = 1 - stage
    zi = lax.rem(z, 2)
    dev_x = (r, 1 - x)
    dev_y = (r + 2 - 4 * y, x)
    dev_s = (r + 1 - 2 * c, x)
    z_dst = (z + 1 - 2 * zi, other * 2, other * 2 + 1)
    dev_z = tuple((zz * 4 + y * 2 + c, x) for zz in z_dst)
    barrier = pltpu.get_barrier_semaphore()
    partners = (dev_x, dev_y, dev_s) + dev_z
    for dev in partners:
        pl.semaphore_signal(barrier, 1, device_id=dev, device_id_type=MESH_ID)

    def loads(i, layer):
        copies = []
        for k, step in enumerate((1, 2 * stage)):
            src = steps[i].at[step, layer] if len(steps[i].shape) == 4 else steps[i].at[step]
            dst = bufs[i].at[pl.ds(k * TOKENS, TOKENS)]
            copies.append(pltpu.make_async_copy(src, dst, in_sem.at[layer, 2 * i + k]))
        return copies

    def fetch(i, layer):
        for copy in loads(i, layer):
            copy.start()

    def fetched(i, layer):
        for copy in loads(i, layer):
            copy.wait()

    for i in (8, 9, 10, 11):
        fetch(i, 0)
    for i in range(8):
        fetch(i, 0)
    pl.semaphore_wait(barrier, len(partners))
    started = {}

    def push(u, src, dst, slot, dev, idx=None):
        cp = pltpu.make_async_remote_copy(
            src_ref=src,
            dst_ref=dst,
            send_sem=send.at[u, slot],
            recv_sem=recv.at[u, slot if idx is None else idx],
            device_id=dev,
            device_id_type=MESH_ID,
        )
        cp.start()
        started[u, slot] = cp

    def arrived(u, dst, idx):
        wait_all_of(dst, recv.at[u, idx])

    def part_of(u, part):
        _, _, _, rows, half, (dim, cut) = units[u]
        if dim == 0:
            return (pl.ds(0, cut), pl.ds(0, half)) if part == 0 else (pl.ds(cut, rows - cut), pl.ds(0, half))
        return (pl.ds(0, rows), pl.ds(0, cut)) if part == 0 else (pl.ds(0, rows), pl.ds(cut, half - cut))

    block, strip = turned.shape[0], 3 * LANES

    def multiply(out, rows, right, m, begin, count, wide, extra=None):
        def one(cols, out_cols):
            product = jnp.dot(turned[...], right[:, cols], preferred_element_type=jnp.float32)
            if extra is not None:
                product = product + extra[...]
            product = product.astype(jnp.bfloat16)
            for k in range(block // rows):
                s = m * (block // rows) + k
                out[s // 4, (s // 2) % 2, s % 2, :, out_cols] = product[k * rows : (k + 1) * rows]

        if count == 1:
            one(slice(0, wide), slice(begin, begin + wide))
        else:

            @pl.loop(0, count)
            def _(i):
                cols = pl.ds(pl.multiple_of(i * wide, LANES), wide)
                one(cols, cols)

    def product(u):
        a, layer, _, rows, half, _ = units[u]
        if a == 4:
            for i in (8, 9, 10, 11):
                fetched(i, 0)
            turned[...] = bufs[9][...].T
            multiply(made[4], rows, bufs[8], 0, 0, bufs[8].shape[1] // strip, strip)
            turned[...] = bufs[10][...].T
            gains = gain_grads[1] + gain_grads[2 - 2 * stage]
            zeros = jnp.zeros((LANES, gains.shape[1]), jnp.float32)
            tall = jnp.concatenate([zeros[:out_count], gains, zeros[out_count + 8 :]], 0)
            gain_cols[...] = tall.T
            multiply(made[4], rows, bufs[11], 0, bufs[8].shape[1], 1, LANES, gain_cols)
        else:
            fetched(2 * a, layer)
            fetched(2 * a + 1, layer)
            if layer > 0:
                for h in range(2):
                    started.pop((u - 4, h)).wait_send()
            for m in range(bufs[2 * a].shape[1] // block):
                turned[...] = bufs[2 * a][:, m * block : (m + 1) * block].T
                multiply(made[a], rows, bufs[2 * a + 1], m, 0, 2 * half // strip, strip)
            if layer + 1 < units[-1][1] + 1:
                fetch(2 * a, layer + 1)
                fetch(2 * a + 1, layer + 1)
        for h in range(2):
            cols = pl.ds(h * half, half)
            push(u, made[a].at[:, :, 1 - c, :, cols], acc[u].at[:, :, h], h, dev_s)

    def chip_sum(u):
        a, layer, _, rows, half, _ = units[u]
        for h in range(2):
            arrived(u, acc[u].at[:, :, h], h)

        @pl.loop(0, 4)
        def _(zz):
            for yy in range(2):
                for h in range(2):
                    mine = made[a][zz, yy, c, :, h * half : (h + 1) * half]
                    acc[u][zz, yy, h] = acc[u][zz, yy, h] + mine

        for part, dev in ((0, dev_y), (1, dev_x)):
            rs, cs = part_of(u, part)
            push(u, acc[u].at[:, 1 - y, 1 - x, rs, cs], in_d[u].at[:, rs, cs], 2 + part, dev)

    def side_sum(u):
        for part, yy, h, dev, into in ((0, y, 1 - x, dev_x, in_x), (1, 1 - y, x, dev_y, in_y)):
            rs, cs = part_of(u, part)
            arrived(u, in_d[u].at[:, rs, cs], 2 + part)

            @pl.loop(0, 4)
            def _(zz):
                acc[u][zz, yy, h, rs, cs] = acc[u][zz, yy, h, rs, cs] + in_d[u][zz, rs, cs]

            push(u, acc[u].at[:, yy, h], into[u], 4 + part, dev)

    def plane_sum(u):
        arrived(u, in_x[u], 4)
        arrived(u, in_y[u], 5)

        @pl.loop(0, 4)
        def _(zz):
            acc[u][zz, y, x] = (
                acc[u][zz, y, x].astype(jnp.float32)
                + in_x[u][zz].astype(jnp.float32)
                + in_y[u][zz].astype(jnp.float32)
            ).astype(jnp.bfloat16)

        for i in range(2):
            push(u, acc[u].at[z_dst[1 + i], y, x], in_z[u].at[1 + zi], 7 + i, dev_z[1 + i], idx=7 + zi)
        push(u, acc[u].at[z_dst[0], y, x], in_z[u].at[0], 6, dev_z[0])

    def owned(u, b, h):
        a, layer, layers, _, half, _ = units[u]
        return outs[a].at[layers * b + layer, :, pl.ds(pl.multiple_of(h * half, LANES), half)]

    def totals(u):
        return ((acc[u].at[z, y, x], stage), (in_z[u].at[1], other))

    def total(u):
        for j in range(3):
            arrived(u, in_z[u].at[j], 6 + j)
        acc[u][z, y, x] = acc[u][z, y, x] + in_z[u][0]
        in_z[u][1] = in_z[u][1] + in_z[u][2]
        for k, (src, b) in enumerate(totals(u)):
            push(u, src, owned(u, b, x), 9 + k, dev_x)
            pltpu.make_async_copy(src, owned(u, b, x), local_out.at[u, k]).start()

    lags = (0, 1, 3, 5, 7)
    for t in range(n + lags[-1]):
        for lag, part in zip(lags, (product, chip_sum, side_sum, plane_sum, total)):
            if 0 <= t - lag < n:
                part(t - lag)
    for u in range(n):
        for k, (src, b) in enumerate(totals(u)):
            arrived(u, owned(u, b, 1 - x), 9 + k)
            pltpu.make_async_copy(src, owned(u, b, x), local_out.at[u, k]).wait()
    for cp in started.values():
        cp.wait_send()


def summed_products(operands, gain_grads, out_count, shards, collective_id):
    low = jnp.bfloat16
    out = [jax.ShapeDtypeStruct(s.shape, low) for s in shards]
    units = units_of(out, 0.75)
    n = len(units)
    layers = max(u[1] for u in units) + 1
    n_pairs = len(operands) // 2
    width = operands[0].shape[-1]
    hbm, vmem = pl.BlockSpec(memory_space=pl.ANY), pl.BlockSpec(memory_space=pltpu.VMEM)

    def slots(lead):
        return [pltpu.VMEM(lead + (u[3], u[4]), low) for u in units]

    return pl.pallas_call(
        functools.partial(products_kernel, units, n_pairs, out_count),
        out_shape=out,
        in_specs=[hbm] * (2 * n_pairs) + [vmem],
        out_specs=[hbm] * 5,
        scratch_shapes=[
            pltpu.VMEM((2 * TOKENS, part.shape[-1]), low) for part in operands
        ]
        + [pltpu.VMEM((4, 2, 2) + s.shape[1:], low) for s in shards]
        + [pltpu.VMEM((width, 2 * TOKENS), low)]
        + slots((4, 2, 2))
        + slots((4,))
        + slots((4,))
        + slots((4,))
        + slots((3,))
        + [
            pltpu.VMEM((width, LANES), jnp.float32),
            pltpu.SemaphoreType.DMA((layers, 4 * n_pairs)),
            pltpu.SemaphoreType.DMA((n, 11)),
            pltpu.SemaphoreType.DMA((n, 11)),
            pltpu.SemaphoreType.DMA((n, 2)),
        ],
        compiler_params=pltpu.CompilerParams(
            collective_id=collective_id, has_side_effects=True, vmem_limit_bytes=62 * 2**20
        ),
        name="summed_products",
    )(*operands, gain_grads)


def dot(left, right, dims=((1,), (0,))):
    return lax.dot_general(left, right, (dims, ((), ())), preferred_element_type=jnp.float32)


def normalize(hidden):
    center = hidden - jnp.mean(hidden, -1, keepdims=True)
    inverse = lax.rsqrt(jnp.mean(center * center, -1, keepdims=True) + EPS_NORM)
    return (center * inverse, inverse)


def normalize_back(normed, inverse, grad_normed):
    mean_grad = jnp.mean(grad_normed, -1, keepdims=True)
    mean_proj = jnp.mean(grad_normed * normed, -1, keepdims=True)
    return inverse * (grad_normed - mean_grad - normed * mean_proj)


def padded(count, unit):
    return -(-count // unit) * unit


def side_columns(classes, channels, out, gains):
    table = padded(classes, LANES)
    last = table + padded(channels, LANES)
    return table, last, padded(last + out + gains, 2 * LANES)


def pack_side(w_table, w_in, w_out, gains):
    blocks, classes, shard = w_table.shape
    channels, out, gain_count = w_in.shape[1], w_out.shape[2], gains.shape[1]
    table, last, total = side_columns(classes, channels, out, gain_count)

    def gap(count):
        return jnp.zeros((blocks, shard, count), w_table.dtype)

    return jnp.concatenate(
        [
            jnp.swapaxes(w_table, 1, 2),
            gap(table - classes),
            jnp.swapaxes(w_in, 1, 2),
            gap(last - table - channels),
            w_out,
            jnp.swapaxes(gains, 1, 2),
            gap(total - last - out - gain_count),
        ],
        2,
    )


def split_side(side, classes, channels, out, gains):
    table, last, _ = side_columns(classes, channels, out, gains)
    return (
        jnp.swapaxes(side[..., :classes], -1, -2),
        jnp.swapaxes(side[..., table : table + channels], -1, -2),
        side[..., last : last + out],
        jnp.swapaxes(side[..., last + out : last + out + gains], -1, -2),
    )


def heads_of(flat, rows):
    return flat.reshape(rows, -1, HEADS, HEAD_DIM)


def attention_scores(query, key_rows, attend):
    scores = jnp.einsum(
        "rqhd,rkhd->rhqk", query, key_rows, preferred_element_type=jnp.float32
    ) * HEAD_DIM ** (-0.5)
    return jnp.where(attend[:, None], scores, MASKED)


def forward_block(inputs, seg_ids, labels, weights, sizes):
    w_qkv, w_o, w_up, w_down, side = weights
    classes, channels, out, gain_count = sizes
    table, last, _ = side_columns(*sizes)
    rows, length, _ = inputs.shape
    tokens = rows * length
    width = side.shape[0]
    places = jnp.arange(length, dtype=jnp.int32)
    attend = (seg_ids[:, :, None] == seg_ids[:, None, :]) & (
        places[None, :, None] >= places[None, None, :]
    )
    same_seg = jnp.concatenate(
        [jnp.zeros((rows, 1), bool), seg_ids[:, 1:] == seg_ids[:, :-1]], 1
    )[..., None]
    onehot = labels.reshape(tokens, 1) == jnp.arange(table)[None, :]
    start = jnp.concatenate(
        [
            onehot.astype(jnp.bfloat16),
            inputs.reshape(tokens, channels).astype(jnp.bfloat16),
            jnp.zeros((tokens, last - table - channels), jnp.bfloat16),
        ],
        1,
    )
    gain_rows = side[:, last + out : last + out + gain_count].astype(jnp.float32).T
    hidden = dot(start, side[:, :last], ((1,), (1,)))
    kept = []
    for layer in range(w_qkv.shape[0]):
        normed_a, inverse_a = normalize(hidden)
        act_a = (normed_a * gain_rows[2 * layer]).astype(jnp.bfloat16)
        qkv = dot(act_a, w_qkv[layer]).astype(jnp.bfloat16)
        query, key_rows, value_rows = [
            heads_of(qkv[:, i * width : (i + 1) * width], rows) for i in range(3)
        ]
        scores = attention_scores(query, key_rows, attend)
        row_top = jnp.max(scores, -1, keepdims=True)
        expo_rows = jnp.exp(scores - row_top)
        row_total = jnp.sum(expo_rows, -1, keepdims=True)
        soft_low = (expo_rows / row_total).astype(jnp.bfloat16)
        log_total = row_top + jnp.log(row_total)
        context = jnp.einsum(
            "rhqk,rkhd->rqhd", soft_low, value_rows, preferred_element_type=jnp.float32
        )
        context = context.reshape(tokens, width).astype(jnp.bfloat16)
        middle = hidden + dot(context, w_o[layer])
        normed_m, inverse_m = normalize(middle)
        act_m = (normed_m * gain_rows[2 * layer + 1]).astype(jnp.bfloat16)
        upper = dot(act_m, w_up[layer])
        gelu_low = jax.nn.gelu(upper, approximate=True).astype(jnp.bfloat16)
        hidden = middle + dot(gelu_low, w_down[layer])
        kept.append(
            (
                normed_a,
                inverse_a,
                act_a,
                qkv,
                log_total,
                context,
                normed_m,
                inverse_m,
                act_m,
                upper,
                gelu_low,
            )
        )
    normed_f, inverse_f = normalize(hidden)
    act_f = (normed_f * gain_rows[gain_count - 1]).astype(jnp.bfloat16)
    prediction = dot(act_f, side[:, last : last + out]).reshape(rows, length, out)
    previous = jnp.concatenate([jnp.zeros((rows, 1, out), jnp.float32), prediction[:, :-1]], 1)
    shift = jnp.where(same_seg, previous, 0.0)
    shift_alpha = shift[..., channels:]
    latent = (inputs - shift[..., :channels]) * jnp.exp(-shift_alpha)
    saved = (attend, same_seg, start, kept, normed_f, inverse_f, act_f, shift_alpha, latent)
    return (latent, -jnp.sum(shift_alpha, -1), saved)


def backward_block(grad_latent, saved, weights, sizes):
    w_qkv, w_o, w_up, w_down, side = weights
    classes, channels, out, gain_count = sizes
    table, last, _ = side_columns(*sizes)
    attend, same_seg, start, kept, normed_f, inverse_f, act_f, shift_alpha, latent = saved
    rows, length, _ = latent.shape
    tokens = rows * length
    width = side.shape[0]
    factor = HEAD_DIM ** (-0.5)
    gain_rows = side[:, last + out : last + out + gain_count].astype(jnp.float32).T
    scale_back = jnp.exp(-shift_alpha)
    grad_inputs = grad_latent * scale_back
    grad_prev = jnp.where(
        same_seg, jnp.concatenate([-grad_inputs, 1.0 - grad_latent * latent], 2), 0.0
    )
    grad_pred = jnp.concatenate([grad_prev[:, 1:], jnp.zeros((rows, 1, out), jnp.float32)], 1)
    grad_pred = grad_pred.reshape(tokens, out).astype(jnp.bfloat16)
    grad_act = dot(grad_pred, side[:, last : last + out], ((1,), (1,)))
    gain_grads = [None] * gain_count
    gain_grads[-1] = jnp.sum(grad_act * normed_f, 0)
    grad_hidden = normalize_back(normed_f, inverse_f, grad_act * gain_rows[gain_count - 1])
    pairs = [None] * w_qkv.shape[0]
    for layer in reversed(range(w_qkv.shape[0])):
        (
            normed_a,
            inverse_a,
            act_a,
            qkv,
            log_total,
            context,
            normed_m,
            inverse_m,
            act_m,
            upper,
            gelu_low,
        ) = kept[layer]
        grad_branch = grad_hidden.astype(jnp.bfloat16)
        grad_gelu = dot(grad_branch, w_down[layer], ((1,), (1,)))
        gelu_pull = jax.vjp(partial(jax.nn.gelu, approximate=True), upper)[1]
        grad_upper = gelu_pull(grad_gelu)[0].astype(jnp.bfloat16)
        grad_act_m = dot(grad_upper, w_up[layer], ((1,), (1,)))
        gain_grads[2 * layer + 1] = jnp.sum(grad_act_m * normed_m, 0)
        grad_middle = grad_hidden + normalize_back(
            normed_m, inverse_m, grad_act_m * gain_rows[2 * layer + 1]
        )
        grad_mid_low = grad_middle.astype(jnp.bfloat16)
        grad_context = heads_of(
            dot(grad_mid_low, w_o[layer], ((1,), (1,))).astype(jnp.bfloat16), rows
        )
        query, key_rows, value_rows = [
            heads_of(qkv[:, i * width : (i + 1) * width], rows) for i in range(3)
        ]
        soft_rows = jnp.exp(attention_scores(query, key_rows, attend) - log_total)
        soft_low = soft_rows.astype(jnp.bfloat16)
        grad_soft = jnp.einsum(
            "rqhd,rkhd->rhqk", grad_context, value_rows, preferred_element_type=jnp.float32
        )
        row_delta = jnp.sum(soft_rows * grad_soft, -1, keepdims=True)
        grad_scores = (soft_rows * (grad_soft - row_delta)).astype(jnp.bfloat16)
        grad_query = factor * jnp.einsum(
            "rhqk,rkhd->rqhd", grad_scores, key_rows, preferred_element_type=jnp.float32
        )
        grad_keys = factor * jnp.einsum(
            "rhqk,rqhd->rkhd", grad_scores, query, preferred_element_type=jnp.float32
        )
        grad_values = jnp.einsum(
            "rhqk,rqhd->rkhd", soft_low, grad_context, preferred_element_type=jnp.float32
        )
        grad_qkv = jnp.concatenate(
            [part.reshape(tokens, width) for part in (grad_query, grad_keys, grad_values)], 1
        ).astype(jnp.bfloat16)
        grad_act_a = dot(grad_qkv, w_qkv[layer], ((1,), (1,)))
        gain_grads[2 * layer] = jnp.sum(grad_act_a * normed_a, 0)
        grad_hidden = grad_middle + normalize_back(
            normed_a, inverse_a, grad_act_a * gain_rows[2 * layer]
        )
        pairs[layer] = (
            (act_a, grad_qkv),
            (context, grad_mid_low),
            (act_m, grad_upper),
            (gelu_low, grad_branch),
        )
    grad_start = grad_hidden.astype(jnp.bfloat16)
    grad_inputs = grad_inputs + dot(grad_start, side[:, table : table + channels]).reshape(
        rows, length, channels
    )
    return grad_inputs, (
        pairs,
        (start, grad_start),
        (act_f, grad_pred),
        jnp.stack(gain_grads, 1),
    )


def weight_grads(parts, side_total):
    pairs, (start, grad_start), (act_f, grad_pred), gain_grads = parts
    arrays = [
        jnp.stack([dot(*layer[i], ((0,), (0,))).astype(jnp.bfloat16) for layer in pairs], 0)
        for i in range(4)
    ]
    side = [
        dot(grad_start, start, ((0,), (0,))),
        dot(act_f, grad_pred, ((0,), (0,))),
        gain_grads,
    ]
    count = sum(part.shape[1] for part in side)
    side.append(jnp.zeros((gain_grads.shape[0], side_total - count), jnp.float32))
    side = jnp.concatenate(side, 1).astype(jnp.bfloat16)
    return arrays + [side[None]]


def adam_step(weight, first, second, grad, rate):
    first_new = BETA_ONE * first + (1.0 - BETA_ONE) * grad
    second_new = BETA_TWO * second + (1.0 - BETA_TWO) * grad * grad
    first_hat = first_new / (1.0 - BETA_ONE**STEP)
    second_hat = second_new / (1.0 - BETA_TWO**STEP)
    weight_new = weight - rate * (first_hat / (jnp.sqrt(second_hat) + EPS_ADAM) + DECAY * weight)
    return (first_new, second_new, weight_new)


def segment_of(places, seg_ends):
    return jnp.sum((places[None, :, None] >= seg_ends[:, None, :]).astype(jnp.int32), -1)


def row_facts(seg_lengths, class_labels, length):
    seg_ids = segment_of(jnp.arange(length, dtype=jnp.int32), jnp.cumsum(seg_lengths, 1))
    picked = seg_ids[:, :, None] == jnp.arange(SEGS)[None, None, :]
    return seg_ids, jnp.sum(jnp.where(picked, class_labels[:, None, :], 0), -1)


def pack_kernel(sizes, w_table, w_in, w_out, gains, side):
    classes, channels, out, gain_count = sizes
    table, last, _ = side_columns(*sizes)
    shard = w_out.shape[1]
    down = lax.broadcasted_iota(jnp.int32, (shard, shard), 0)
    same = (down == lane_of((shard, shard))).astype(jnp.bfloat16)
    side[...] = jnp.zeros_like(side)
    for b in range(2):

        def across(part):
            return by_rows(same, part.astype(jnp.bfloat16)).astype(jnp.bfloat16)

        side[b, :, :classes] = w_table[b].astype(jnp.bfloat16)
        side[b, :, table : table + channels] = across(w_in[b])
        side[b, :, last : last + out] = w_out[b].astype(jnp.bfloat16)
        side[b, :, last + out : last + out + gain_count] = across(gains[:, b])


def packed_side(w_table, w_in, w_out, gains, sizes):
    shape = (2, w_out.shape[1], side_columns(*sizes)[2])
    return pl.pallas_call(
        functools.partial(pack_kernel, sizes),
        out_shape=jax.ShapeDtypeStruct(shape, jnp.bfloat16),
        compiler_params=pltpu.CompilerParams(vmem_limit_bytes=32 * 2**20),
        name="pack_side",
    )(jnp.swapaxes(w_table, 1, 2), w_in, w_out, jnp.swapaxes(gains, 0, 1))


def small_updates_kernel(sizes, side, *refs):
    classes, channels, out, gain_count = sizes
    table, last, _ = side_columns(*sizes)
    args, outs = refs[:12], refs[12:]
    shard = side.shape[1]
    down = lax.broadcasted_iota(jnp.int32, (shard, shard), 0)
    same = (down == lane_of((shard, shard))).astype(jnp.bfloat16)
    for b in range(2):

        def across(begin, end):
            return down_columns(side[b, :, begin:end], same)

        tail = across(last, last + LANES)
        grads = (
            across(table, table + LANES)[:channels],
            side[b, :, :classes].astype(jnp.float32),
            side[b, :, last : last + LANES].astype(jnp.float32)[:, :out],
            tail[out : out + gain_count],
        )
        rates = (RATES[0], RATES[1], RATES[6], RATES[7])
        for i in range(4):
            at = (slice(None), b) if i == 3 else (b,)
            now = [ref[at] for ref in args[3 * i : 3 * i + 3]]
            for ref, value in zip(outs[3 * i : 3 * i + 3], adam_step(*now, grads[i], rates[i])):
                ref[at] = value


def small_updates(side, groups, sizes):
    turns = ((0, 0), (1, 2), (0, 0), (0, 1))
    arrays = [jnp.swapaxes(part, *turn) for turn, group in zip(turns, groups) for part in group]
    results = pl.pallas_call(
        functools.partial(small_updates_kernel, sizes),
        out_shape=[jax.ShapeDtypeStruct(part.shape, part.dtype) for part in arrays],
        compiler_params=pltpu.CompilerParams(vmem_limit_bytes=48 * 2**20),
        name="small_updates",
    )(side, *arrays)
    return [jnp.swapaxes(part, *turns[i // 3]) for i, part in enumerate(results)]


def staged(patches, seg_lengths, class_labels, cotangent, low, sizes):
    half = lax.axis_size("rows") // 2
    second = lax.axis_index("rows") >= half
    x = lax.axis_index("seq")
    swap = [(i, (i + half) % (2 * half)) for i in range(2 * half)]
    beside = [(0, 1), (1, 0)]
    both = ("rows", "seq")
    across = [(2 * i + s, 2 * j + 1 - s) for i, j in swap for s in range(2)]
    classes, channels, out, gain_count = sizes
    table, last, _ = side_columns(*sizes)
    held, group, _ = patches.shape
    rows, length = held // 2, 2 * group

    pieces = jnp.concatenate([patches.astype(jnp.float32), cotangent], 2)
    pieces = jnp.pad(pieces, ((0, 0), (0, 0), (0, LANES - 2 * channels)))
    pieces = pieces.reshape(2, rows, group, LANES)
    keep = lax.dynamic_index_in_dim(pieces, x, 0, keepdims=False)
    give = lax.dynamic_index_in_dim(pieces, 1 - x, 0, keepdims=False)
    got = lax.ppermute(give, "seq", beside)
    mine = jnp.where(
        x == 0, jnp.concatenate([keep, got], 1), jnp.concatenate([got, keep], 1)
    ).reshape(TOKENS, LANES)
    theirs = lax.ppermute(mine, "rows", swap)
    facts = jnp.concatenate(
        [jnp.cumsum(seg_lengths, 1), class_labels, jnp.full((held, 1), length, jnp.int32)], 1
    )
    facts = lax.dynamic_slice_in_dim(facts, x * rows, rows, 0)
    their_facts = lax.ppermute(facts, "rows", swap)
    facts = jnp.where(
        second, jnp.stack([their_facts, facts], 0), jnp.stack([facts, their_facts], 0)
    )
    batches = jnp.where(second, jnp.stack([theirs, mine], 0), jnp.stack([mine, theirs], 0))
    batches, facts, low = lax.optimization_barrier((batches, facts, low))
    weights = gather_blocks(low, 1)
    lane = jnp.arange(LANES) < channels
    inputs = jnp.where(lane, batches, 0.0)
    cotangent = jnp.where(lane, jnp.roll(batches, -channels, 2), 0.0)
    (latents, grad_inputs, gain_grads), pairs = two_blocks(
        facts, inputs, cotangent, weights, table, channels, 3
    )

    def halves(part):
        part = part.reshape(rows, 2, group, LANES)
        ours = lax.dynamic_index_in_dim(part, x, 1, keepdims=False)
        return ours, lax.dynamic_index_in_dim(part, 1 - x, 1, keepdims=False)

    def in_order(ours, beside_us):
        return jnp.where(
            x == 0, jnp.concatenate([ours, beside_us], 0), jnp.concatenate([beside_us, ours], 0)
        )

    own = halves(jnp.where(second, latents[2], grad_inputs[2]))
    away = halves(jnp.where(second, latents[1], grad_inputs[1]))
    own_side = lax.ppermute(own[1], "seq", beside)
    away_here = lax.ppermute(away[0], "rows", swap)
    away_side = lax.ppermute(away[1], both, across)
    sums = summed_products(pairs, gain_grads, out, low, 2)
    ours, others = in_order(own[0], own_side), in_order(away_here, away_side)
    outcome = jnp.where(second, ours, others)
    patch_grad = jnp.where(second, others, ours)
    return outcome[..., :channels], outcome[..., channels], patch_grad[..., :channels], sums


def unstaged(mine, low, sizes):
    inputs, cotangent, seg_ids, labels = mine
    whole = [lax.all_gather(part, "rows", axis=1, tiled=True) for part in low]

    def block(index):
        picked = [part[index * LAYERS : (index + 1) * LAYERS] for part in whole[:4]]
        return picked + [whole[4][index]]

    back = seg_ids[:, ::-1], labels[:, ::-1]
    latent_one, det_one, saved_one = forward_block(inputs, seg_ids, labels, block(0), sizes)
    latent_two, det_two, saved_two = forward_block(latent_one[:, ::-1], *back, block(1), sizes)
    outcome = jnp.concatenate([latent_two, (det_two + det_one[:, ::-1])[..., None]], 2)
    grad_mid, parts_two = backward_block(cotangent, saved_two, block(1), sizes)
    patch_grad, parts_one = backward_block(grad_mid[:, ::-1], saved_one, block(0), sizes)
    grads = [
        jnp.concatenate(pair, 0)
        for pair in zip(
            weight_grads(parts_one, low[4].shape[2]), weight_grads(parts_two, low[4].shape[2])
        )
    ]
    sums = [
        lax.psum(
            lax.psum_scatter(grad, "rows", scatter_dimension=1, tiled=True).astype(jnp.float32),
            "seq",
        )
        for grad in grads
    ]
    return outcome, patch_grad, sums


def body(
    patches,
    seg_lengths,
    class_labels,
    cotangent,
    w_in,
    m_in,
    v_in,
    w_table,
    m_table,
    v_table,
    w_qkv,
    m_qkv,
    v_qkv,
    w_o,
    m_o,
    v_o,
    w_up,
    m_up,
    v_up,
    w_down,
    m_down,
    v_down,
    w_out,
    m_out,
    v_out,
    gains,
    m_gains,
    v_gains,
):
    masters = (w_in, w_table, w_qkv, w_o, w_up, w_down, w_out, gains)
    firsts = (m_in, m_table, m_qkv, m_o, m_up, m_down, m_out, m_gains)
    seconds = (v_in, v_table, v_qkv, v_o, v_up, v_down, v_out, v_gains)
    sizes = (w_table.shape[1], w_in.shape[1], w_out.shape[2], gains.shape[1])
    shards = [weight.astype(jnp.bfloat16) for weight in masters[2:6]]
    held, group, channels = patches.shape
    seq_count = lax.axis_size("seq")
    length = group * seq_count
    groups = list(zip(masters, firsts, seconds))
    fits = held == 4 and group * held == TOKENS and sizes[2] == 2 * channels and sizes[2] % 8 == 0
    if seq_count == 2 and lax.axis_size("rows") == 16 and fits:
        shards.append(packed_side(w_table, w_in, w_out, gains, sizes))
        latents, logdet, patch_grad, sums = staged(
            patches, seg_lengths, class_labels, cotangent, shards, sizes
        )
        small = small_updates(sums[4], [groups[i] for i in (0, 1, 6, 7)], sizes)
        updates = [None] * 8
        for i, where_at in enumerate((0, 1, 6, 7)):
            updates[where_at] = small[3 * i : 3 * i + 3]
        for i, where_at in enumerate((2, 3, 4, 5)):
            updates[where_at] = adam_step(
                *groups[where_at], sums[i].astype(jnp.float32), RATES[where_at]
            )
        results = (latents, logdet, patch_grad)
    else:
        small = [masters[i].astype(jnp.bfloat16) for i in (1, 0, 6, 7)]
        shards.append(pack_side(*small))
        share = max(1, held // seq_count)
        copies = seq_count * share // held
        first_row = (lax.axis_index("seq") // copies) * share
        pieces = jnp.concatenate([patches.astype(jnp.float32), cotangent], 2)
        pieces = lax.all_gather(pieces, "seq", axis=1, tiled=True)
        pieces = lax.dynamic_slice_in_dim(pieces, first_row, share, 0)
        seg_ids, labels = row_facts(
            lax.dynamic_slice_in_dim(seg_lengths, first_row, share, 0),
            lax.dynamic_slice_in_dim(class_labels, first_row, share, 0),
            length,
        )
        mine = (pieces[..., :channels], pieces[..., channels:], seg_ids, labels)
        outcome, patch_grad, sums = unstaged(mine, shards, sizes)
        results = lax.all_gather(jnp.concatenate([outcome, patch_grad], 2), "seq", axis=0)
        results = results[::copies].reshape((held,) + results.shape[2:])
        results = lax.dynamic_slice_in_dim(results, lax.axis_index("seq") * group, group, 1)
        results = (
            results[..., :channels],
            results[..., channels],
            results[..., channels + 1 :],
        )
        sums = [total.astype(jnp.float32) / copies for total in sums]
        table, first, last, gain = split_side(sums[4], *sizes)
        grads = (first, table, sums[0], sums[1], sums[2], sums[3], last, gain)
        updates = [adam_step(*item) for item in zip(masters, firsts, seconds, grads, RATES)]
    return results + tuple(part for update in updates for part in update)


def solution(mesh):
    tokens = P("rows", "seq", None)
    row = P("rows", None)
    last, middle = P(None, None, "rows"), P(None, "rows", None)
    weights = (last,) * 6 + (middle,) * 15 + (last,) * 3
    return jax.shard_map(
        body,
        mesh=mesh,
        in_specs=(tokens, row, row, tokens) + weights,
        out_specs=(tokens, P("rows", "seq"), tokens) + weights,
        check_vma=False,
    )
```

```python
import functools
from functools import partial

import jax
import jax.numpy as jnp
from jax import lax
from jax.experimental import pallas as pl
from jax.experimental.pallas import tpu as pltpu
from jax.sharding import PartitionSpec as P

HEADS = 12
HEAD_DIM = 64
LAYERS = 2
SEGS = 4
STEP = 10

EPS_NORM = 1e-05
MASKED = -1000000000.0
BETA_ONE = 0.9
BETA_TWO = 0.95
EPS_ADAM = 1e-08
DECAY = 0.1
RATES = (0.05, 0.3, 0.02, 0.05, 0.02, 0.01, 0.01, 0.3)

MESH_ID = pl.DeviceIdType.MESH
LANES = 128
LATE = (0, 1, 2)
GATHER_LAGS = (1.5, 3.5, 5.5, 8.5, 0.0, 1.0, 1.7, 3.0)


def place():
    r = lax.axis_index("rows")
    x = lax.axis_index("seq")
    c = lax.rem(r, 2)
    y = lax.rem(r // 2, 2)
    z = r // 4
    return r, x, y, z, c


def units_of(shards, d1_share):
    units = []
    order = sorted(range(len(shards)), key=lambda a: shards[a].shape[0])
    layers = max(s.shape[0] // 2 for s in shards)
    todo = [(a, 0) for a in order if shards[a].shape[0] == 2]
    for l in range(layers):
        todo += [(a, l) for a in order if shards[a].shape[0] > 2]
    for a, l in todo:
        n, rows, cols = shards[a].shape
        half = cols // 2
        if rows >= 64:
            first = max(16, round(rows * d1_share / 16) * 16)
            split = (0, first)
        else:
            first = max(LANES, round(half * d1_share / LANES) * LANES)
            split = (1, first)
        units.append((a, l, n // 2, rows, half, split))
    return units


def wait_all_of(cell, sem):
    pltpu.make_async_copy(cell, cell, sem).wait()


def gathering(units, late, lags, srcs, outs, send, recv, local):
    r, x, y, z, c = place()
    stage = z // 2
    other = 1 - stage
    zi = lax.rem(z, 2)
    dev_x = (r, 1 - x)
    dev_y = (r + 2 - 4 * y, x)
    dev_s = (r + 1 - 2 * c, x)
    z_near = z + 1 - 2 * zi
    z_src = (z_near, other * 2, other * 2 + 1)
    dev_z = tuple((zz * 4 + y * 2 + c, x) for zz in z_src)
    barrier = pltpu.get_barrier_semaphore()
    partners = (dev_x, dev_y, dev_s) + dev_z
    for dev in partners:
        pl.semaphore_signal(barrier, 1, device_id=dev, device_id_type=MESH_ID)
    pl.semaphore_wait(barrier, len(partners))

    inner = stage != zi
    dev_inner = ((1 + other) * 4 + y * 2 + c, x)
    side_of = jnp.where(inner, other, stage)
    z_mine, z_theirs = 2 * side_of, 2 - 2 * side_of
    started = []

    def alike(src):
        what = src.args + (None,) * 3
        if src.func is own_ref:
            return own(what[0], stage, None if what[2] is None else x)
        return cell(what[0], z, y, c, None if what[4] is None else x, what[5])

    def cell(*what):
        return functools.partial(cell_ref, *what)

    def own(*what):
        return functools.partial(own_ref, *what)

    def cell_ref(u, zz, yy, cc, h=None, part=None):
        a, l, _, rows, half, (dim, first) = units[u]
        row0, nrow = (zz * 4 + yy * 2 + cc) * rows, rows
        col0, ncol = (0, 2 * half) if h is None else (h * half, half)
        if part is not None:
            if dim == 0:
                row0, nrow = (row0, first) if part == 0 else (row0 + first, rows - first)
            else:
                col0, ncol = (col0, first) if part == 0 else (col0 + first, half - first)
        if h is not None:
            col0 = pl.multiple_of(col0, LANES)
        block = outs[a] if len(outs[a].shape) == 2 else outs[a].at[l]
        return block.at[pl.ds(pl.multiple_of(row0, 16), nrow), pl.ds(col0, ncol)]

    def own_ref(u, b, h=None):
        a, l, layers, rows, half, _ = units[u]
        if h is None:
            return srcs[a].at[layers * b + l]
        return srcs[a].at[layers * b + l, :, pl.ds(pl.multiple_of(h * half, LANES), half)]

    def push(u, src, dst, idx, dev, slot=None):
        slot = idx if slot is None else slot
        pltpu.make_async_remote_copy(
            src_ref=src(),
            dst_ref=dst(),
            send_sem=send.at[u, slot],
            recv_sem=recv.at[u, idx],
            device_id=dev,
            device_id_type=MESH_ID,
        ).start()
        started.append((u, slot, alike(src)))

    def arrived(u, dst, idx):
        wait_all_of(dst(), recv.at[u, idx])

    def relay_copy(u, piece, j):
        return pltpu.make_async_remote_copy(
            src_ref=piece(),
            dst_ref=piece(),
            send_sem=send.at[u, 24 + j],
            recv_sem=recv.at[u, j],
            device_id=dev_z[0],
            device_id_type=MESH_ID,
        )

    def relay(u, piece, j):
        @pl.when(inner)
        def _():
            relay_copy(u, piece, j).start()

    def begin(u):
        mine = cell(u, z, y, c, x)
        push(u, own(u, other, x), mine, 1 + zi, dev_inner, slot=1)
        if u in late:

            @pl.when(inner)
            def _():
                near_copy(u).start()

            @pl.when(jnp.logical_not(inner))
            def _():
                own_copy(u).start()

            return
        push(u, own(u, stage, x), mine, 0, dev_z[0])
        push(u, own(u, stage, x), mine, 10, dev_y)
        push(u, own(u, stage), cell(u, z, y, c), 17, dev_s)
        pltpu.make_async_copy(own(u, stage)(), cell(u, z, y, c)(), local.at[u]).start()

    def near_copy(u):
        return pltpu.make_async_remote_copy(
            src_ref=own(u, stage, x)(),
            dst_ref=cell(u, z, y, c, x)(),
            send_sem=send.at[u, 0],
            recv_sem=recv.at[u, 1 + zi],
            device_id=dev_z[0],
            device_id_type=MESH_ID,
        )

    def own_copy(u):
        return pltpu.make_async_copy(own(u, stage, x)(), cell(u, z, y, c, x)(), recv.at[u, 1 + zi])

    def near(u):
        if u in late:
            return
        arrived(u, cell(u, z, 1 - y, c, x), 10)
        push(u, cell(u, z, 1 - y, c, x), cell(u, z, 1 - y, c, x), 6, dev_x)
        side(u, 0, z_src[0], 0)

    def side(u, j, zz, idx):
        piece = cell(u, zz, y, c, x)
        arrived(u, piece, idx)
        if u not in late and j > 0:
            relay(u, piece, j)
        push(u, piece, piece, 3 + j, dev_x)
        push(u, piece, piece, 7 + j, dev_y)

    def spread(u):
        if u in late:
            for j in range(2):
                side(u, j, z_mine + j, 1 + j)
        else:
            for j in (1, 2):
                side(u, j, z_src[j], j)

    def turn(u, j, zz):
        arrived(u, cell(u, zz, y, c, 1 - x), 3 + j)
        part = cell(u, zz, y, c, 1 - x, 0)
        push(u, part, part, 11 + j, dev_y)
        arrived(u, cell(u, zz, 1 - y, c, x), 7 + j)
        part = cell(u, zz, 1 - y, c, x, 1)
        push(u, part, part, 14 + j, dev_x)

    def near_corner(u):
        if u not in late:
            turn(u, 0, z_src[0])
            slab = cell(u, z_src[0], y, c)
            push(u, slab, slab, 19, dev_s)

    def corner(u):
        if u in late:
            for j in range(2):
                turn(u, j, z_mine + j)
        else:
            for j in (1, 2):
                turn(u, j, z_src[j])
                slab = cell(u, z_src[j], y, c)
                push(u, slab, slab, 19 + j, dev_s)

    def corners_in(u, j, zz):
        arrived(u, cell(u, zz, 1 - y, c, 1 - x, 0), 11 + j)
        arrived(u, cell(u, zz, 1 - y, c, 1 - x, 1), 14 + j)

    def finish(u):
        if u in late:
            for j in range(2):
                corners_in(u, j, z_mine + j)
                for yy in range(2):
                    slab = cell(u, z_mine + j, yy, c)
                    push(u, slab, slab, (0, 5, 6, 9)[2 * j + yy], dev_z[0], slot=(2, 5, 6, 9)[2 * j + yy])
                    push(u, slab, slab, 17 + 2 * j + yy, dev_s)
            return
        arrived(u, cell(u, z, 1 - y, c, 1 - x), 6)
        slab = cell(u, z, 1 - y, c)
        push(u, slab, slab, 18, dev_s)
        for j in range(3):
            corners_in(u, j, z_src[j])
            slab = cell(u, z_src[j], 1 - y, c)
            push(u, slab, slab, 22 + j, dev_s)

    def last(u):
        if u in late:
            for j in range(2):
                for yy in range(2):
                    slab = cell(u, z_theirs + j, yy, c)
                    arrived(u, slab, (0, 5, 6, 9)[2 * j + yy])
                    push(u, slab, slab, 21 + 2 * j + yy, dev_s)

    n = len(units)
    order = sorted(range(n), key=lambda u: u not in late)
    events = [(1.0 * i - lags[7], begin, u) for i, u in enumerate(order)]
    events += [(lags[0] + 1.0 * i, spread, u) for i, u in enumerate(order)]
    events += [(lags[1] + 1.0 * i, corner, u) for i, u in enumerate(order)]
    events += [(lags[2] + 1.0 * i, finish, u) for i, u in enumerate(order)]
    events += [(lags[3] + 1.0 * i, last, u) for i, u in enumerate(order)]
    events += [(lags[4] + lags[5] * i, near, u) for i, u in enumerate(order)]
    events += [(lags[6] + 1.0 * i, near_corner, u) for i, u in enumerate(order)]
    events.sort(key=lambda event: event[0])

    def ready(u):
        while any(event[2] == u for event in events):
            _, act, unit = events.pop(0)
            act(unit)
        if u in late:
            for j in range(2):
                for yy in range(2):
                    arrived(u, cell(u, z_mine + j, yy, 1 - c), 17 + 2 * j + yy)
                    arrived(u, cell(u, z_theirs + j, yy, 1 - c), 21 + 2 * j + yy)
            return
        arrived(u, cell(u, z, y, 1 - c), 17)
        arrived(u, cell(u, z, 1 - y, 1 - c), 18)
        for j in range(3):
            arrived(u, cell(u, z_src[j], y, 1 - c), 19 + j)
            arrived(u, cell(u, z_src[j], 1 - y, 1 - c), 22 + j)
        pltpu.make_async_copy(own(u, stage)(), cell(u, z, y, c)(), local.at[u]).wait()

    def done():
        for u in range(n):
            if u in late:

                @pl.when(inner)
                def _():
                    near_copy(u).wait_send()

            else:

                @pl.when(inner)
                def _():
                    for j in (1, 2):
                        relay_copy(u, cell(u, z_src[j], y, c, x), j).wait_send()

        for u, slot, place_of in started:
            wait_all_of(place_of(), send.at[u, slot])

    return ready, done


TOKENS = 256
HALF_LANES = 64
FORWARD_VMEM = 58 * 2**20


def lane_of(shape):
    return lax.broadcasted_iota(jnp.int32, shape, len(shape) - 1)


def norm_rows(hidden):
    center = hidden - jnp.mean(hidden, -1, keepdims=True)
    inverse = lax.rsqrt(jnp.mean(center * center, -1, keepdims=True) + EPS_NORM)
    return center * inverse, inverse


def gelu_and_slope(v):
    root = 0.7978845608028654
    square = v * v
    wave = jnp.tanh(root * (v + 0.044715 * (square * v)))
    near = 0.5 * (1.0 + wave)
    slope = near + (0.5 * root) * v * (1.0 - wave * wave) * (1.0 + (3 * 0.044715) * square)
    return v * near, slope


def turned_round(part):
    length = part.shape[0]
    down = lax.broadcasted_iota(jnp.int32, (length, length), 0)
    flip = (down + lane_of((length, length)) == length - 1).astype(jnp.bfloat16)
    total = None
    for _ in range(3):
        high = part.astype(jnp.bfloat16)
        part = part - high.astype(jnp.float32)
        moved = jnp.dot(flip, high, preferred_element_type=jnp.float32)
        total = moved if total is None else total + moved
    return total


def packed_pair(part, length):
    lane = lane_of((length, LANES))
    return jnp.where(lane < HALF_LANES, part[:length], pltpu.roll(part[length:], HALF_LANES, 1))


def unpacked(part, row):
    lane = lane_of(part.shape)
    part = part if row == 0 else pltpu.roll(part, HALF_LANES, 1)
    return jnp.where(lane < HALF_LANES, part, 0.0)


def facts_of(facts, batch, second, row, places):
    at = jnp.where(second, facts[batch, row, 8] - 1 - places, places)
    segment = jnp.zeros(places.shape, jnp.int32)
    for k in range(SEGS):
        segment = segment + (at >= facts[batch, row, k]).astype(jnp.int32)
    label = jnp.zeros(places.shape, jnp.int32)
    for k in range(SEGS):
        label = jnp.where(segment == k, facts[batch, row, SEGS + k], label)
    return segment, label


def columns_of(facts, batch, second, rows, length):
    parts = []
    for row in range(rows):
        places = lax.broadcasted_iota(jnp.int32, (length, LANES), 0)
        segment, label = facts_of(facts, batch, second, row, places)
        before, _ = facts_of(facts, batch, second, row, places - 1)
        parts.append((segment, label, (places >= 1) & (segment == before)))
    return [
        jnp.concatenate([part[i].astype(jnp.int32) for part in parts], 0)[:, :1] for i in range(3)
    ]


def gain_rows_of(w_side, last, out, count):
    return w_side[:, last:].astype(jnp.float32).T[out : out + count]


def both_heads(pair, first):
    zero = jnp.zeros_like(pair)
    return jnp.concatenate([jnp.where(first, pair, zero), jnp.where(first, zero, pair)], 0)


def norm_rows_back(normed, inverse, grad_normed):
    mean_grad = jnp.mean(grad_normed, -1, keepdims=True)
    mean_proj = jnp.mean(grad_normed * normed, -1, keepdims=True)
    return inverse * (grad_normed - mean_grad - normed * mean_proj)


def by_rows(left, right):
    return lax.dot_general(
        left, right, (((1,), (1,)), ((), ())), preferred_element_type=jnp.float32
    )


def down_columns(left, right):
    return lax.dot_general(
        left, right, (((0,), (0,)), ((), ())), preferred_element_type=jnp.float32
    )


def blocks_kernel(
    sizes,
    units,
    facts,
    patches,
    cotangent,
    low_qkv,
    low_o,
    low_up,
    low_down,
    low_side,
    out_latent,
    out_grad,
    out_gains,
    hbm_na,
    hbm_aa,
    hbm_q,
    hbm_p,
    hbm_ctx,
    hbm_nm,
    hbm_am,
    hbm_slope,
    hbm_gelu,
    hbm_stat,
    hbm_nf,
    hbm_af,
    hbm_tail,
    hbm_start,
    hbm_gqkv,
    hbm_gmid,
    hbm_gup,
    hbm_gbr,
    hbm_gstart,
    hbm_gpred,
    w_qkv,
    w_o,
    w_up,
    w_down,
    w_side,
    na,
    aa,
    qkv,
    prob,
    ctx,
    nm,
    am,
    slope,
    gelu,
    stat,
    nf,
    af,
    tail,
    start,
    gqkv,
    gmid,
    gup,
    gbr,
    gstart,
    gpred,
    hidden,
    inputs,
    gain_rows,
    gact,
    gctx,
    sent,
    received,
    gather_send,
    gather_recv,
    gather_local,
    save_sem,
    last_sem,
    load_sem,
    once_sem,
    grad_sem,
    end_sem,
    send_sem,
    recv_sem,
):
    rows, length, table, channels = sizes
    layers, width = w_qkv.shape[0], w_qkv.shape[1]
    pairs = width // LANES
    half = lax.axis_size("rows") // 2
    me = lax.axis_index("rows")
    second = me >= half
    partner = (jnp.where(second, me - half, me + half), lax.axis_index("seq"))
    ready, done = gathering(
        units,
        LATE,
        GATHER_LAGS,
        (low_qkv, low_o, low_up, low_down, low_side),
        (w_qkv, w_o, w_up, w_down, w_side),
        gather_send,
        gather_recv,
        gather_local,
    )
    unit_of = {(unit[0], unit[1]): i for i, unit in enumerate(units)}

    def hop(slot):
        return pltpu.make_async_remote_copy(
            src_ref=sent.at[slot],
            dst_ref=received.at[slot],
            send_sem=send_sem.at[slot],
            recv_sem=recv_sem.at[slot],
            device_id=partner,
            device_id_type=MESH_ID,
        )

    lane = lane_of((TOKENS, LANES))

    layered = (
        (na, hbm_na),
        (aa, hbm_aa),
        (qkv, hbm_q),
        (prob, hbm_p),
        (ctx, hbm_ctx),
        (nm, hbm_nm),
        (am, hbm_am),
        (slope, hbm_slope),
        (gelu, hbm_gelu),
        (stat, hbm_stat),
    )
    single = ((nf, hbm_nf), (af, hbm_af), (tail, hbm_tail), (start, hbm_start))

    @pl.loop(0, 3)
    def _(step):
        batch = jnp.where(second, jnp.maximum(step - 1, 0), jnp.minimum(step, 1))

        def saving(layer, i):
            src, dst = layered[i]
            src = src if i == 7 else src.at[layer]
            return pltpu.make_async_copy(src, dst.at[step, layer], save_sem.at[layer, i])

        def whole(array, layer):
            @pl.when(step == 0)
            def _():
                ready(unit_of[array, layer])

        whole(4, 0)

        @pl.when(step == 0)
        def _():
            gain_rows[...] = gain_rows_of(w_side, table + LANES, 2 * channels, 8)

        for slot in range(2):

            @pl.when(step == slot + 1)
            def _():
                hop(slot).wait_recv()

        for row in range(rows):
            toks = pl.ds(row * length, length)

            @pl.when(jnp.logical_not(second))
            def _():
                inputs[toks, :] = patches[batch, toks, :]

            @pl.when(second & (step > 0))
            def _():
                before = received[jnp.maximum(step - 1, 0)]
                inputs[toks, :] = turned_round(unpacked(before, row))

            @pl.when(second & (step == 0))
            def _():
                inputs[toks, :] = jnp.zeros((length, LANES), jnp.float32)

        seg_col, labels, same = columns_of(facts, batch, second, rows, length)
        start[:, :table] = (labels == lane_of((TOKENS, table))).astype(jnp.bfloat16)
        start[:, table:] = inputs[...].astype(jnp.bfloat16)
        hidden[...] = by_rows(start[...], w_side[:, : table + LANES])
        for layer in range(layers):
            normed, inverse_a = norm_rows(hidden[...])
            na[layer] = normed
            saving(layer, 0).start()
            aa[layer] = (normed * gain_rows[2 * layer : 2 * layer + 1, :]).astype(jnp.bfloat16)
            saving(layer, 1).start()
            whole(0, layer)

            @pl.loop(0, 3)
            def _(i):
                cols = pl.ds(pl.multiple_of(i * width, LANES), width)
                qkv[layer, :, cols] = jnp.dot(
                    aa[layer], w_qkv[layer, :, cols], preferred_element_type=jnp.float32
                ).astype(jnp.bfloat16)

            saving(layer, 2).start()
            for row in range(rows):
                toks = pl.ds(row * length, length)
                causal = lax.broadcasted_iota(jnp.int32, (length, length), 0) >= lane_of(
                    (length, length)
                )
                places = lax.broadcasted_iota(jnp.int32, (8, length), 1)
                seg_row = facts_of(facts, batch, second, row, places)[0][:1]
                attend = (seg_col[row * length : (row + 1) * length] == seg_row) & causal
                attend = jnp.concatenate([attend.astype(jnp.float32)] * 2, 0) > 0.5
                first = lane_of((length, LANES)) < HALF_LANES
                for pair in range(pairs):

                    def part(i):
                        return qkv[layer, toks, pl.ds(i * width + pair * LANES, LANES)]

                    scores = by_rows(both_heads(part(0), first), part(1)) * HEAD_DIM ** (-0.5)
                    scores = jnp.where(attend, scores, MASKED)
                    expo = jnp.exp(scores - jnp.max(scores, -1, keepdims=True))
                    soft = expo / jnp.sum(expo, -1, keepdims=True)
                    prob[layer, row * pairs + pair] = soft
                    mixed = jnp.dot(
                        soft.astype(jnp.bfloat16), part(2), preferred_element_type=jnp.float32
                    )
                    ctx[layer, toks, pl.ds(pair * LANES, LANES)] = jnp.where(
                        first, mixed[:length], mixed[length:]
                    ).astype(jnp.bfloat16)

            saving(layer, 3).start()
            saving(layer, 4).start()
            whole(1, layer)
            hidden[...] = hidden[...] + jnp.dot(
                ctx[layer], w_o[layer], preferred_element_type=jnp.float32
            )
            normed, inverse_m = norm_rows(hidden[...])
            nm[layer] = normed
            saving(layer, 5).start()
            am[layer] = (normed * gain_rows[2 * layer + 1 : 2 * layer + 2, :]).astype(jnp.bfloat16)
            saving(layer, 6).start()
            stat[layer] = jnp.where(lane == 0, inverse_a, inverse_m)
            saving(layer, 9).start()
            whole(2, layer)
            if layer > 0:
                saving(layer - 1, 7).wait()

            @pl.loop(0, w_up.shape[2] // width)
            def _(i):
                cols = pl.ds(pl.multiple_of(i * width, LANES), width)
                upper = jnp.dot(am[layer], w_up[layer, :, cols], preferred_element_type=jnp.float32)
                value, rate = gelu_and_slope(upper)
                gelu[layer, :, cols] = value.astype(jnp.bfloat16)
                slope[:, cols] = rate

            saving(layer, 7).start()
            saving(layer, 8).start()
            whole(3, layer)
            hidden[...] = hidden[...] + jnp.dot(
                gelu[layer], w_down[layer], preferred_element_type=jnp.float32
            )

        normed, inverse_f = norm_rows(hidden[...])
        nf[...] = normed
        af[...] = (normed * gain_rows[2 * layers : 2 * layers + 1, :]).astype(jnp.bfloat16)
        prediction = jnp.dot(
            af[...], w_side[:, table + LANES :], preferred_element_type=jnp.float32
        )
        previous = pltpu.roll(prediction, 1, 0)
        shown = (same > 0) & (lane < channels)
        shift_alpha = jnp.where(shown, pltpu.roll(previous, LANES - channels, 1), 0.0)
        shift_mu = jnp.where(shown, previous, 0.0)
        latent = (inputs[...] - shift_mu) * jnp.exp(-shift_alpha)
        logdet = -jnp.sum(shift_alpha, -1, keepdims=True)
        result = jnp.where(lane == channels, logdet + inputs[...], latent)
        out_latent[step] = result
        for slot in range(2):

            @pl.when(step == slot)
            def _():
                sent[slot] = packed_pair(result, length)
                hop(slot).start()

        tail[0] = latent
        tail[1] = shift_alpha
        tail[2] = jnp.broadcast_to(inverse_f, (TOKENS, LANES))
        for i, (src, dst) in enumerate(single):
            pltpu.make_async_copy(src, dst.at[step], last_sem.at[i]).start()
        for layer in range(layers):
            for i in range(len(layered)):
                if i != 7 or layer == layers - 1:
                    saving(layer, i).wait()
        for i, (src, dst) in enumerate(single):
            pltpu.make_async_copy(src, dst.at[step], last_sem.at[i]).wait()

    back = ((nm, hbm_nm), (prob, hbm_p), (qkv, hbm_q), (na, hbm_na), (stat, hbm_stat))
    once = ((tail, hbm_tail), (nf, hbm_nf))
    order = list(reversed(range(layers)))

    @pl.loop(0, 3)
    def _(turn):
        batch = jnp.where(second, jnp.maximum(1 - turn, 0), jnp.minimum(2 - turn, 1))
        slot_of = 2 - turn

        def fetch(layer, i, step):
            src, dst = back[i][1], back[i][0]
            return pltpu.make_async_copy(src.at[step, layer], dst.at[layer], load_sem.at[layer, i])

        def fetch_slope(layer, step):
            return pltpu.make_async_copy(hbm_slope.at[step, layer], slope, load_sem.at[layer, 5])

        def fetch_once(i, step):
            return pltpu.make_async_copy(once[i][1].at[step], once[i][0], once_sem.at[i])

        def refill(copy_of):
            @pl.when(turn < 2)
            def _():
                copy_of(jnp.maximum(slot_of - 1, 0)).start()

        def await_load(copy_of):
            @pl.when(turn > 0)
            def _():
                copy_of(slot_of).wait()

        def saving(layer, i):
            src, dst = ((gqkv, hbm_gqkv), (gmid, hbm_gmid), (gup, hbm_gup), (gbr, hbm_gbr))[i]
            src = src if i == 2 else src.at[layer]
            return pltpu.make_async_copy(src, dst.at[slot_of, layer], grad_sem.at[layer, i])

        for slot in (2, 3):

            @pl.when(turn == slot - 1)
            def _():
                hop(slot).wait_recv()

        for row in range(rows):
            toks = pl.ds(row * length, length)

            @pl.when(second)
            def _():
                inputs[toks, :] = cotangent[batch, toks, :]

            @pl.when(jnp.logical_not(second) & (turn > 0))
            def _():
                before = received[jnp.maximum(turn, 1) + 1]
                inputs[toks, :] = turned_round(unpacked(before, row))

            @pl.when(jnp.logical_not(second) & (turn == 0))
            def _():
                inputs[toks, :] = jnp.zeros((length, LANES), jnp.float32)

        same = columns_of(facts, batch, second, rows, length)[2]
        await_load(functools.partial(fetch_once, 0))
        await_load(functools.partial(fetch_once, 1))
        scaled = inputs[...] * jnp.exp(-tail[1])
        grad_alpha = 1.0 - inputs[...] * tail[0]
        grad_prev = jnp.where(lane < channels, -scaled, pltpu.roll(grad_alpha, channels, 1))
        grad_prev = jnp.where((same > 0) & (lane < 2 * channels), grad_prev, 0.0)
        gpred[...] = pltpu.roll(grad_prev, TOKENS - 1, 0).astype(jnp.bfloat16)
        gact[...] = by_rows(gpred[...], w_side[:, table + LANES :])
        out_gains[turn] = jnp.zeros((8, width), jnp.float32)

        def through_norm(normed, inverse, index):
            grad = gact[...]
            out_gains[turn, index : index + 1, :] = jnp.sum(grad * normed, 0, keepdims=True)
            return norm_rows_back(normed, inverse, grad * gain_rows[index : index + 1, :])

        hidden[...] = through_norm(nf[...], tail[2][:, :1], 2 * layers)
        refill(functools.partial(fetch_once, 0))
        refill(functools.partial(fetch_once, 1))
        for layer in order:
            gbr[layer] = hidden[...].astype(jnp.bfloat16)
            saving(layer, 3).start()
            if layer == order[0]:
                await_load(functools.partial(fetch_slope, layer))
            else:
                fetch_slope(layer, slot_of).wait()
                saving(layer + 1, 2).wait()

            @pl.loop(0, w_up.shape[2] // width)
            def _(i):
                cols = pl.ds(pl.multiple_of(i * width, LANES), width)
                gup[:, cols] = (
                    by_rows(gbr[layer], w_down[layer, cols, :]) * slope[:, cols]
                ).astype(jnp.bfloat16)

            saving(layer, 2).start()
            if layer > 0:
                fetch_slope(layer - 1, slot_of).start()
            else:
                refill(functools.partial(fetch_slope, order[0]))
            gact[...] = by_rows(gup[...], w_up[layer])
            await_load(functools.partial(fetch, layer, 0))
            await_load(functools.partial(fetch, layer, 4))
            hidden[...] = hidden[...] + through_norm(
                nm[layer], stat[layer][:, 1:2], 2 * layer + 1
            )
            refill(functools.partial(fetch, layer, 0))
            gmid[layer] = hidden[...].astype(jnp.bfloat16)
            saving(layer, 1).start()
            gctx[...] = by_rows(gmid[layer], w_o[layer]).astype(jnp.bfloat16)
            await_load(functools.partial(fetch, layer, 1))
            await_load(functools.partial(fetch, layer, 2))
            for row in range(rows):
                toks = pl.ds(row * length, length)
                first = lane_of((length, LANES)) < HALF_LANES
                for pair in range(pairs):

                    def at(i):
                        return pl.ds(i * width + pair * LANES, LANES)

                    query = both_heads(qkv[layer, toks, at(0)], first)
                    key = qkv[layer, toks, at(1)]
                    value = qkv[layer, toks, at(2)]
                    grad = both_heads(gctx[toks, at(0)], first)
                    soft = prob[layer, row * pairs + pair]
                    grad_soft = by_rows(grad, value)
                    delta = jnp.sum(soft * grad_soft, -1, keepdims=True)
                    grad_scores = (soft * (grad_soft - delta)).astype(jnp.bfloat16)
                    factor = HEAD_DIM ** (-0.5)
                    mixed = jnp.dot(grad_scores, key, preferred_element_type=jnp.float32) * factor
                    gqkv[layer, toks, at(0)] = jnp.where(
                        first, mixed[:length], mixed[length:]
                    ).astype(jnp.bfloat16)
                    gqkv[layer, toks, at(1)] = (
                        down_columns(grad_scores, query) * factor
                    ).astype(jnp.bfloat16)
                    gqkv[layer, toks, at(2)] = down_columns(
                        soft.astype(jnp.bfloat16), grad
                    ).astype(jnp.bfloat16)

            refill(functools.partial(fetch, layer, 1))
            refill(functools.partial(fetch, layer, 2))
            saving(layer, 0).start()
            gact[...] = by_rows(gqkv[layer], w_qkv[layer])
            await_load(functools.partial(fetch, layer, 3))
            hidden[...] = hidden[...] + through_norm(na[layer], stat[layer][:, :1], 2 * layer)
            refill(functools.partial(fetch, layer, 3))
            refill(functools.partial(fetch, layer, 4))
        gstart[...] = hidden[...].astype(jnp.bfloat16)
        grad_inputs = scaled + jnp.dot(
            gstart[...], w_side[:, table : table + LANES], preferred_element_type=jnp.float32
        )
        grad_inputs = jnp.where(lane < channels, grad_inputs, 0.0)
        out_grad[turn] = grad_inputs
        for slot in (2, 3):

            @pl.when(turn == slot - 2)
            def _():
                sent[slot] = packed_pair(grad_inputs, length)
                hop(slot).start()

        ends = ((gstart, hbm_gstart), (gpred, hbm_gpred))
        for i, (src, dst) in enumerate(ends):
            pltpu.make_async_copy(src, dst.at[slot_of], end_sem.at[i]).start()
        for layer in range(layers):
            for i in range(4):
                if i != 2 or layer == 0:
                    saving(layer, i).wait()
        for i, (src, dst) in enumerate(ends):
            pltpu.make_async_copy(src, dst.at[slot_of], end_sem.at[i]).wait()

    for slot in range(4):
        hop(slot).wait_send()
    done()


def two_blocks(facts, patches, cotangent, shards, table, channels, collective_id):
    rows = facts.shape[1]
    length = TOKENS // rows
    layers, width, hidden = shards[2].shape[0] // 2, 16 * shards[2].shape[1], shards[2].shape[2]
    units = units_of(shards, 0.5)
    n = len(units)
    pairs = rows * width // LANES
    low, full = jnp.bfloat16, jnp.float32
    kept = [
        ((layers, TOKENS, width), full),
        ((layers, TOKENS, width), low),
        ((layers, TOKENS, 3 * width), low),
        ((layers, pairs, 2 * length, length), full),
        ((layers, TOKENS, width), low),
        ((layers, TOKENS, width), full),
        ((layers, TOKENS, width), low),
        ((layers, TOKENS, hidden), full),
        ((layers, TOKENS, hidden), low),
        ((layers, TOKENS, LANES), full),
        ((TOKENS, width), full),
        ((TOKENS, width), low),
        ((3, TOKENS, LANES), full),
        ((TOKENS, table + LANES), low),
        ((layers, TOKENS, 3 * width), low),
        ((layers, TOKENS, width), low),
        ((layers, TOKENS, hidden), low),
        ((layers, TOKENS, width), low),
        ((TOKENS, width), low),
        ((TOKENS, LANES), low),
    ]
    scratch = [pltpu.VMEM((layers, 16 * s.shape[1], s.shape[2]), low) for s in shards[:4]]
    scratch.append(pltpu.VMEM((width, shards[4].shape[2]), low))
    for i, (shape, kind) in enumerate(kept):
        scratch.append(pltpu.VMEM(shape[1:] if i in (7, 16) else shape, kind))
    dma = pltpu.SemaphoreType.DMA
    scratch += [
        pltpu.VMEM((TOKENS, width), full),
        pltpu.VMEM((TOKENS, LANES), full),
        pltpu.VMEM((8, width), full),
        pltpu.VMEM((TOKENS, width), full),
        pltpu.VMEM((TOKENS, width), low),
        pltpu.VMEM((4, length, LANES), full),
        pltpu.VMEM((4, length, LANES), full),
        dma((n, 27)),
        dma((n, 25)),
        dma((n,)),
        dma((layers, 10)),
        dma((4,)),
        dma((layers, 6)),
        dma((2,)),
        dma((layers, 4)),
        dma((2,)),
        dma((4,)),
        dma((4,)),
    ]
    vmem, hbm = pl.BlockSpec(memory_space=pltpu.VMEM), pl.BlockSpec(memory_space=pl.ANY)
    smem = pl.BlockSpec(memory_space=pltpu.SMEM)
    results = pl.pallas_call(
        functools.partial(blocks_kernel, (rows, length, table, channels), units),
        out_shape=[jax.ShapeDtypeStruct((3, TOKENS, LANES), full)] * 2
        + [jax.ShapeDtypeStruct((3, 8, width), full)]
        + [jax.ShapeDtypeStruct((3,) + shape, kind) for shape, kind in kept],
        in_specs=[smem] + [vmem] * 2 + [hbm] * 5,
        out_specs=[vmem] * 3 + [hbm] * len(kept),
        scratch_shapes=scratch,
        compiler_params=pltpu.CompilerParams(
            collective_id=collective_id, has_side_effects=True, vmem_limit_bytes=61 * 2**20
        ),
        name="two_blocks",
    )(facts, patches, cotangent, *shards)
    _, aa, _, _, ctx, _, am, _, gelu, _, _, af, _, start = results[3:17]
    gqkv, gmid, gup, gbr, gstart, gpred = results[17:]
    pairs = (aa, gqkv, ctx, gmid, am, gup, gelu, gbr, start, gstart, af, gpred)
    return results[:3], pairs


EARLY = (4, 8)
CORNER_SHARE = 0.7
SUM_LAGS = (0, 1, 3, 4, 6, 8)


def products_kernel(units, early, n_pairs, out_count, *refs):
    per = 2 * n_pairs
    steps, gain_grads = refs[:per], refs[per]
    outs = refs[per + 1 : per + 6]
    rest = refs[per + 6 :]
    bufs, made, turned = rest[:per], rest[per : per + 5], rest[per + 5]
    rest = rest[per + 6 :]
    n = len(units)
    acc, in_x, in_y, in_d, in_z, in_n = [rest[i * n : (i + 1) * n] for i in range(6)]
    gain_cols, in_sem, send, recv, local_out = rest[6 * n :]
    r, x, y, z, c = place()
    stage = z // 2
    other = 1 - stage
    zi = lax.rem(z, 2)
    dev_x = (r, 1 - x)
    dev_y = (r + 2 - 4 * y, x)
    dev_s = (r + 1 - 2 * c, x)
    z_dst = (z + 1 - 2 * zi, other * 2, other * 2 + 1)
    dev_z = tuple((zz * 4 + y * 2 + c, x) for zz in z_dst)
    inner = stage != zi
    side_of = jnp.where(inner, other, stage)
    z_mine, z_theirs = 2 * side_of, 2 - 2 * side_of
    barrier = pltpu.get_barrier_semaphore()
    partners = (dev_x, dev_y, dev_s) + dev_z
    for dev in partners:
        pl.semaphore_signal(barrier, 1, device_id=dev, device_id_type=MESH_ID)

    def loads(i, layer):
        copies = []
        for k, step in enumerate((1, 2 * stage)):
            src = steps[i].at[step, layer] if len(steps[i].shape) == 4 else steps[i].at[step]
            dst = bufs[i].at[pl.ds(k * TOKENS, TOKENS)]
            copies.append(pltpu.make_async_copy(src, dst, in_sem.at[layer, 2 * i + k]))
        return copies

    def fetch(i, layer):
        for copy in loads(i, layer):
            copy.start()

    def fetched(i, layer):
        for copy in loads(i, layer):
            copy.wait()

    for i in (8, 9, 10, 11):
        fetch(i, 0)
    for i in range(8):
        fetch(i, 0)
    pl.semaphore_wait(barrier, len(partners))
    started = {}

    def copy_of(u, src, dst, slot, dev, idx=None):
        return pltpu.make_async_remote_copy(
            src_ref=src,
            dst_ref=dst,
            send_sem=send.at[u, slot],
            recv_sem=recv.at[u, slot if idx is None else idx],
            device_id=dev,
            device_id_type=MESH_ID,
        )

    def push(u, src, dst, slot, dev, idx=None):
        started[u, slot] = copy_of(u, src, dst, slot, dev, idx)
        started[u, slot].start()

    def planes(u):
        return (z_mine, 2) if u in early else (0, 4)

    def arrived(u, dst, idx):
        wait_all_of(dst, recv.at[u, idx])

    def part_of(u, part):
        _, _, _, rows, half, (dim, cut) = units[u]
        if dim == 0:
            return (pl.ds(0, cut), pl.ds(0, half)) if part == 0 else (pl.ds(cut, rows - cut), pl.ds(0, half))
        return (pl.ds(0, rows), pl.ds(0, cut)) if part == 0 else (pl.ds(0, rows), pl.ds(cut, half - cut))

    block, strip = turned.shape[0], 3 * LANES

    def multiply(out, rows, right, m, begin, count, wide, extra=None):
        def one(cols, out_cols):
            product = jnp.dot(turned[...], right[:, cols], preferred_element_type=jnp.float32)
            if extra is not None:
                product = product + extra[...]
            product = product.astype(jnp.bfloat16)
            for k in range(block // rows):
                s = m * (block // rows) + k
                out[s // 4, (s // 2) % 2, s % 2, :, out_cols] = product[k * rows : (k + 1) * rows]

        if count == 1:
            one(slice(0, wide), slice(begin, begin + wide))
        else:

            @pl.loop(0, count)
            def _(i):
                cols = pl.ds(pl.multiple_of(i * wide, LANES), wide)
                one(cols, cols)

    def product(u):
        a, layer, _, rows, half, _ = units[u]
        if a == 4:
            for i in (8, 9, 10, 11):
                fetched(i, 0)
            turned[...] = bufs[9][...].T
            multiply(made[4], rows, bufs[8], 0, 0, bufs[8].shape[1] // strip, strip)
            turned[...] = bufs[10][...].T
            gains = gain_grads[1] + gain_grads[2 - 2 * stage]
            zeros = jnp.zeros((LANES, gains.shape[1]), jnp.float32)
            tall = jnp.concatenate([zeros[:out_count], gains, zeros[out_count + 8 :]], 0)
            gain_cols[...] = tall.T
            multiply(made[4], rows, bufs[11], 0, bufs[8].shape[1], 1, LANES, gain_cols)
        else:
            fetched(2 * a, layer)
            fetched(2 * a + 1, layer)
            if layer > 0:
                for h in range(2):
                    started.pop((u - 4, h)).wait_send()
            for m in range(bufs[2 * a].shape[1] // block):
                turned[...] = bufs[2 * a][:, m * block : (m + 1) * block].T
                multiply(made[a], rows, bufs[2 * a + 1], m, 0, 2 * half // strip, strip)
            if layer + 1 < units[-1][1] + 1:
                fetch(2 * a, layer + 1)
                fetch(2 * a + 1, layer + 1)
        for h in range(2):
            cols = pl.ds(h * half, half)
            push(u, made[a].at[:, :, 1 - c, :, cols], acc[u].at[:, :, h], h, dev_s)

    def chip_sum(u):
        a, layer, _, rows, half, _ = units[u]
        for h in range(2):
            arrived(u, acc[u].at[:, :, h], h)

        @pl.loop(0, 4)
        def _(zz):
            for yy in range(2):
                for h in range(2):
                    mine = made[a][zz, yy, c, :, h * half : (h + 1) * half]
                    acc[u][zz, yy, h] = acc[u][zz, yy, h] + mine

        if u in early:
            push(u, acc[u].at[pl.ds(z_theirs, 2)], in_n[u], 11, dev_z[0])
        else:
            corner(u)

    def near_sum(u):
        if u in early:
            arrived(u, in_n[u], 11)

            @pl.loop(0, 2)
            def _(i):
                for yy in range(2):
                    for h in range(2):
                        acc[u][z_mine + i, yy, h] = acc[u][z_mine + i, yy, h] + in_n[u][i, yy, h]

            corner(u)

    def corner(u):
        base, count = planes(u)
        for part, dev in ((0, dev_y), (1, dev_x)):
            rs, cs = part_of(u, part)
            src = acc[u].at[pl.ds(base, count), 1 - y, 1 - x, rs, cs]
            push(u, src, in_d[u].at[:, rs, cs], 2 + part, dev)

    def side_sum(u):
        base, count = planes(u)
        for part, yy, h, dev, into in ((0, y, 1 - x, dev_x, in_x), (1, 1 - y, x, dev_y, in_y)):
            rs, cs = part_of(u, part)
            arrived(u, in_d[u].at[:, rs, cs], 2 + part)

            @pl.loop(0, count)
            def _(i):
                zz = base + i
                acc[u][zz, yy, h, rs, cs] = acc[u][zz, yy, h, rs, cs] + in_d[u][i, rs, cs]

            push(u, acc[u].at[pl.ds(base, count), yy, h], into[u], 4 + part, dev)

    def to_near(u):
        return copy_of(u, acc[u].at[z_dst[0], y, x], in_z[u].at[0], 6, dev_z[0])

    def to_far(u, i):
        where_to = in_z[u].at[1] if u in early else in_z[u].at[1 + zi]
        idx = 7 if u in early else 7 + zi
        return copy_of(u, acc[u].at[z_dst[1 + i], y, x], where_to, 7 + i, dev_z[1 + i], idx)

    def plane_sum(u):
        arrived(u, in_x[u], 4)
        arrived(u, in_y[u], 5)
        base, count = planes(u)

        @pl.loop(0, count)
        def _(i):
            acc[u][base + i, y, x] = (
                acc[u][base + i, y, x].astype(jnp.float32)
                + in_x[u][i].astype(jnp.float32)
                + in_y[u][i].astype(jnp.float32)
            ).astype(jnp.bfloat16)

        along_z(u, "start")

    def along_z(u, what):
        if u in early:

            @pl.when(inner)
            def _():
                for i in range(2):
                    getattr(to_far(u, i), what)()

            @pl.when(jnp.logical_not(inner))
            def _():
                getattr(to_near(u), what)()
        else:
            for copy in (to_far(u, 0), to_far(u, 1), to_near(u)):
                getattr(copy, what)()

    def owned(u, b, h):
        a, layer, layers, _, half, _ = units[u]
        return outs[a].at[layers * b + layer, :, pl.ds(pl.multiple_of(h * half, LANES), half)]

    def totals(u):
        return ((acc[u].at[z, y, x], stage), (in_z[u].at[1], other))

    def total(u):
        if u in early:
            started.pop((u, 11)).wait_send()
            arrived(u, in_z[u].at[1], 7)

            @pl.when(inner)
            def _():
                arrived(u, in_z[u].at[0], 6)
                acc[u][z, y, x] = in_z[u][0]
        else:
            for j in range(3):
                arrived(u, in_z[u].at[j], 6 + j)
            acc[u][z, y, x] = acc[u][z, y, x] + in_z[u][0]
            in_z[u][1] = in_z[u][1] + in_z[u][2]
        for k, (src, b) in enumerate(totals(u)):
            push(u, src, owned(u, b, x), 9 + k, dev_x)
            pltpu.make_async_copy(src, owned(u, b, x), local_out.at[u, k]).start()

    acts = (product, chip_sum, near_sum, side_sum, plane_sum, total)
    for t in range(n + SUM_LAGS[-1]):
        for lag, act in zip(SUM_LAGS, acts):
            if 0 <= t - lag < n:
                act(t - lag)
    for u in range(n):
        for k, (src, b) in enumerate(totals(u)):
            arrived(u, owned(u, b, 1 - x), 9 + k)
            pltpu.make_async_copy(src, owned(u, b, x), local_out.at[u, k]).wait()
        along_z(u, "wait_send")
    for cp in started.values():
        cp.wait_send()


def summed_products(operands, gain_grads, out_count, shards, collective_id):
    low = jnp.bfloat16
    out = [jax.ShapeDtypeStruct(s.shape, low) for s in shards]
    units = units_of(out, CORNER_SHARE)
    n = len(units)
    layers = max(u[1] for u in units) + 1
    n_pairs = len(operands) // 2
    width = operands[0].shape[-1]
    hbm, vmem = pl.BlockSpec(memory_space=pl.ANY), pl.BlockSpec(memory_space=pltpu.VMEM)

    def slots(lead, early_lead=None):
        leads = [early_lead if i in EARLY and early_lead else lead for i in range(n)]
        return [pltpu.VMEM(some + (u[3], u[4]), low) for some, u in zip(leads, units)]

    return pl.pallas_call(
        functools.partial(products_kernel, units, EARLY, n_pairs, out_count),
        out_shape=out,
        in_specs=[hbm] * (2 * n_pairs) + [vmem],
        out_specs=[hbm] * 5,
        scratch_shapes=[
            pltpu.VMEM((2 * TOKENS, part.shape[-1]), low) for part in operands
        ]
        + [pltpu.VMEM((4, 2, 2) + s.shape[1:], low) for s in shards]
        + [pltpu.VMEM((width, 2 * TOKENS), low)]
        + slots((4, 2, 2))
        + slots((4,), (2,))
        + slots((4,), (2,))
        + slots((4,), (2,))
        + slots((3,), (2,))
        + [
            pltpu.VMEM((2, 2, 2, u[3], u[4]) if i in EARLY else (16, LANES), low)
            for i, u in enumerate(units)
        ]
        + [
            pltpu.VMEM((width, LANES), jnp.float32),
            pltpu.SemaphoreType.DMA((layers, 4 * n_pairs)),
            pltpu.SemaphoreType.DMA((n, 12)),
            pltpu.SemaphoreType.DMA((n, 12)),
            pltpu.SemaphoreType.DMA((n, 2)),
        ],
        compiler_params=pltpu.CompilerParams(
            collective_id=collective_id, has_side_effects=True, vmem_limit_bytes=62 * 2**20
        ),
        name="summed_products",
    )(*operands, gain_grads)


def dot(left, right, dims=((1,), (0,))):
    return lax.dot_general(left, right, (dims, ((), ())), preferred_element_type=jnp.float32)


def normalize(hidden):
    center = hidden - jnp.mean(hidden, -1, keepdims=True)
    inverse = lax.rsqrt(jnp.mean(center * center, -1, keepdims=True) + EPS_NORM)
    return (center * inverse, inverse)


def normalize_back(normed, inverse, grad_normed):
    mean_grad = jnp.mean(grad_normed, -1, keepdims=True)
    mean_proj = jnp.mean(grad_normed * normed, -1, keepdims=True)
    return inverse * (grad_normed - mean_grad - normed * mean_proj)


def padded(count, unit):
    return -(-count // unit) * unit


def side_columns(classes, channels, out, gains):
    table = padded(classes, LANES)
    last = table + padded(channels, LANES)
    return table, last, padded(last + out + gains, 2 * LANES)


def pack_side(w_table, w_in, w_out, gains):
    blocks, classes, shard = w_table.shape
    channels, out, gain_count = w_in.shape[1], w_out.shape[2], gains.shape[1]
    table, last, total = side_columns(classes, channels, out, gain_count)

    def gap(count):
        return jnp.zeros((blocks, shard, count), w_table.dtype)

    return jnp.concatenate(
        [
            jnp.swapaxes(w_table, 1, 2),
            gap(table - classes),
            jnp.swapaxes(w_in, 1, 2),
            gap(last - table - channels),
            w_out,
            jnp.swapaxes(gains, 1, 2),
            gap(total - last - out - gain_count),
        ],
        2,
    )


def split_side(side, classes, channels, out, gains):
    table, last, _ = side_columns(classes, channels, out, gains)
    return (
        jnp.swapaxes(side[..., :classes], -1, -2),
        jnp.swapaxes(side[..., table : table + channels], -1, -2),
        side[..., last : last + out],
        jnp.swapaxes(side[..., last + out : last + out + gains], -1, -2),
    )


def heads_of(flat, rows):
    return flat.reshape(rows, -1, HEADS, HEAD_DIM)


def attention_scores(query, key_rows, attend):
    scores = jnp.einsum(
        "rqhd,rkhd->rhqk", query, key_rows, preferred_element_type=jnp.float32
    ) * HEAD_DIM ** (-0.5)
    return jnp.where(attend[:, None], scores, MASKED)


def forward_block(inputs, seg_ids, labels, weights, sizes):
    w_qkv, w_o, w_up, w_down, side = weights
    classes, channels, out, gain_count = sizes
    table, last, _ = side_columns(*sizes)
    rows, length, _ = inputs.shape
    tokens = rows * length
    width = side.shape[0]
    places = jnp.arange(length, dtype=jnp.int32)
    attend = (seg_ids[:, :, None] == seg_ids[:, None, :]) & (
        places[None, :, None] >= places[None, None, :]
    )
    same_seg = jnp.concatenate(
        [jnp.zeros((rows, 1), bool), seg_ids[:, 1:] == seg_ids[:, :-1]], 1
    )[..., None]
    onehot = labels.reshape(tokens, 1) == jnp.arange(table)[None, :]
    start = jnp.concatenate(
        [
            onehot.astype(jnp.bfloat16),
            inputs.reshape(tokens, channels).astype(jnp.bfloat16),
            jnp.zeros((tokens, last - table - channels), jnp.bfloat16),
        ],
        1,
    )
    gain_rows = side[:, last + out : last + out + gain_count].astype(jnp.float32).T
    hidden = dot(start, side[:, :last], ((1,), (1,)))
    kept = []
    for layer in range(w_qkv.shape[0]):
        normed_a, inverse_a = normalize(hidden)
        act_a = (normed_a * gain_rows[2 * layer]).astype(jnp.bfloat16)
        qkv = dot(act_a, w_qkv[layer]).astype(jnp.bfloat16)
        query, key_rows, value_rows = [
            heads_of(qkv[:, i * width : (i + 1) * width], rows) for i in range(3)
        ]
        scores = attention_scores(query, key_rows, attend)
        row_top = jnp.max(scores, -1, keepdims=True)
        expo_rows = jnp.exp(scores - row_top)
        row_total = jnp.sum(expo_rows, -1, keepdims=True)
        soft_low = (expo_rows / row_total).astype(jnp.bfloat16)
        log_total = row_top + jnp.log(row_total)
        context = jnp.einsum(
            "rhqk,rkhd->rqhd", soft_low, value_rows, preferred_element_type=jnp.float32
        )
        context = context.reshape(tokens, width).astype(jnp.bfloat16)
        middle = hidden + dot(context, w_o[layer])
        normed_m, inverse_m = normalize(middle)
        act_m = (normed_m * gain_rows[2 * layer + 1]).astype(jnp.bfloat16)
        upper = dot(act_m, w_up[layer])
        gelu_low = jax.nn.gelu(upper, approximate=True).astype(jnp.bfloat16)
        hidden = middle + dot(gelu_low, w_down[layer])
        kept.append(
            (
                normed_a,
                inverse_a,
                act_a,
                qkv,
                log_total,
                context,
                normed_m,
                inverse_m,
                act_m,
                upper,
                gelu_low,
            )
        )
    normed_f, inverse_f = normalize(hidden)
    act_f = (normed_f * gain_rows[gain_count - 1]).astype(jnp.bfloat16)
    prediction = dot(act_f, side[:, last : last + out]).reshape(rows, length, out)
    previous = jnp.concatenate([jnp.zeros((rows, 1, out), jnp.float32), prediction[:, :-1]], 1)
    shift = jnp.where(same_seg, previous, 0.0)
    shift_alpha = shift[..., channels:]
    latent = (inputs - shift[..., :channels]) * jnp.exp(-shift_alpha)
    saved = (attend, same_seg, start, kept, normed_f, inverse_f, act_f, shift_alpha, latent)
    return (latent, -jnp.sum(shift_alpha, -1), saved)


def backward_block(grad_latent, saved, weights, sizes):
    w_qkv, w_o, w_up, w_down, side = weights
    classes, channels, out, gain_count = sizes
    table, last, _ = side_columns(*sizes)
    attend, same_seg, start, kept, normed_f, inverse_f, act_f, shift_alpha, latent = saved
    rows, length, _ = latent.shape
    tokens = rows * length
    width = side.shape[0]
    factor = HEAD_DIM ** (-0.5)
    gain_rows = side[:, last + out : last + out + gain_count].astype(jnp.float32).T
    scale_back = jnp.exp(-shift_alpha)
    grad_inputs = grad_latent * scale_back
    grad_prev = jnp.where(
        same_seg, jnp.concatenate([-grad_inputs, 1.0 - grad_latent * latent], 2), 0.0
    )
    grad_pred = jnp.concatenate([grad_prev[:, 1:], jnp.zeros((rows, 1, out), jnp.float32)], 1)
    grad_pred = grad_pred.reshape(tokens, out).astype(jnp.bfloat16)
    grad_act = dot(grad_pred, side[:, last : last + out], ((1,), (1,)))
    gain_grads = [None] * gain_count
    gain_grads[-1] = jnp.sum(grad_act * normed_f, 0)
    grad_hidden = normalize_back(normed_f, inverse_f, grad_act * gain_rows[gain_count - 1])
    pairs = [None] * w_qkv.shape[0]
    for layer in reversed(range(w_qkv.shape[0])):
        (
            normed_a,
            inverse_a,
            act_a,
            qkv,
            log_total,
            context,
            normed_m,
            inverse_m,
            act_m,
            upper,
            gelu_low,
        ) = kept[layer]
        grad_branch = grad_hidden.astype(jnp.bfloat16)
        grad_gelu = dot(grad_branch, w_down[layer], ((1,), (1,)))
        gelu_pull = jax.vjp(partial(jax.nn.gelu, approximate=True), upper)[1]
        grad_upper = gelu_pull(grad_gelu)[0].astype(jnp.bfloat16)
        grad_act_m = dot(grad_upper, w_up[layer], ((1,), (1,)))
        gain_grads[2 * layer + 1] = jnp.sum(grad_act_m * normed_m, 0)
        grad_middle = grad_hidden + normalize_back(
            normed_m, inverse_m, grad_act_m * gain_rows[2 * layer + 1]
        )
        grad_mid_low = grad_middle.astype(jnp.bfloat16)
        grad_context = heads_of(
            dot(grad_mid_low, w_o[layer], ((1,), (1,))).astype(jnp.bfloat16), rows
        )
        query, key_rows, value_rows = [
            heads_of(qkv[:, i * width : (i + 1) * width], rows) for i in range(3)
        ]
        soft_rows = jnp.exp(attention_scores(query, key_rows, attend) - log_total)
        soft_low = soft_rows.astype(jnp.bfloat16)
        grad_soft = jnp.einsum(
            "rqhd,rkhd->rhqk", grad_context, value_rows, preferred_element_type=jnp.float32
        )
        row_delta = jnp.sum(soft_rows * grad_soft, -1, keepdims=True)
        grad_scores = (soft_rows * (grad_soft - row_delta)).astype(jnp.bfloat16)
        grad_query = factor * jnp.einsum(
            "rhqk,rkhd->rqhd", grad_scores, key_rows, preferred_element_type=jnp.float32
        )
        grad_keys = factor * jnp.einsum(
            "rhqk,rqhd->rkhd", grad_scores, query, preferred_element_type=jnp.float32
        )
        grad_values = jnp.einsum(
            "rhqk,rqhd->rkhd", soft_low, grad_context, preferred_element_type=jnp.float32
        )
        grad_qkv = jnp.concatenate(
            [part.reshape(tokens, width) for part in (grad_query, grad_keys, grad_values)], 1
        ).astype(jnp.bfloat16)
        grad_act_a = dot(grad_qkv, w_qkv[layer], ((1,), (1,)))
        gain_grads[2 * layer] = jnp.sum(grad_act_a * normed_a, 0)
        grad_hidden = grad_middle + normalize_back(
            normed_a, inverse_a, grad_act_a * gain_rows[2 * layer]
        )
        pairs[layer] = (
            (act_a, grad_qkv),
            (context, grad_mid_low),
            (act_m, grad_upper),
            (gelu_low, grad_branch),
        )
    grad_start = grad_hidden.astype(jnp.bfloat16)
    grad_inputs = grad_inputs + dot(grad_start, side[:, table : table + channels]).reshape(
        rows, length, channels
    )
    return grad_inputs, (
        pairs,
        (start, grad_start),
        (act_f, grad_pred),
        jnp.stack(gain_grads, 1),
    )


def weight_grads(parts, side_total):
    pairs, (start, grad_start), (act_f, grad_pred), gain_grads = parts
    arrays = [
        jnp.stack([dot(*layer[i], ((0,), (0,))).astype(jnp.bfloat16) for layer in pairs], 0)
        for i in range(4)
    ]
    side = [
        dot(grad_start, start, ((0,), (0,))),
        dot(act_f, grad_pred, ((0,), (0,))),
        gain_grads,
    ]
    count = sum(part.shape[1] for part in side)
    side.append(jnp.zeros((gain_grads.shape[0], side_total - count), jnp.float32))
    side = jnp.concatenate(side, 1).astype(jnp.bfloat16)
    return arrays + [side[None]]


def adam_step(weight, first, second, grad, rate):
    first_new = BETA_ONE * first + (1.0 - BETA_ONE) * grad
    second_new = BETA_TWO * second + (1.0 - BETA_TWO) * grad * grad
    first_hat = first_new / (1.0 - BETA_ONE**STEP)
    second_hat = second_new / (1.0 - BETA_TWO**STEP)
    weight_new = weight - rate * (first_hat / (jnp.sqrt(second_hat) + EPS_ADAM) + DECAY * weight)
    return (first_new, second_new, weight_new)


def segment_of(places, seg_ends):
    return jnp.sum((places[None, :, None] >= seg_ends[:, None, :]).astype(jnp.int32), -1)


def row_facts(seg_lengths, class_labels, length):
    seg_ids = segment_of(jnp.arange(length, dtype=jnp.int32), jnp.cumsum(seg_lengths, 1))
    picked = seg_ids[:, :, None] == jnp.arange(SEGS)[None, None, :]
    return seg_ids, jnp.sum(jnp.where(picked, class_labels[:, None, :], 0), -1)


def pack_kernel(sizes, w_table, w_in, w_out, gains, side):
    classes, channels, out, gain_count = sizes
    table, last, _ = side_columns(*sizes)
    shard = w_out.shape[1]
    down = lax.broadcasted_iota(jnp.int32, (shard, shard), 0)
    same = (down == lane_of((shard, shard))).astype(jnp.bfloat16)
    side[...] = jnp.zeros_like(side)
    for b in range(2):

        def across(part):
            return by_rows(same, part.astype(jnp.bfloat16)).astype(jnp.bfloat16)

        side[b, :, :classes] = w_table[b].astype(jnp.bfloat16)
        side[b, :, table : table + channels] = across(w_in[b])
        side[b, :, last : last + out] = w_out[b].astype(jnp.bfloat16)
        side[b, :, last + out : last + out + gain_count] = across(gains[:, b])


def packed_side(w_table, w_in, w_out, gains, sizes):
    shape = (2, w_out.shape[1], side_columns(*sizes)[2])
    return pl.pallas_call(
        functools.partial(pack_kernel, sizes),
        out_shape=jax.ShapeDtypeStruct(shape, jnp.bfloat16),
        compiler_params=pltpu.CompilerParams(vmem_limit_bytes=32 * 2**20),
        name="pack_side",
    )(jnp.swapaxes(w_table, 1, 2), w_in, w_out, jnp.swapaxes(gains, 0, 1))


def small_updates_kernel(sizes, side, *refs):
    classes, channels, out, gain_count = sizes
    table, last, _ = side_columns(*sizes)
    args, outs = refs[:12], refs[12:]
    shard = side.shape[1]
    down = lax.broadcasted_iota(jnp.int32, (shard, shard), 0)
    same = (down == lane_of((shard, shard))).astype(jnp.bfloat16)
    for b in range(2):

        def across(begin, end):
            return down_columns(side[b, :, begin:end], same)

        tail = across(last, last + LANES)
        grads = (
            across(table, table + LANES)[:channels],
            side[b, :, :classes].astype(jnp.float32),
            side[b, :, last : last + LANES].astype(jnp.float32)[:, :out],
            tail[out : out + gain_count],
        )
        rates = (RATES[0], RATES[1], RATES[6], RATES[7])
        for i in range(4):
            at = (slice(None), b) if i == 3 else (b,)
            now = [ref[at] for ref in args[3 * i : 3 * i + 3]]
            for ref, value in zip(outs[3 * i : 3 * i + 3], adam_step(*now, grads[i], rates[i])):
                ref[at] = value


def small_updates(side, groups, sizes):
    turns = ((0, 0), (1, 2), (0, 0), (0, 1))
    arrays = [jnp.swapaxes(part, *turn) for turn, group in zip(turns, groups) for part in group]
    results = pl.pallas_call(
        functools.partial(small_updates_kernel, sizes),
        out_shape=[jax.ShapeDtypeStruct(part.shape, part.dtype) for part in arrays],
        compiler_params=pltpu.CompilerParams(vmem_limit_bytes=48 * 2**20),
        name="small_updates",
    )(side, *arrays)
    return [jnp.swapaxes(part, *turns[i // 3]) for i, part in enumerate(results)]


def staged(patches, seg_lengths, class_labels, cotangent, low, sizes):
    half = lax.axis_size("rows") // 2
    second = lax.axis_index("rows") >= half
    x = lax.axis_index("seq")
    swap = [(i, (i + half) % (2 * half)) for i in range(2 * half)]
    beside = [(0, 1), (1, 0)]
    both = ("rows", "seq")
    across = [(2 * i + s, 2 * j + 1 - s) for i, j in swap for s in range(2)]
    classes, channels, out, gain_count = sizes
    table, last, _ = side_columns(*sizes)
    held, group, _ = patches.shape
    rows, length = held // 2, 2 * group

    pieces = jnp.concatenate([patches.astype(jnp.float32), cotangent], 2)
    pieces = jnp.pad(pieces, ((0, 0), (0, 0), (0, LANES - 2 * channels)))
    pieces = pieces.reshape(2, rows, group, LANES)
    keep = lax.dynamic_index_in_dim(pieces, x, 0, keepdims=False)
    give = lax.dynamic_index_in_dim(pieces, 1 - x, 0, keepdims=False)
    got = lax.ppermute(give, "seq", beside)
    mine = jnp.where(
        x == 0, jnp.concatenate([keep, got], 1), jnp.concatenate([got, keep], 1)
    ).reshape(TOKENS, LANES)
    theirs = lax.ppermute(mine, "rows", swap)
    facts = jnp.concatenate(
        [jnp.cumsum(seg_lengths, 1), class_labels, jnp.full((held, 1), length, jnp.int32)], 1
    )
    facts = lax.dynamic_slice_in_dim(facts, x * rows, rows, 0)
    their_facts = lax.ppermute(facts, "rows", swap)
    facts = jnp.where(
        second, jnp.stack([their_facts, facts], 0), jnp.stack([facts, their_facts], 0)
    )
    batches = jnp.where(second, jnp.stack([theirs, mine], 0), jnp.stack([mine, theirs], 0))
    batches, facts, low = lax.optimization_barrier((batches, facts, low))
    lane = jnp.arange(LANES) < channels
    inputs = jnp.where(lane, batches, 0.0)
    cotangent = jnp.where(lane, jnp.roll(batches, -channels, 2), 0.0)
    (latents, grad_inputs, gain_grads), pairs = two_blocks(
        facts, inputs, cotangent, low, table, channels, 1
    )

    def halves(part):
        part = part.reshape(rows, 2, group, LANES)
        ours = lax.dynamic_index_in_dim(part, x, 1, keepdims=False)
        return ours, lax.dynamic_index_in_dim(part, 1 - x, 1, keepdims=False)

    def in_order(ours, beside_us):
        return jnp.where(
            x == 0, jnp.concatenate([ours, beside_us], 0), jnp.concatenate([beside_us, ours], 0)
        )

    own = halves(jnp.where(second, latents[2], grad_inputs[2]))
    away = halves(jnp.where(second, latents[1], grad_inputs[1]))
    own_side = lax.ppermute(own[1], "seq", beside)
    away_here = lax.ppermute(away[0], "rows", swap)
    away_side = lax.ppermute(away[1], both, across)
    sums = summed_products(pairs, gain_grads, out, low, 2)
    ours, others = in_order(own[0], own_side), in_order(away_here, away_side)
    outcome = jnp.where(second, ours, others)
    patch_grad = jnp.where(second, others, ours)
    return outcome[..., :channels], outcome[..., channels], patch_grad[..., :channels], sums


def unstaged(mine, low, sizes):
    inputs, cotangent, seg_ids, labels = mine
    whole = [lax.all_gather(part, "rows", axis=1, tiled=True) for part in low]

    def block(index):
        picked = [part[index * LAYERS : (index + 1) * LAYERS] for part in whole[:4]]
        return picked + [whole[4][index]]

    back = seg_ids[:, ::-1], labels[:, ::-1]
    latent_one, det_one, saved_one = forward_block(inputs, seg_ids, labels, block(0), sizes)
    latent_two, det_two, saved_two = forward_block(latent_one[:, ::-1], *back, block(1), sizes)
    outcome = jnp.concatenate([latent_two, (det_two + det_one[:, ::-1])[..., None]], 2)
    grad_mid, parts_two = backward_block(cotangent, saved_two, block(1), sizes)
    patch_grad, parts_one = backward_block(grad_mid[:, ::-1], saved_one, block(0), sizes)
    grads = [
        jnp.concatenate(pair, 0)
        for pair in zip(
            weight_grads(parts_one, low[4].shape[2]), weight_grads(parts_two, low[4].shape[2])
        )
    ]
    sums = [
        lax.psum(
            lax.psum_scatter(grad, "rows", scatter_dimension=1, tiled=True).astype(jnp.float32),
            "seq",
        )
        for grad in grads
    ]
    return outcome, patch_grad, sums


def body(
    patches,
    seg_lengths,
    class_labels,
    cotangent,
    w_in,
    m_in,
    v_in,
    w_table,
    m_table,
    v_table,
    w_qkv,
    m_qkv,
    v_qkv,
    w_o,
    m_o,
    v_o,
    w_up,
    m_up,
    v_up,
    w_down,
    m_down,
    v_down,
    w_out,
    m_out,
    v_out,
    gains,
    m_gains,
    v_gains,
):
    masters = (w_in, w_table, w_qkv, w_o, w_up, w_down, w_out, gains)
    firsts = (m_in, m_table, m_qkv, m_o, m_up, m_down, m_out, m_gains)
    seconds = (v_in, v_table, v_qkv, v_o, v_up, v_down, v_out, v_gains)
    sizes = (w_table.shape[1], w_in.shape[1], w_out.shape[2], gains.shape[1])
    shards = [weight.astype(jnp.bfloat16) for weight in masters[2:6]]
    held, group, channels = patches.shape
    seq_count = lax.axis_size("seq")
    length = group * seq_count
    groups = list(zip(masters, firsts, seconds))
    fits = held == 4 and group * held == TOKENS and sizes[2] == 2 * channels and sizes[2] % 8 == 0
    if seq_count == 2 and lax.axis_size("rows") == 16 and fits:
        shards.append(packed_side(w_table, w_in, w_out, gains, sizes))
        latents, logdet, patch_grad, sums = staged(
            patches, seg_lengths, class_labels, cotangent, shards, sizes
        )
        small = small_updates(sums[4], [groups[i] for i in (0, 1, 6, 7)], sizes)
        updates = [None] * 8
        for i, where_at in enumerate((0, 1, 6, 7)):
            updates[where_at] = small[3 * i : 3 * i + 3]
        for i, where_at in enumerate((2, 3, 4, 5)):
            updates[where_at] = adam_step(
                *groups[where_at], sums[i].astype(jnp.float32), RATES[where_at]
            )
        results = (latents, logdet, patch_grad)
    else:
        small = [masters[i].astype(jnp.bfloat16) for i in (1, 0, 6, 7)]
        shards.append(pack_side(*small))
        share = max(1, held // seq_count)
        copies = seq_count * share // held
        first_row = (lax.axis_index("seq") // copies) * share
        pieces = jnp.concatenate([patches.astype(jnp.float32), cotangent], 2)
        pieces = lax.all_gather(pieces, "seq", axis=1, tiled=True)
        pieces = lax.dynamic_slice_in_dim(pieces, first_row, share, 0)
        seg_ids, labels = row_facts(
            lax.dynamic_slice_in_dim(seg_lengths, first_row, share, 0),
            lax.dynamic_slice_in_dim(class_labels, first_row, share, 0),
            length,
        )
        mine = (pieces[..., :channels], pieces[..., channels:], seg_ids, labels)
        outcome, patch_grad, sums = unstaged(mine, shards, sizes)
        results = lax.all_gather(jnp.concatenate([outcome, patch_grad], 2), "seq", axis=0)
        results = results[::copies].reshape((held,) + results.shape[2:])
        results = lax.dynamic_slice_in_dim(results, lax.axis_index("seq") * group, group, 1)
        results = (
            results[..., :channels],
            results[..., channels],
            results[..., channels + 1 :],
        )
        sums = [total.astype(jnp.float32) / copies for total in sums]
        table, first, last, gain = split_side(sums[4], *sizes)
        grads = (first, table, sums[0], sums[1], sums[2], sums[3], last, gain)
        updates = [adam_step(*item) for item in zip(masters, firsts, seconds, grads, RATES)]
    return results + tuple(part for update in updates for part in update)


def solution(mesh):
    tokens = P("rows", "seq", None)
    row = P("rows", None)
    last, middle = P(None, None, "rows"), P(None, "rows", None)
    weights = (last,) * 6 + (middle,) * 15 + (last,) * 3
    return jax.shard_map(
        body,
        mesh=mesh,
        in_specs=(tokens, row, row, tokens) + weights,
        out_specs=(tokens, P("rows", "seq"), tokens) + weights,
        check_vma=False,
    )
```

```python
import functools
from functools import partial

import jax
import jax.numpy as jnp
from jax import lax
from jax.experimental import pallas as pl
from jax.experimental.pallas import tpu as pltpu
from jax.sharding import PartitionSpec as P

HEADS = 12
HEAD_DIM = 64
LAYERS = 2
SEGS = 4
STEP = 10

EPS_NORM = 1e-05
MASKED = -1000000000.0
BETA_ONE = 0.9
BETA_TWO = 0.95
EPS_ADAM = 1e-08
DECAY = 0.1
RATES = (0.05, 0.3, 0.02, 0.05, 0.02, 0.01, 0.01, 0.3)

MESH_ID = pl.DeviceIdType.MESH
LANES = 128
LATE = (0, 1, 2)
GATHER_LAGS = (1.5, 3.5, 5.5, 8.5, 0.0, 1.0, 1.7, 3.0)


def place():
    r = lax.axis_index("rows")
    x = lax.axis_index("seq")
    c = lax.rem(r, 2)
    y = lax.rem(r // 2, 2)
    z = r // 4
    return r, x, y, z, c


def units_of(shards, d1_share):
    units = []
    order = sorted(range(len(shards)), key=lambda a: shards[a].shape[0])
    layers = max(s.shape[0] // 2 for s in shards)
    todo = [(a, 0) for a in order if shards[a].shape[0] == 2]
    for l in range(layers):
        todo += [(a, l) for a in order if shards[a].shape[0] > 2]
    for a, l in todo:
        n, rows, cols = shards[a].shape
        half = cols // 2
        if rows >= 64:
            first = max(16, round(rows * d1_share / 16) * 16)
            split = (0, first)
        else:
            first = max(LANES, round(half * d1_share / LANES) * LANES)
            split = (1, first)
        units.append((a, l, n // 2, rows, half, split))
    return units


def wait_all_of(cell, sem):
    pltpu.make_async_copy(cell, cell, sem).wait()


def gathering(units, late, lags, srcs, outs, send, recv, local):
    r, x, y, z, c = place()
    stage = z // 2
    other = 1 - stage
    zi = lax.rem(z, 2)
    dev_x = (r, 1 - x)
    dev_y = (r + 2 - 4 * y, x)
    dev_s = (r + 1 - 2 * c, x)
    z_near = z + 1 - 2 * zi
    z_src = (z_near, other * 2, other * 2 + 1)
    dev_z = tuple((zz * 4 + y * 2 + c, x) for zz in z_src)
    barrier = pltpu.get_barrier_semaphore()
    partners = (dev_x, dev_y, dev_s) + dev_z
    for dev in partners:
        pl.semaphore_signal(barrier, 1, device_id=dev, device_id_type=MESH_ID)
    pl.semaphore_wait(barrier, len(partners))

    inner = stage != zi
    dev_inner = ((1 + other) * 4 + y * 2 + c, x)
    side_of = jnp.where(inner, other, stage)
    z_mine, z_theirs = 2 * side_of, 2 - 2 * side_of
    started = []

    def alike(src):
        what = src.args + (None,) * 3
        if src.func is own_ref:
            return own(what[0], stage, None if what[2] is None else x)
        return cell(what[0], z, y, c, None if what[4] is None else x, what[5])

    def cell(*what):
        return functools.partial(cell_ref, *what)

    def own(*what):
        return functools.partial(own_ref, *what)

    def cell_ref(u, zz, yy, cc, h=None, part=None):
        a, l, _, rows, half, (dim, first) = units[u]
        row0, nrow = (zz * 4 + yy * 2 + cc) * rows, rows
        col0, ncol = (0, 2 * half) if h is None else (h * half, half)
        if part is not None:
            if dim == 0:
                row0, nrow = (row0, first) if part == 0 else (row0 + first, rows - first)
            else:
                col0, ncol = (col0, first) if part == 0 else (col0 + first, half - first)
        if h is not None:
            col0 = pl.multiple_of(col0, LANES)
        block = outs[a] if len(outs[a].shape) == 2 else outs[a].at[l]
        return block.at[pl.ds(pl.multiple_of(row0, 16), nrow), pl.ds(col0, ncol)]

    def own_ref(u, b, h=None):
        a, l, layers, rows, half, _ = units[u]
        if h is None:
            return srcs[a].at[layers * b + l]
        return srcs[a].at[layers * b + l, :, pl.ds(pl.multiple_of(h * half, LANES), half)]

    def push(u, src, dst, idx, dev, slot=None):
        slot = idx if slot is None else slot
        pltpu.make_async_remote_copy(
            src_ref=src(),
            dst_ref=dst(),
            send_sem=send.at[u, slot],
            recv_sem=recv.at[u, idx],
            device_id=dev,
            device_id_type=MESH_ID,
        ).start()
        started.append((u, slot, alike(src)))

    def arrived(u, dst, idx):
        wait_all_of(dst(), recv.at[u, idx])

    def relay_copy(u, piece, j):
        return pltpu.make_async_remote_copy(
            src_ref=piece(),
            dst_ref=piece(),
            send_sem=send.at[u, 24 + j],
            recv_sem=recv.at[u, j],
            device_id=dev_z[0],
            device_id_type=MESH_ID,
        )

    def relay(u, piece, j):
        @pl.when(inner)
        def _():
            relay_copy(u, piece, j).start()

    def begin(u):
        mine = cell(u, z, y, c, x)
        push(u, own(u, other, x), mine, 1 + zi, dev_inner, slot=1)
        if u in late:

            @pl.when(inner)
            def _():
                near_copy(u).start()

            @pl.when(jnp.logical_not(inner))
            def _():
                own_copy(u).start()

            return
        push(u, own(u, stage, x), mine, 0, dev_z[0])
        push(u, own(u, stage, x), mine, 10, dev_y)
        push(u, own(u, stage), cell(u, z, y, c), 17, dev_s)
        pltpu.make_async_copy(own(u, stage)(), cell(u, z, y, c)(), local.at[u]).start()

    def near_copy(u):
        return pltpu.make_async_remote_copy(
            src_ref=own(u, stage, x)(),
            dst_ref=cell(u, z, y, c, x)(),
            send_sem=send.at[u, 0],
            recv_sem=recv.at[u, 1 + zi],
            device_id=dev_z[0],
            device_id_type=MESH_ID,
        )

    def own_copy(u):
        return pltpu.make_async_copy(own(u, stage, x)(), cell(u, z, y, c, x)(), recv.at[u, 1 + zi])

    def near(u):
        if u in late:
            return
        arrived(u, cell(u, z, 1 - y, c, x), 10)
        push(u, cell(u, z, 1 - y, c, x), cell(u, z, 1 - y, c, x), 6, dev_x)
        side(u, 0, z_src[0], 0)

    def side(u, j, zz, idx):
        piece = cell(u, zz, y, c, x)
        arrived(u, piece, idx)
        if u not in late and j > 0:
            relay(u, piece, j)
        push(u, piece, piece, 3 + j, dev_x)
        push(u, piece, piece, 7 + j, dev_y)

    def spread(u):
        if u in late:
            for j in range(2):
                side(u, j, z_mine + j, 1 + j)
        else:
            for j in (1, 2):
                side(u, j, z_src[j], j)

    def turn(u, j, zz):
        arrived(u, cell(u, zz, y, c, 1 - x), 3 + j)
        part = cell(u, zz, y, c, 1 - x, 0)
        push(u, part, part, 11 + j, dev_y)
        arrived(u, cell(u, zz, 1 - y, c, x), 7 + j)
        part = cell(u, zz, 1 - y, c, x, 1)
        push(u, part, part, 14 + j, dev_x)

    def near_corner(u):
        if u not in late:
            turn(u, 0, z_src[0])
            slab = cell(u, z_src[0], y, c)
            push(u, slab, slab, 19, dev_s)

    def corner(u):
        if u in late:
            for j in range(2):
                turn(u, j, z_mine + j)
        else:
            for j in (1, 2):
                turn(u, j, z_src[j])
                slab = cell(u, z_src[j], y, c)
                push(u, slab, slab, 19 + j, dev_s)

    def corners_in(u, j, zz):
        arrived(u, cell(u, zz, 1 - y, c, 1 - x, 0), 11 + j)
        arrived(u, cell(u, zz, 1 - y, c, 1 - x, 1), 14 + j)

    def finish(u):
        if u in late:
            for j in range(2):
                corners_in(u, j, z_mine + j)
                for yy in range(2):
                    slab = cell(u, z_mine + j, yy, c)
                    push(u, slab, slab, (0, 5, 6, 9)[2 * j + yy], dev_z[0], slot=(2, 5, 6, 9)[2 * j + yy])
                    push(u, slab, slab, 17 + 2 * j + yy, dev_s)
            return
        arrived(u, cell(u, z, 1 - y, c, 1 - x), 6)
        slab = cell(u, z, 1 - y, c)
        push(u, slab, slab, 18, dev_s)
        for j in range(3):
            corners_in(u, j, z_src[j])
            slab = cell(u, z_src[j], 1 - y, c)
            push(u, slab, slab, 22 + j, dev_s)

    def last(u):
        if u in late:
            for j in range(2):
                for yy in range(2):
                    slab = cell(u, z_theirs + j, yy, c)
                    arrived(u, slab, (0, 5, 6, 9)[2 * j + yy])
                    push(u, slab, slab, 21 + 2 * j + yy, dev_s)

    n = len(units)
    order = sorted(range(n), key=lambda u: u not in late)
    events = [(1.0 * i - lags[7], begin, u) for i, u in enumerate(order)]
    events += [(lags[0] + 1.0 * i, spread, u) for i, u in enumerate(order)]
    events += [(lags[1] + 1.0 * i, corner, u) for i, u in enumerate(order)]
    events += [(lags[2] + 1.0 * i, finish, u) for i, u in enumerate(order)]
    events += [(lags[3] + 1.0 * i, last, u) for i, u in enumerate(order)]
    events += [(lags[4] + lags[5] * i, near, u) for i, u in enumerate(order)]
    events += [(lags[6] + 1.0 * i, near_corner, u) for i, u in enumerate(order)]
    events.sort(key=lambda event: event[0])

    def ready(u):
        while any(event[2] == u for event in events):
            _, act, unit = events.pop(0)
            act(unit)
        if u in late:
            for j in range(2):
                for yy in range(2):
                    arrived(u, cell(u, z_mine + j, yy, 1 - c), 17 + 2 * j + yy)
                    arrived(u, cell(u, z_theirs + j, yy, 1 - c), 21 + 2 * j + yy)
            return
        arrived(u, cell(u, z, y, 1 - c), 17)
        arrived(u, cell(u, z, 1 - y, 1 - c), 18)
        for j in range(3):
            arrived(u, cell(u, z_src[j], y, 1 - c), 19 + j)
            arrived(u, cell(u, z_src[j], 1 - y, 1 - c), 22 + j)
        pltpu.make_async_copy(own(u, stage)(), cell(u, z, y, c)(), local.at[u]).wait()

    def done():
        for u in range(n):
            if u in late:

                @pl.when(inner)
                def _():
                    near_copy(u).wait_send()

            else:

                @pl.when(inner)
                def _():
                    for j in (1, 2):
                        relay_copy(u, cell(u, z_src[j], y, c, x), j).wait_send()

        for u, slot, place_of in started:
            wait_all_of(place_of(), send.at[u, slot])

    return ready, done


TOKENS = 256
HALF_LANES = 64
FORWARD_VMEM = 58 * 2**20


def lane_of(shape):
    return lax.broadcasted_iota(jnp.int32, shape, len(shape) - 1)


def norm_rows(hidden):
    center = hidden - jnp.mean(hidden, -1, keepdims=True)
    inverse = lax.rsqrt(jnp.mean(center * center, -1, keepdims=True) + EPS_NORM)
    return center * inverse, inverse


def gelu_and_slope(v):
    root = 0.7978845608028654
    square = v * v
    wave = jnp.tanh(root * (v + 0.044715 * (square * v)))
    near = 0.5 * (1.0 + wave)
    slope = near + (0.5 * root) * v * (1.0 - wave * wave) * (1.0 + (3 * 0.044715) * square)
    return v * near, slope


def turned_round(part):
    length = part.shape[0]
    down = lax.broadcasted_iota(jnp.int32, (length, length), 0)
    flip = (down + lane_of((length, length)) == length - 1).astype(jnp.bfloat16)
    total = None
    for _ in range(3):
        high = part.astype(jnp.bfloat16)
        part = part - high.astype(jnp.float32)
        moved = jnp.dot(flip, high, preferred_element_type=jnp.float32)
        total = moved if total is None else total + moved
    return total


def packed_pair(part, length):
    lane = lane_of((length, LANES))
    return jnp.where(lane < HALF_LANES, part[:length], pltpu.roll(part[length:], HALF_LANES, 1))


def unpacked(part, row):
    lane = lane_of(part.shape)
    part = part if row == 0 else pltpu.roll(part, HALF_LANES, 1)
    return jnp.where(lane < HALF_LANES, part, 0.0)


def facts_of(facts, batch, second, row, places):
    at = jnp.where(second, facts[batch, row, 8] - 1 - places, places)
    segment = jnp.zeros(places.shape, jnp.int32)
    for k in range(SEGS):
        segment = segment + (at >= facts[batch, row, k]).astype(jnp.int32)
    label = jnp.zeros(places.shape, jnp.int32)
    for k in range(SEGS):
        label = jnp.where(segment == k, facts[batch, row, SEGS + k], label)
    return segment, label


def columns_of(facts, batch, second, rows, length):
    parts = []
    for row in range(rows):
        places = lax.broadcasted_iota(jnp.int32, (length, LANES), 0)
        segment, label = facts_of(facts, batch, second, row, places)
        before, _ = facts_of(facts, batch, second, row, places - 1)
        parts.append((segment, label, (places >= 1) & (segment == before)))
    return [
        jnp.concatenate([part[i].astype(jnp.int32) for part in parts], 0)[:, :1] for i in range(3)
    ]


def gain_rows_of(w_side, last, out, count):
    return w_side[:, last:].astype(jnp.float32).T[out : out + count]


def both_heads(pair, first):
    zero = jnp.zeros_like(pair)
    return jnp.concatenate([jnp.where(first, pair, zero), jnp.where(first, zero, pair)], 0)


def norm_rows_back(normed, inverse, grad_normed):
    mean_grad = jnp.mean(grad_normed, -1, keepdims=True)
    mean_proj = jnp.mean(grad_normed * normed, -1, keepdims=True)
    return inverse * (grad_normed - mean_grad - normed * mean_proj)


def by_rows(left, right):
    return lax.dot_general(
        left, right, (((1,), (1,)), ((), ())), preferred_element_type=jnp.float32
    )


def down_columns(left, right):
    return lax.dot_general(
        left, right, (((0,), (0,)), ((), ())), preferred_element_type=jnp.float32
    )


def blocks_kernel(
    sizes,
    units,
    facts,
    patches,
    cotangent,
    low_qkv,
    low_o,
    low_up,
    low_down,
    low_side,
    out_latent,
    out_grad,
    out_gains,
    hbm_na,
    hbm_aa,
    hbm_q,
    hbm_p,
    hbm_ctx,
    hbm_nm,
    hbm_am,
    hbm_slope,
    hbm_gelu,
    hbm_stat,
    hbm_nf,
    hbm_af,
    hbm_tail,
    hbm_start,
    hbm_gqkv,
    hbm_gmid,
    hbm_gup,
    hbm_gbr,
    hbm_gstart,
    hbm_gpred,
    w_qkv,
    w_o,
    w_up,
    w_down,
    w_side,
    na,
    aa,
    qkv,
    prob,
    ctx,
    nm,
    am,
    slope,
    gelu,
    stat,
    nf,
    af,
    tail,
    start,
    gqkv,
    gmid,
    gup,
    gbr,
    gstart,
    gpred,
    hidden,
    inputs,
    gain_rows,
    gact,
    gctx,
    sent,
    received,
    gather_send,
    gather_recv,
    gather_local,
    save_sem,
    last_sem,
    load_sem,
    once_sem,
    grad_sem,
    end_sem,
    send_sem,
    recv_sem,
):
    rows, length, table, channels = sizes
    layers, width = w_qkv.shape[0], w_qkv.shape[1]
    pairs = width // LANES
    half = lax.axis_size("rows") // 2
    me = lax.axis_index("rows")
    second = me >= half
    partner = (jnp.where(second, me - half, me + half), lax.axis_index("seq"))
    ready, done = gathering(
        units,
        LATE,
        GATHER_LAGS,
        (low_qkv, low_o, low_up, low_down, low_side),
        (w_qkv, w_o, w_up, w_down, w_side),
        gather_send,
        gather_recv,
        gather_local,
    )
    unit_of = {(unit[0], unit[1]): i for i, unit in enumerate(units)}

    def hop(slot):
        return pltpu.make_async_remote_copy(
            src_ref=sent.at[slot],
            dst_ref=received.at[slot],
            send_sem=send_sem.at[slot],
            recv_sem=recv_sem.at[slot],
            device_id=partner,
            device_id_type=MESH_ID,
        )

    lane = lane_of((TOKENS, LANES))

    layered = (
        (na, hbm_na),
        (aa, hbm_aa),
        (qkv, hbm_q),
        (prob, hbm_p),
        (ctx, hbm_ctx),
        (nm, hbm_nm),
        (am, hbm_am),
        (slope, hbm_slope),
        (gelu, hbm_gelu),
        (stat, hbm_stat),
    )
    single = ((nf, hbm_nf), (af, hbm_af), (tail, hbm_tail), (start, hbm_start))

    @pl.loop(0, 3)
    def _(step):
        batch = jnp.where(second, jnp.maximum(step - 1, 0), jnp.minimum(step, 1))

        def saving(layer, i):
            src, dst = layered[i]
            src = src if i == 7 else src.at[layer]
            return pltpu.make_async_copy(src, dst.at[step, layer], save_sem.at[layer, i])

        def whole(array, layer):
            @pl.when(step == 0)
            def _():
                ready(unit_of[array, layer])

        whole(4, 0)

        @pl.when(step == 0)
        def _():
            gain_rows[...] = gain_rows_of(w_side, table + LANES, 2 * channels, 8)

        for slot in range(2):

            @pl.when(step == slot + 1)
            def _():
                hop(slot).wait_recv()

        for row in range(rows):
            toks = pl.ds(row * length, length)

            @pl.when(jnp.logical_not(second))
            def _():
                inputs[toks, :] = patches[batch, toks, :]

            @pl.when(second & (step > 0))
            def _():
                before = received[jnp.maximum(step - 1, 0)]
                inputs[toks, :] = turned_round(unpacked(before, row))

            @pl.when(second & (step == 0))
            def _():
                inputs[toks, :] = jnp.zeros((length, LANES), jnp.float32)

        seg_col, labels, same = columns_of(facts, batch, second, rows, length)
        start[:, :table] = (labels == lane_of((TOKENS, table))).astype(jnp.bfloat16)
        start[:, table:] = inputs[...].astype(jnp.bfloat16)
        hidden[...] = by_rows(start[...], w_side[:, : table + LANES])
        for layer in range(layers):
            normed, inverse_a = norm_rows(hidden[...])
            na[layer] = normed
            saving(layer, 0).start()
            aa[layer] = (normed * gain_rows[2 * layer : 2 * layer + 1, :]).astype(jnp.bfloat16)
            saving(layer, 1).start()
            whole(0, layer)

            @pl.loop(0, 3)
            def _(i):
                cols = pl.ds(pl.multiple_of(i * width, LANES), width)
                qkv[layer, :, cols] = jnp.dot(
                    aa[layer], w_qkv[layer, :, cols], preferred_element_type=jnp.float32
                ).astype(jnp.bfloat16)

            saving(layer, 2).start()
            for row in range(rows):
                toks = pl.ds(row * length, length)
                causal = lax.broadcasted_iota(jnp.int32, (length, length), 0) >= lane_of(
                    (length, length)
                )
                places = lax.broadcasted_iota(jnp.int32, (8, length), 1)
                seg_row = facts_of(facts, batch, second, row, places)[0][:1]
                attend = (seg_col[row * length : (row + 1) * length] == seg_row) & causal
                attend = jnp.concatenate([attend.astype(jnp.float32)] * 2, 0) > 0.5
                first = lane_of((length, LANES)) < HALF_LANES
                for pair in range(pairs):

                    def part(i):
                        return qkv[layer, toks, pl.ds(i * width + pair * LANES, LANES)]

                    scores = by_rows(both_heads(part(0), first), part(1)) * HEAD_DIM ** (-0.5)
                    scores = jnp.where(attend, scores, MASKED)
                    expo = jnp.exp(scores - jnp.max(scores, -1, keepdims=True))
                    soft = expo / jnp.sum(expo, -1, keepdims=True)
                    prob[layer, row * pairs + pair] = soft
                    mixed = jnp.dot(
                        soft.astype(jnp.bfloat16), part(2), preferred_element_type=jnp.float32
                    )
                    ctx[layer, toks, pl.ds(pair * LANES, LANES)] = jnp.where(
                        first, mixed[:length], mixed[length:]
                    ).astype(jnp.bfloat16)

            saving(layer, 3).start()
            saving(layer, 4).start()
            whole(1, layer)
            hidden[...] = hidden[...] + jnp.dot(
                ctx[layer], w_o[layer], preferred_element_type=jnp.float32
            )
            normed, inverse_m = norm_rows(hidden[...])
            nm[layer] = normed
            saving(layer, 5).start()
            am[layer] = (normed * gain_rows[2 * layer + 1 : 2 * layer + 2, :]).astype(jnp.bfloat16)
            saving(layer, 6).start()
            stat[layer] = jnp.where(lane == 0, inverse_a, inverse_m)
            saving(layer, 9).start()
            whole(2, layer)
            if layer > 0:
                saving(layer - 1, 7).wait()

            wide = 2 * width

            @pl.loop(0, w_up.shape[2] // wide)
            def _(i):
                cols = pl.ds(pl.multiple_of(i * wide, LANES), wide)
                upper = jnp.dot(am[layer], w_up[layer, :, cols], preferred_element_type=jnp.float32)
                value, rate = gelu_and_slope(upper)
                gelu[layer, :, cols] = value.astype(jnp.bfloat16)
                slope[:, cols] = rate

            saving(layer, 7).start()
            saving(layer, 8).start()
            whole(3, layer)
            hidden[...] = hidden[...] + jnp.dot(
                gelu[layer], w_down[layer], preferred_element_type=jnp.float32
            )

        normed, inverse_f = norm_rows(hidden[...])
        nf[...] = normed
        af[...] = (normed * gain_rows[2 * layers : 2 * layers + 1, :]).astype(jnp.bfloat16)
        prediction = jnp.dot(
            af[...], w_side[:, table + LANES :], preferred_element_type=jnp.float32
        )
        previous = pltpu.roll(prediction, 1, 0)
        shown = (same > 0) & (lane < channels)
        shift_alpha = jnp.where(shown, pltpu.roll(previous, LANES - channels, 1), 0.0)
        shift_mu = jnp.where(shown, previous, 0.0)
        latent = (inputs[...] - shift_mu) * jnp.exp(-shift_alpha)
        logdet = -jnp.sum(shift_alpha, -1, keepdims=True)
        result = jnp.where(lane == channels, logdet + inputs[...], latent)
        out_latent[step] = result
        for slot in range(2):

            @pl.when(step == slot)
            def _():
                sent[slot] = packed_pair(result, length)
                hop(slot).start()

        tail[0] = latent
        tail[1] = shift_alpha
        tail[2] = jnp.broadcast_to(inverse_f, (TOKENS, LANES))
        for i, (src, dst) in enumerate(single):
            pltpu.make_async_copy(src, dst.at[step], last_sem.at[i]).start()
        for layer in range(layers):
            for i in range(len(layered)):
                if i != 7 or layer == layers - 1:
                    saving(layer, i).wait()
        for i, (src, dst) in enumerate(single):
            pltpu.make_async_copy(src, dst.at[step], last_sem.at[i]).wait()

    back = ((nm, hbm_nm), (prob, hbm_p), (qkv, hbm_q), (na, hbm_na), (stat, hbm_stat))
    once = ((tail, hbm_tail), (nf, hbm_nf))
    order = list(reversed(range(layers)))

    @pl.loop(0, 3)
    def _(turn):
        batch = jnp.where(second, jnp.maximum(1 - turn, 0), jnp.minimum(2 - turn, 1))
        slot_of = 2 - turn

        def fetch(layer, i, step):
            src, dst = back[i][1], back[i][0]
            return pltpu.make_async_copy(src.at[step, layer], dst.at[layer], load_sem.at[layer, i])

        def fetch_slope(layer, step):
            return pltpu.make_async_copy(hbm_slope.at[step, layer], slope, load_sem.at[layer, 5])

        def fetch_once(i, step):
            return pltpu.make_async_copy(once[i][1].at[step], once[i][0], once_sem.at[i])

        def refill(copy_of):
            @pl.when(turn < 2)
            def _():
                copy_of(jnp.maximum(slot_of - 1, 0)).start()

        def await_load(copy_of):
            @pl.when(turn > 0)
            def _():
                copy_of(slot_of).wait()

        def saving(layer, i):
            src, dst = ((gqkv, hbm_gqkv), (gmid, hbm_gmid), (gup, hbm_gup), (gbr, hbm_gbr))[i]
            src = src if i == 2 else src.at[layer]
            return pltpu.make_async_copy(src, dst.at[slot_of, layer], grad_sem.at[layer, i])

        for slot in (2, 3):

            @pl.when(turn == slot - 1)
            def _():
                hop(slot).wait_recv()

        for row in range(rows):
            toks = pl.ds(row * length, length)

            @pl.when(second)
            def _():
                inputs[toks, :] = cotangent[batch, toks, :]

            @pl.when(jnp.logical_not(second) & (turn > 0))
            def _():
                before = received[jnp.maximum(turn, 1) + 1]
                inputs[toks, :] = turned_round(unpacked(before, row))

            @pl.when(jnp.logical_not(second) & (turn == 0))
            def _():
                inputs[toks, :] = jnp.zeros((length, LANES), jnp.float32)

        same = columns_of(facts, batch, second, rows, length)[2]
        await_load(functools.partial(fetch_once, 0))
        await_load(functools.partial(fetch_once, 1))
        scaled = inputs[...] * jnp.exp(-tail[1])
        grad_alpha = 1.0 - inputs[...] * tail[0]
        grad_prev = jnp.where(lane < channels, -scaled, pltpu.roll(grad_alpha, channels, 1))
        grad_prev = jnp.where((same > 0) & (lane < 2 * channels), grad_prev, 0.0)
        gpred[...] = pltpu.roll(grad_prev, TOKENS - 1, 0).astype(jnp.bfloat16)
        gact[...] = by_rows(gpred[...], w_side[:, table + LANES :])
        out_gains[turn] = jnp.zeros((8, width), jnp.float32)

        def through_norm(normed, inverse, index):
            grad = gact[...]
            out_gains[turn, index : index + 1, :] = jnp.sum(grad * normed, 0, keepdims=True)
            return norm_rows_back(normed, inverse, grad * gain_rows[index : index + 1, :])

        hidden[...] = through_norm(nf[...], tail[2][:, :1], 2 * layers)
        refill(functools.partial(fetch_once, 0))
        refill(functools.partial(fetch_once, 1))
        for layer in order:
            gbr[layer] = hidden[...].astype(jnp.bfloat16)
            saving(layer, 3).start()
            if layer == order[0]:
                await_load(functools.partial(fetch_slope, layer))
            else:
                fetch_slope(layer, slot_of).wait()
                saving(layer + 1, 2).wait()

            wide = 2 * width

            @pl.loop(0, w_up.shape[2] // wide)
            def _(i):
                cols = pl.ds(pl.multiple_of(i * wide, LANES), wide)
                gup[:, cols] = (
                    by_rows(gbr[layer], w_down[layer, cols, :]) * slope[:, cols]
                ).astype(jnp.bfloat16)

            saving(layer, 2).start()
            if layer > 0:
                fetch_slope(layer - 1, slot_of).start()
            else:
                refill(functools.partial(fetch_slope, order[0]))
            gact[...] = by_rows(gup[...], w_up[layer])
            await_load(functools.partial(fetch, layer, 0))
            await_load(functools.partial(fetch, layer, 4))
            hidden[...] = hidden[...] + through_norm(
                nm[layer], stat[layer][:, 1:2], 2 * layer + 1
            )
            refill(functools.partial(fetch, layer, 0))
            gmid[layer] = hidden[...].astype(jnp.bfloat16)
            saving(layer, 1).start()
            gctx[...] = by_rows(gmid[layer], w_o[layer]).astype(jnp.bfloat16)
            await_load(functools.partial(fetch, layer, 1))
            await_load(functools.partial(fetch, layer, 2))
            for row in range(rows):
                toks = pl.ds(row * length, length)
                first = lane_of((length, LANES)) < HALF_LANES
                for pair in range(pairs):

                    def at(i):
                        return pl.ds(i * width + pair * LANES, LANES)

                    query = both_heads(qkv[layer, toks, at(0)], first)
                    key = qkv[layer, toks, at(1)]
                    value = qkv[layer, toks, at(2)]
                    grad = both_heads(gctx[toks, at(0)], first)
                    soft = prob[layer, row * pairs + pair]
                    grad_soft = by_rows(grad, value)
                    delta = jnp.sum(soft * grad_soft, -1, keepdims=True)
                    grad_scores = (soft * (grad_soft - delta)).astype(jnp.bfloat16)
                    factor = HEAD_DIM ** (-0.5)
                    mixed = jnp.dot(grad_scores, key, preferred_element_type=jnp.float32) * factor
                    gqkv[layer, toks, at(0)] = jnp.where(
                        first, mixed[:length], mixed[length:]
                    ).astype(jnp.bfloat16)
                    gqkv[layer, toks, at(1)] = (
                        down_columns(grad_scores, query) * factor
                    ).astype(jnp.bfloat16)
                    gqkv[layer, toks, at(2)] = down_columns(
                        soft.astype(jnp.bfloat16), grad
                    ).astype(jnp.bfloat16)

            refill(functools.partial(fetch, layer, 1))
            refill(functools.partial(fetch, layer, 2))
            saving(layer, 0).start()
            gact[...] = by_rows(gqkv[layer], w_qkv[layer])
            await_load(functools.partial(fetch, layer, 3))
            hidden[...] = hidden[...] + through_norm(na[layer], stat[layer][:, :1], 2 * layer)
            refill(functools.partial(fetch, layer, 3))
            refill(functools.partial(fetch, layer, 4))
        gstart[...] = hidden[...].astype(jnp.bfloat16)
        grad_inputs = scaled + jnp.dot(
            gstart[...], w_side[:, table : table + LANES], preferred_element_type=jnp.float32
        )
        grad_inputs = jnp.where(lane < channels, grad_inputs, 0.0)
        out_grad[turn] = grad_inputs
        for slot in (2, 3):

            @pl.when(turn == slot - 2)
            def _():
                sent[slot] = packed_pair(grad_inputs, length)
                hop(slot).start()

        ends = ((gstart, hbm_gstart), (gpred, hbm_gpred))
        for i, (src, dst) in enumerate(ends):
            pltpu.make_async_copy(src, dst.at[slot_of], end_sem.at[i]).start()
        for layer in range(layers):
            for i in range(4):
                if i != 2 or layer == 0:
                    saving(layer, i).wait()
        for i, (src, dst) in enumerate(ends):
            pltpu.make_async_copy(src, dst.at[slot_of], end_sem.at[i]).wait()

    for slot in range(4):
        hop(slot).wait_send()
    done()


def two_blocks(facts, patches, cotangent, shards, table, channels, collective_id):
    rows = facts.shape[1]
    length = TOKENS // rows
    layers, width, hidden = shards[2].shape[0] // 2, 16 * shards[2].shape[1], shards[2].shape[2]
    units = units_of(shards, 0.5)
    n = len(units)
    pairs = rows * width // LANES
    low, full = jnp.bfloat16, jnp.float32
    kept = [
        ((layers, TOKENS, width), full),
        ((layers, TOKENS, width), low),
        ((layers, TOKENS, 3 * width), low),
        ((layers, pairs, 2 * length, length), full),
        ((layers, TOKENS, width), low),
        ((layers, TOKENS, width), full),
        ((layers, TOKENS, width), low),
        ((layers, TOKENS, hidden), full),
        ((layers, TOKENS, hidden), low),
        ((layers, TOKENS, LANES), full),
        ((TOKENS, width), full),
        ((TOKENS, width), low),
        ((3, TOKENS, LANES), full),
        ((TOKENS, table + LANES), low),
        ((layers, TOKENS, 3 * width), low),
        ((layers, TOKENS, width), low),
        ((layers, TOKENS, hidden), low),
        ((layers, TOKENS, width), low),
        ((TOKENS, width), low),
        ((TOKENS, LANES), low),
    ]
    scratch = [pltpu.VMEM((layers, 16 * s.shape[1], s.shape[2]), low) for s in shards[:4]]
    scratch.append(pltpu.VMEM((width, shards[4].shape[2]), low))
    for i, (shape, kind) in enumerate(kept):
        scratch.append(pltpu.VMEM(shape[1:] if i in (7, 16) else shape, kind))
    dma = pltpu.SemaphoreType.DMA
    scratch += [
        pltpu.VMEM((TOKENS, width), full),
        pltpu.VMEM((TOKENS, LANES), full),
        pltpu.VMEM((8, width), full),
        pltpu.VMEM((TOKENS, width), full),
        pltpu.VMEM((TOKENS, width), low),
        pltpu.VMEM((4, length, LANES), full),
        pltpu.VMEM((4, length, LANES), full),
        dma((n, 27)),
        dma((n, 25)),
        dma((n,)),
        dma((layers, 10)),
        dma((4,)),
        dma((layers, 6)),
        dma((2,)),
        dma((layers, 4)),
        dma((2,)),
        dma((4,)),
        dma((4,)),
    ]
    vmem, hbm = pl.BlockSpec(memory_space=pltpu.VMEM), pl.BlockSpec(memory_space=pl.ANY)
    smem = pl.BlockSpec(memory_space=pltpu.SMEM)
    results = pl.pallas_call(
        functools.partial(blocks_kernel, (rows, length, table, channels), units),
        out_shape=[jax.ShapeDtypeStruct((3, TOKENS, LANES), full)] * 2
        + [jax.ShapeDtypeStruct((3, 8, width), full)]
        + [jax.ShapeDtypeStruct((3,) + shape, kind) for shape, kind in kept],
        in_specs=[smem] + [vmem] * 2 + [hbm] * 5,
        out_specs=[vmem] * 3 + [hbm] * len(kept),
        scratch_shapes=scratch,
        compiler_params=pltpu.CompilerParams(
            collective_id=collective_id, has_side_effects=True, vmem_limit_bytes=61 * 2**20
        ),
        name="two_blocks",
    )(facts, patches, cotangent, *shards)
    _, aa, _, _, ctx, _, am, _, gelu, _, _, af, _, start = results[3:17]
    gqkv, gmid, gup, gbr, gstart, gpred = results[17:]
    pairs = (aa, gqkv, ctx, gmid, am, gup, gelu, gbr, start, gstart, af, gpred)
    return results[:3], pairs


EARLY = (4, 8)
CORNER_SHARE = 0.7
SUM_LAGS = (0, 1, 3, 4, 6, 8)


def products_kernel(units, early, n_pairs, out_count, *refs):
    per = 2 * n_pairs
    steps, gain_grads = refs[:per], refs[per]
    outs = refs[per + 1 : per + 6]
    rest = refs[per + 6 :]
    bufs, made, turned = rest[:per], rest[per : per + 5], rest[per + 5]
    rest = rest[per + 6 :]
    n = len(units)
    acc, in_x, in_y, in_d, in_z, in_n = [rest[i * n : (i + 1) * n] for i in range(6)]
    gain_cols, in_sem, send, recv, local_out = rest[6 * n :]
    r, x, y, z, c = place()
    stage = z // 2
    other = 1 - stage
    zi = lax.rem(z, 2)
    dev_x = (r, 1 - x)
    dev_y = (r + 2 - 4 * y, x)
    dev_s = (r + 1 - 2 * c, x)
    z_dst = (z + 1 - 2 * zi, other * 2, other * 2 + 1)
    dev_z = tuple((zz * 4 + y * 2 + c, x) for zz in z_dst)
    inner = stage != zi
    side_of = jnp.where(inner, other, stage)
    z_mine, z_theirs = 2 * side_of, 2 - 2 * side_of
    barrier = pltpu.get_barrier_semaphore()
    partners = (dev_x, dev_y, dev_s) + dev_z
    for dev in partners:
        pl.semaphore_signal(barrier, 1, device_id=dev, device_id_type=MESH_ID)

    def loads(i, layer):
        copies = []
        for k, step in enumerate((1, 2 * stage)):
            src = steps[i].at[step, layer] if len(steps[i].shape) == 4 else steps[i].at[step]
            dst = bufs[i].at[pl.ds(k * TOKENS, TOKENS)]
            copies.append(pltpu.make_async_copy(src, dst, in_sem.at[layer, 2 * i + k]))
        return copies

    def fetch(i, layer):
        for copy in loads(i, layer):
            copy.start()

    def fetched(i, layer):
        for copy in loads(i, layer):
            copy.wait()

    for i in (8, 9, 10, 11):
        fetch(i, 0)
    for i in range(8):
        fetch(i, 0)
    pl.semaphore_wait(barrier, len(partners))
    started = {}

    def copy_of(u, src, dst, slot, dev, idx=None):
        return pltpu.make_async_remote_copy(
            src_ref=src,
            dst_ref=dst,
            send_sem=send.at[u, slot],
            recv_sem=recv.at[u, slot if idx is None else idx],
            device_id=dev,
            device_id_type=MESH_ID,
        )

    def push(u, src, dst, slot, dev, idx=None):
        started[u, slot] = copy_of(u, src, dst, slot, dev, idx)
        started[u, slot].start()

    def planes(u):
        return (z_mine, 2) if u in early else (0, 4)

    def arrived(u, dst, idx):
        wait_all_of(dst, recv.at[u, idx])

    def part_of(u, part):
        _, _, _, rows, half, (dim, cut) = units[u]
        if dim == 0:
            return (pl.ds(0, cut), pl.ds(0, half)) if part == 0 else (pl.ds(cut, rows - cut), pl.ds(0, half))
        return (pl.ds(0, rows), pl.ds(0, cut)) if part == 0 else (pl.ds(0, rows), pl.ds(cut, half - cut))

    block, strip = turned.shape[0], 3 * LANES

    def multiply(out, rows, right, m, begin, count, wide, extra=None):
        def one(cols, out_cols):
            product = jnp.dot(turned[...], right[:, cols], preferred_element_type=jnp.float32)
            if extra is not None:
                product = product + extra[...]
            product = product.astype(jnp.bfloat16)
            for k in range(block // rows):
                s = m * (block // rows) + k
                out[s // 4, (s // 2) % 2, s % 2, :, out_cols] = product[k * rows : (k + 1) * rows]

        if count == 1:
            one(slice(0, wide), slice(begin, begin + wide))
        else:

            @pl.loop(0, count)
            def _(i):
                cols = pl.ds(pl.multiple_of(i * wide, LANES), wide)
                one(cols, cols)

    def product(u):
        a, layer, _, rows, half, _ = units[u]
        if a == 4:
            for i in (8, 9, 10, 11):
                fetched(i, 0)
            turned[...] = bufs[9][...].T
            multiply(made[4], rows, bufs[8], 0, 0, bufs[8].shape[1] // strip, strip)
            turned[...] = bufs[10][...].T
            gains = gain_grads[1] + gain_grads[2 - 2 * stage]
            zeros = jnp.zeros((LANES, gains.shape[1]), jnp.float32)
            tall = jnp.concatenate([zeros[:out_count], gains, zeros[out_count + 8 :]], 0)
            gain_cols[...] = tall.T
            multiply(made[4], rows, bufs[11], 0, bufs[8].shape[1], 1, LANES, gain_cols)
        else:
            fetched(2 * a, layer)
            fetched(2 * a + 1, layer)
            if layer > 0:
                for h in range(2):
                    started.pop((u - 4, h)).wait_send()
            for m in range(bufs[2 * a].shape[1] // block):
                turned[...] = bufs[2 * a][:, m * block : (m + 1) * block].T
                multiply(made[a], rows, bufs[2 * a + 1], m, 0, 2 * half // strip, strip)
            if layer + 1 < units[-1][1] + 1:
                fetch(2 * a, layer + 1)
                fetch(2 * a + 1, layer + 1)
        for h in range(2):
            cols = pl.ds(h * half, half)
            push(u, made[a].at[:, :, 1 - c, :, cols], acc[u].at[:, :, h], h, dev_s)

    def chip_sum(u):
        a, layer, _, rows, half, _ = units[u]
        for h in range(2):
            arrived(u, acc[u].at[:, :, h], h)

        @pl.loop(0, 4)
        def _(zz):
            for yy in range(2):
                for h in range(2):
                    mine = made[a][zz, yy, c, :, h * half : (h + 1) * half]
                    acc[u][zz, yy, h] = acc[u][zz, yy, h] + mine

        if u in early:
            push(u, acc[u].at[pl.ds(z_theirs, 2)], in_n[u], 11, dev_z[0])
        else:
            corner(u)

    def near_sum(u):
        if u in early:
            arrived(u, in_n[u], 11)

            @pl.loop(0, 2)
            def _(i):
                for yy in range(2):
                    for h in range(2):
                        acc[u][z_mine + i, yy, h] = acc[u][z_mine + i, yy, h] + in_n[u][i, yy, h]

            corner(u)

    def corner(u):
        base, count = planes(u)
        for part, dev in ((0, dev_y), (1, dev_x)):
            rs, cs = part_of(u, part)
            src = acc[u].at[pl.ds(base, count), 1 - y, 1 - x, rs, cs]
            push(u, src, in_d[u].at[:, rs, cs], 2 + part, dev)

    def side_sum(u):
        base, count = planes(u)
        for part, yy, h, dev, into in ((0, y, 1 - x, dev_x, in_x), (1, 1 - y, x, dev_y, in_y)):
            rs, cs = part_of(u, part)
            arrived(u, in_d[u].at[:, rs, cs], 2 + part)

            @pl.loop(0, count)
            def _(i):
                zz = base + i
                acc[u][zz, yy, h, rs, cs] = acc[u][zz, yy, h, rs, cs] + in_d[u][i, rs, cs]

            push(u, acc[u].at[pl.ds(base, count), yy, h], into[u], 4 + part, dev)

    def to_near(u):
        return copy_of(u, acc[u].at[z_dst[0], y, x], in_z[u].at[0], 6, dev_z[0])

    def to_far(u, i):
        where_to = in_z[u].at[1] if u in early else in_z[u].at[1 + zi]
        idx = 7 if u in early else 7 + zi
        return copy_of(u, acc[u].at[z_dst[1 + i], y, x], where_to, 7 + i, dev_z[1 + i], idx)

    def plane_sum(u):
        arrived(u, in_x[u], 4)
        arrived(u, in_y[u], 5)
        base, count = planes(u)

        @pl.loop(0, count)
        def _(i):
            acc[u][base + i, y, x] = (
                acc[u][base + i, y, x].astype(jnp.float32)
                + in_x[u][i].astype(jnp.float32)
                + in_y[u][i].astype(jnp.float32)
            ).astype(jnp.bfloat16)

        along_z(u, "start")

    def along_z(u, what):
        if u in early:

            @pl.when(inner)
            def _():
                for i in range(2):
                    getattr(to_far(u, i), what)()

            @pl.when(jnp.logical_not(inner))
            def _():
                getattr(to_near(u), what)()
        else:
            for copy in (to_far(u, 0), to_far(u, 1), to_near(u)):
                getattr(copy, what)()

    def owned(u, b, h):
        a, layer, layers, _, half, _ = units[u]
        return outs[a].at[layers * b + layer, :, pl.ds(pl.multiple_of(h * half, LANES), half)]

    def totals(u):
        return ((acc[u].at[z, y, x], stage), (in_z[u].at[1], other))

    def total(u):
        if u in early:
            started.pop((u, 11)).wait_send()
            arrived(u, in_z[u].at[1], 7)

            @pl.when(inner)
            def _():
                arrived(u, in_z[u].at[0], 6)
                acc[u][z, y, x] = in_z[u][0]
        else:
            for j in range(3):
                arrived(u, in_z[u].at[j], 6 + j)
            acc[u][z, y, x] = acc[u][z, y, x] + in_z[u][0]
            in_z[u][1] = in_z[u][1] + in_z[u][2]
        for k, (src, b) in enumerate(totals(u)):
            push(u, src, owned(u, b, x), 9 + k, dev_x)
            pltpu.make_async_copy(src, owned(u, b, x), local_out.at[u, k]).start()

    acts = (product, chip_sum, near_sum, side_sum, plane_sum, total)
    for t in range(n + SUM_LAGS[-1]):
        for lag, act in zip(SUM_LAGS, acts):
            if 0 <= t - lag < n:
                act(t - lag)
    for u in range(n):
        for k, (src, b) in enumerate(totals(u)):
            arrived(u, owned(u, b, 1 - x), 9 + k)
            pltpu.make_async_copy(src, owned(u, b, x), local_out.at[u, k]).wait()
        along_z(u, "wait_send")
    for cp in started.values():
        cp.wait_send()


def summed_products(operands, gain_grads, out_count, shards, collective_id):
    low = jnp.bfloat16
    out = [jax.ShapeDtypeStruct(s.shape, low) for s in shards]
    units = units_of(out, CORNER_SHARE)
    n = len(units)
    layers = max(u[1] for u in units) + 1
    n_pairs = len(operands) // 2
    width = operands[0].shape[-1]
    hbm, vmem = pl.BlockSpec(memory_space=pl.ANY), pl.BlockSpec(memory_space=pltpu.VMEM)

    def slots(lead, early_lead=None):
        leads = [early_lead if i in EARLY and early_lead else lead for i in range(n)]
        return [pltpu.VMEM(some + (u[3], u[4]), low) for some, u in zip(leads, units)]

    return pl.pallas_call(
        functools.partial(products_kernel, units, EARLY, n_pairs, out_count),
        out_shape=out,
        in_specs=[hbm] * (2 * n_pairs) + [vmem],
        out_specs=[hbm] * 5,
        scratch_shapes=[
            pltpu.VMEM((2 * TOKENS, part.shape[-1]), low) for part in operands
        ]
        + [pltpu.VMEM((4, 2, 2) + s.shape[1:], low) for s in shards]
        + [pltpu.VMEM((width, 2 * TOKENS), low)]
        + slots((4, 2, 2))
        + slots((4,), (2,))
        + slots((4,), (2,))
        + slots((4,), (2,))
        + slots((3,), (2,))
        + [
            pltpu.VMEM((2, 2, 2, u[3], u[4]) if i in EARLY else (16, LANES), low)
            for i, u in enumerate(units)
        ]
        + [
            pltpu.VMEM((width, LANES), jnp.float32),
            pltpu.SemaphoreType.DMA((layers, 4 * n_pairs)),
            pltpu.SemaphoreType.DMA((n, 12)),
            pltpu.SemaphoreType.DMA((n, 12)),
            pltpu.SemaphoreType.DMA((n, 2)),
        ],
        compiler_params=pltpu.CompilerParams(
            collective_id=collective_id, has_side_effects=True, vmem_limit_bytes=62 * 2**20
        ),
        name="summed_products",
    )(*operands, gain_grads)


def dot(left, right, dims=((1,), (0,))):
    return lax.dot_general(left, right, (dims, ((), ())), preferred_element_type=jnp.float32)


def normalize(hidden):
    center = hidden - jnp.mean(hidden, -1, keepdims=True)
    inverse = lax.rsqrt(jnp.mean(center * center, -1, keepdims=True) + EPS_NORM)
    return (center * inverse, inverse)


def normalize_back(normed, inverse, grad_normed):
    mean_grad = jnp.mean(grad_normed, -1, keepdims=True)
    mean_proj = jnp.mean(grad_normed * normed, -1, keepdims=True)
    return inverse * (grad_normed - mean_grad - normed * mean_proj)


def padded(count, unit):
    return -(-count // unit) * unit


def side_columns(classes, channels, out, gains):
    table = padded(classes, LANES)
    last = table + padded(channels, LANES)
    return table, last, padded(last + out + gains, 2 * LANES)


def pack_side(w_table, w_in, w_out, gains):
    blocks, classes, shard = w_table.shape
    channels, out, gain_count = w_in.shape[1], w_out.shape[2], gains.shape[1]
    table, last, total = side_columns(classes, channels, out, gain_count)

    def gap(count):
        return jnp.zeros((blocks, shard, count), w_table.dtype)

    return jnp.concatenate(
        [
            jnp.swapaxes(w_table, 1, 2),
            gap(table - classes),
            jnp.swapaxes(w_in, 1, 2),
            gap(last - table - channels),
            w_out,
            jnp.swapaxes(gains, 1, 2),
            gap(total - last - out - gain_count),
        ],
        2,
    )


def split_side(side, classes, channels, out, gains):
    table, last, _ = side_columns(classes, channels, out, gains)
    return (
        jnp.swapaxes(side[..., :classes], -1, -2),
        jnp.swapaxes(side[..., table : table + channels], -1, -2),
        side[..., last : last + out],
        jnp.swapaxes(side[..., last + out : last + out + gains], -1, -2),
    )


def heads_of(flat, rows):
    return flat.reshape(rows, -1, HEADS, HEAD_DIM)


def attention_scores(query, key_rows, attend):
    scores = jnp.einsum(
        "rqhd,rkhd->rhqk", query, key_rows, preferred_element_type=jnp.float32
    ) * HEAD_DIM ** (-0.5)
    return jnp.where(attend[:, None], scores, MASKED)


def forward_block(inputs, seg_ids, labels, weights, sizes):
    w_qkv, w_o, w_up, w_down, side = weights
    classes, channels, out, gain_count = sizes
    table, last, _ = side_columns(*sizes)
    rows, length, _ = inputs.shape
    tokens = rows * length
    width = side.shape[0]
    places = jnp.arange(length, dtype=jnp.int32)
    attend = (seg_ids[:, :, None] == seg_ids[:, None, :]) & (
        places[None, :, None] >= places[None, None, :]
    )
    same_seg = jnp.concatenate(
        [jnp.zeros((rows, 1), bool), seg_ids[:, 1:] == seg_ids[:, :-1]], 1
    )[..., None]
    onehot = labels.reshape(tokens, 1) == jnp.arange(table)[None, :]
    start = jnp.concatenate(
        [
            onehot.astype(jnp.bfloat16),
            inputs.reshape(tokens, channels).astype(jnp.bfloat16),
            jnp.zeros((tokens, last - table - channels), jnp.bfloat16),
        ],
        1,
    )
    gain_rows = side[:, last + out : last + out + gain_count].astype(jnp.float32).T
    hidden = dot(start, side[:, :last], ((1,), (1,)))
    kept = []
    for layer in range(w_qkv.shape[0]):
        normed_a, inverse_a = normalize(hidden)
        act_a = (normed_a * gain_rows[2 * layer]).astype(jnp.bfloat16)
        qkv = dot(act_a, w_qkv[layer]).astype(jnp.bfloat16)
        query, key_rows, value_rows = [
            heads_of(qkv[:, i * width : (i + 1) * width], rows) for i in range(3)
        ]
        scores = attention_scores(query, key_rows, attend)
        row_top = jnp.max(scores, -1, keepdims=True)
        expo_rows = jnp.exp(scores - row_top)
        row_total = jnp.sum(expo_rows, -1, keepdims=True)
        soft_low = (expo_rows / row_total).astype(jnp.bfloat16)
        log_total = row_top + jnp.log(row_total)
        context = jnp.einsum(
            "rhqk,rkhd->rqhd", soft_low, value_rows, preferred_element_type=jnp.float32
        )
        context = context.reshape(tokens, width).astype(jnp.bfloat16)
        middle = hidden + dot(context, w_o[layer])
        normed_m, inverse_m = normalize(middle)
        act_m = (normed_m * gain_rows[2 * layer + 1]).astype(jnp.bfloat16)
        upper = dot(act_m, w_up[layer])
        gelu_low = jax.nn.gelu(upper, approximate=True).astype(jnp.bfloat16)
        hidden = middle + dot(gelu_low, w_down[layer])
        kept.append(
            (
                normed_a,
                inverse_a,
                act_a,
                qkv,
                log_total,
                context,
                normed_m,
                inverse_m,
                act_m,
                upper,
                gelu_low,
            )
        )
    normed_f, inverse_f = normalize(hidden)
    act_f = (normed_f * gain_rows[gain_count - 1]).astype(jnp.bfloat16)
    prediction = dot(act_f, side[:, last : last + out]).reshape(rows, length, out)
    previous = jnp.concatenate([jnp.zeros((rows, 1, out), jnp.float32), prediction[:, :-1]], 1)
    shift = jnp.where(same_seg, previous, 0.0)
    shift_alpha = shift[..., channels:]
    latent = (inputs - shift[..., :channels]) * jnp.exp(-shift_alpha)
    saved = (attend, same_seg, start, kept, normed_f, inverse_f, act_f, shift_alpha, latent)
    return (latent, -jnp.sum(shift_alpha, -1), saved)


def backward_block(grad_latent, saved, weights, sizes):
    w_qkv, w_o, w_up, w_down, side = weights
    classes, channels, out, gain_count = sizes
    table, last, _ = side_columns(*sizes)
    attend, same_seg, start, kept, normed_f, inverse_f, act_f, shift_alpha, latent = saved
    rows, length, _ = latent.shape
    tokens = rows * length
    width = side.shape[0]
    factor = HEAD_DIM ** (-0.5)
    gain_rows = side[:, last + out : last + out + gain_count].astype(jnp.float32).T
    scale_back = jnp.exp(-shift_alpha)
    grad_inputs = grad_latent * scale_back
    grad_prev = jnp.where(
        same_seg, jnp.concatenate([-grad_inputs, 1.0 - grad_latent * latent], 2), 0.0
    )
    grad_pred = jnp.concatenate([grad_prev[:, 1:], jnp.zeros((rows, 1, out), jnp.float32)], 1)
    grad_pred = grad_pred.reshape(tokens, out).astype(jnp.bfloat16)
    grad_act = dot(grad_pred, side[:, last : last + out], ((1,), (1,)))
    gain_grads = [None] * gain_count
    gain_grads[-1] = jnp.sum(grad_act * normed_f, 0)
    grad_hidden = normalize_back(normed_f, inverse_f, grad_act * gain_rows[gain_count - 1])
    pairs = [None] * w_qkv.shape[0]
    for layer in reversed(range(w_qkv.shape[0])):
        (
            normed_a,
            inverse_a,
            act_a,
            qkv,
            log_total,
            context,
            normed_m,
            inverse_m,
            act_m,
            upper,
            gelu_low,
        ) = kept[layer]
        grad_branch = grad_hidden.astype(jnp.bfloat16)
        grad_gelu = dot(grad_branch, w_down[layer], ((1,), (1,)))
        gelu_pull = jax.vjp(partial(jax.nn.gelu, approximate=True), upper)[1]
        grad_upper = gelu_pull(grad_gelu)[0].astype(jnp.bfloat16)
        grad_act_m = dot(grad_upper, w_up[layer], ((1,), (1,)))
        gain_grads[2 * layer + 1] = jnp.sum(grad_act_m * normed_m, 0)
        grad_middle = grad_hidden + normalize_back(
            normed_m, inverse_m, grad_act_m * gain_rows[2 * layer + 1]
        )
        grad_mid_low = grad_middle.astype(jnp.bfloat16)
        grad_context = heads_of(
            dot(grad_mid_low, w_o[layer], ((1,), (1,))).astype(jnp.bfloat16), rows
        )
        query, key_rows, value_rows = [
            heads_of(qkv[:, i * width : (i + 1) * width], rows) for i in range(3)
        ]
        soft_rows = jnp.exp(attention_scores(query, key_rows, attend) - log_total)
        soft_low = soft_rows.astype(jnp.bfloat16)
        grad_soft = jnp.einsum(
            "rqhd,rkhd->rhqk", grad_context, value_rows, preferred_element_type=jnp.float32
        )
        row_delta = jnp.sum(soft_rows * grad_soft, -1, keepdims=True)
        grad_scores = (soft_rows * (grad_soft - row_delta)).astype(jnp.bfloat16)
        grad_query = factor * jnp.einsum(
            "rhqk,rkhd->rqhd", grad_scores, key_rows, preferred_element_type=jnp.float32
        )
        grad_keys = factor * jnp.einsum(
            "rhqk,rqhd->rkhd", grad_scores, query, preferred_element_type=jnp.float32
        )
        grad_values = jnp.einsum(
            "rhqk,rqhd->rkhd", soft_low, grad_context, preferred_element_type=jnp.float32
        )
        grad_qkv = jnp.concatenate(
            [part.reshape(tokens, width) for part in (grad_query, grad_keys, grad_values)], 1
        ).astype(jnp.bfloat16)
        grad_act_a = dot(grad_qkv, w_qkv[layer], ((1,), (1,)))
        gain_grads[2 * layer] = jnp.sum(grad_act_a * normed_a, 0)
        grad_hidden = grad_middle + normalize_back(
            normed_a, inverse_a, grad_act_a * gain_rows[2 * layer]
        )
        pairs[layer] = (
            (act_a, grad_qkv),
            (context, grad_mid_low),
            (act_m, grad_upper),
            (gelu_low, grad_branch),
        )
    grad_start = grad_hidden.astype(jnp.bfloat16)
    grad_inputs = grad_inputs + dot(grad_start, side[:, table : table + channels]).reshape(
        rows, length, channels
    )
    return grad_inputs, (
        pairs,
        (start, grad_start),
        (act_f, grad_pred),
        jnp.stack(gain_grads, 1),
    )


def weight_grads(parts, side_total):
    pairs, (start, grad_start), (act_f, grad_pred), gain_grads = parts
    arrays = [
        jnp.stack([dot(*layer[i], ((0,), (0,))).astype(jnp.bfloat16) for layer in pairs], 0)
        for i in range(4)
    ]
    side = [
        dot(grad_start, start, ((0,), (0,))),
        dot(act_f, grad_pred, ((0,), (0,))),
        gain_grads,
    ]
    count = sum(part.shape[1] for part in side)
    side.append(jnp.zeros((gain_grads.shape[0], side_total - count), jnp.float32))
    side = jnp.concatenate(side, 1).astype(jnp.bfloat16)
    return arrays + [side[None]]


def adam_step(weight, first, second, grad, rate):
    first_new = BETA_ONE * first + (1.0 - BETA_ONE) * grad
    second_new = BETA_TWO * second + (1.0 - BETA_TWO) * grad * grad
    first_hat = first_new / (1.0 - BETA_ONE**STEP)
    second_hat = second_new / (1.0 - BETA_TWO**STEP)
    weight_new = weight - rate * (first_hat / (jnp.sqrt(second_hat) + EPS_ADAM) + DECAY * weight)
    return (first_new, second_new, weight_new)


def segment_of(places, seg_ends):
    return jnp.sum((places[None, :, None] >= seg_ends[:, None, :]).astype(jnp.int32), -1)


def row_facts(seg_lengths, class_labels, length):
    seg_ids = segment_of(jnp.arange(length, dtype=jnp.int32), jnp.cumsum(seg_lengths, 1))
    picked = seg_ids[:, :, None] == jnp.arange(SEGS)[None, None, :]
    return seg_ids, jnp.sum(jnp.where(picked, class_labels[:, None, :], 0), -1)


def pack_kernel(sizes, w_table, w_in, w_out, gains, side):
    classes, channels, out, gain_count = sizes
    table, last, _ = side_columns(*sizes)
    shard = w_out.shape[1]
    down = lax.broadcasted_iota(jnp.int32, (shard, shard), 0)
    same = (down == lane_of((shard, shard))).astype(jnp.bfloat16)
    side[...] = jnp.zeros_like(side)
    for b in range(2):

        def across(part):
            return by_rows(same, part.astype(jnp.bfloat16)).astype(jnp.bfloat16)

        side[b, :, :classes] = w_table[b].astype(jnp.bfloat16)
        side[b, :, table : table + channels] = across(w_in[b])
        side[b, :, last : last + out] = w_out[b].astype(jnp.bfloat16)
        side[b, :, last + out : last + out + gain_count] = across(gains[:, b])


def packed_side(w_table, w_in, w_out, gains, sizes):
    shape = (2, w_out.shape[1], side_columns(*sizes)[2])
    return pl.pallas_call(
        functools.partial(pack_kernel, sizes),
        out_shape=jax.ShapeDtypeStruct(shape, jnp.bfloat16),
        compiler_params=pltpu.CompilerParams(vmem_limit_bytes=32 * 2**20),
        name="pack_side",
    )(jnp.swapaxes(w_table, 1, 2), w_in, w_out, jnp.swapaxes(gains, 0, 1))


def small_updates_kernel(sizes, side, *refs):
    classes, channels, out, gain_count = sizes
    table, last, _ = side_columns(*sizes)
    args, outs = refs[:12], refs[12:]
    shard = side.shape[1]
    down = lax.broadcasted_iota(jnp.int32, (shard, shard), 0)
    same = (down == lane_of((shard, shard))).astype(jnp.bfloat16)
    for b in range(2):

        def across(begin, end):
            return down_columns(side[b, :, begin:end], same)

        tail = across(last, last + LANES)
        grads = (
            across(table, table + LANES)[:channels],
            side[b, :, :classes].astype(jnp.float32),
            side[b, :, last : last + LANES].astype(jnp.float32)[:, :out],
            tail[out : out + gain_count],
        )
        rates = (RATES[0], RATES[1], RATES[6], RATES[7])
        for i in range(4):
            at = (slice(None), b) if i == 3 else (b,)
            now = [ref[at] for ref in args[3 * i : 3 * i + 3]]
            for ref, value in zip(outs[3 * i : 3 * i + 3], adam_step(*now, grads[i], rates[i])):
                ref[at] = value


def small_updates(side, groups, sizes):
    turns = ((0, 0), (1, 2), (0, 0), (0, 1))
    arrays = [jnp.swapaxes(part, *turn) for turn, group in zip(turns, groups) for part in group]
    results = pl.pallas_call(
        functools.partial(small_updates_kernel, sizes),
        out_shape=[jax.ShapeDtypeStruct(part.shape, part.dtype) for part in arrays],
        compiler_params=pltpu.CompilerParams(vmem_limit_bytes=48 * 2**20),
        name="small_updates",
    )(side, *arrays)
    return [jnp.swapaxes(part, *turns[i // 3]) for i, part in enumerate(results)]


def staged(patches, seg_lengths, class_labels, cotangent, low, sizes):
    half = lax.axis_size("rows") // 2
    second = lax.axis_index("rows") >= half
    x = lax.axis_index("seq")
    swap = [(i, (i + half) % (2 * half)) for i in range(2 * half)]
    beside = [(0, 1), (1, 0)]
    both = ("rows", "seq")
    across = [(2 * i + s, 2 * j + 1 - s) for i, j in swap for s in range(2)]
    classes, channels, out, gain_count = sizes
    table, last, _ = side_columns(*sizes)
    held, group, _ = patches.shape
    rows, length = held // 2, 2 * group

    pieces = jnp.concatenate([patches.astype(jnp.float32), cotangent], 2)
    pieces = jnp.pad(pieces, ((0, 0), (0, 0), (0, LANES - 2 * channels)))
    pieces = pieces.reshape(2, rows, group, LANES)
    keep = lax.dynamic_index_in_dim(pieces, x, 0, keepdims=False)
    give = lax.dynamic_index_in_dim(pieces, 1 - x, 0, keepdims=False)
    got = lax.ppermute(give, "seq", beside)
    mine = jnp.where(
        x == 0, jnp.concatenate([keep, got], 1), jnp.concatenate([got, keep], 1)
    ).reshape(TOKENS, LANES)
    theirs = lax.ppermute(mine, "rows", swap)
    facts = jnp.concatenate(
        [jnp.cumsum(seg_lengths, 1), class_labels, jnp.full((held, 1), length, jnp.int32)], 1
    )
    facts = lax.dynamic_slice_in_dim(facts, x * rows, rows, 0)
    their_facts = lax.ppermute(facts, "rows", swap)
    facts = jnp.where(
        second, jnp.stack([their_facts, facts], 0), jnp.stack([facts, their_facts], 0)
    )
    batches = jnp.where(second, jnp.stack([theirs, mine], 0), jnp.stack([mine, theirs], 0))
    batches, facts, low = lax.optimization_barrier((batches, facts, low))
    lane = jnp.arange(LANES) < channels
    inputs = jnp.where(lane, batches, 0.0)
    cotangent = jnp.where(lane, jnp.roll(batches, -channels, 2), 0.0)
    (latents, grad_inputs, gain_grads), pairs = two_blocks(
        facts, inputs, cotangent, low, table, channels, 1
    )

    def halves(part):
        part = part.reshape(rows, 2, group, LANES)
        ours = lax.dynamic_index_in_dim(part, x, 1, keepdims=False)
        return ours, lax.dynamic_index_in_dim(part, 1 - x, 1, keepdims=False)

    def in_order(ours, beside_us):
        return jnp.where(
            x == 0, jnp.concatenate([ours, beside_us], 0), jnp.concatenate([beside_us, ours], 0)
        )

    own = halves(jnp.where(second, latents[2], grad_inputs[2]))
    away = halves(jnp.where(second, latents[1], grad_inputs[1]))
    own_side = lax.ppermute(own[1], "seq", beside)
    away_here = lax.ppermute(away[0], "rows", swap)
    away_side = lax.ppermute(away[1], both, across)
    sums = summed_products(pairs, gain_grads, out, low, 2)
    ours, others = in_order(own[0], own_side), in_order(away_here, away_side)
    outcome = jnp.where(second, ours, others)
    patch_grad = jnp.where(second, others, ours)
    return outcome[..., :channels], outcome[..., channels], patch_grad[..., :channels], sums


def unstaged(mine, low, sizes):
    inputs, cotangent, seg_ids, labels = mine
    whole = [lax.all_gather(part, "rows", axis=1, tiled=True) for part in low]

    def block(index):
        picked = [part[index * LAYERS : (index + 1) * LAYERS] for part in whole[:4]]
        return picked + [whole[4][index]]

    back = seg_ids[:, ::-1], labels[:, ::-1]
    latent_one, det_one, saved_one = forward_block(inputs, seg_ids, labels, block(0), sizes)
    latent_two, det_two, saved_two = forward_block(latent_one[:, ::-1], *back, block(1), sizes)
    outcome = jnp.concatenate([latent_two, (det_two + det_one[:, ::-1])[..., None]], 2)
    grad_mid, parts_two = backward_block(cotangent, saved_two, block(1), sizes)
    patch_grad, parts_one = backward_block(grad_mid[:, ::-1], saved_one, block(0), sizes)
    grads = [
        jnp.concatenate(pair, 0)
        for pair in zip(
            weight_grads(parts_one, low[4].shape[2]), weight_grads(parts_two, low[4].shape[2])
        )
    ]
    sums = [
        lax.psum(
            lax.psum_scatter(grad, "rows", scatter_dimension=1, tiled=True).astype(jnp.float32),
            "seq",
        )
        for grad in grads
    ]
    return outcome, patch_grad, sums


def body(
    patches,
    seg_lengths,
    class_labels,
    cotangent,
    w_in,
    m_in,
    v_in,
    w_table,
    m_table,
    v_table,
    w_qkv,
    m_qkv,
    v_qkv,
    w_o,
    m_o,
    v_o,
    w_up,
    m_up,
    v_up,
    w_down,
    m_down,
    v_down,
    w_out,
    m_out,
    v_out,
    gains,
    m_gains,
    v_gains,
):
    masters = (w_in, w_table, w_qkv, w_o, w_up, w_down, w_out, gains)
    firsts = (m_in, m_table, m_qkv, m_o, m_up, m_down, m_out, m_gains)
    seconds = (v_in, v_table, v_qkv, v_o, v_up, v_down, v_out, v_gains)
    sizes = (w_table.shape[1], w_in.shape[1], w_out.shape[2], gains.shape[1])
    shards = [weight.astype(jnp.bfloat16) for weight in masters[2:6]]
    held, group, channels = patches.shape
    seq_count = lax.axis_size("seq")
    length = group * seq_count
    groups = list(zip(masters, firsts, seconds))
    fits = held == 4 and group * held == TOKENS and sizes[2] == 2 * channels and sizes[2] % 8 == 0
    if seq_count == 2 and lax.axis_size("rows") == 16 and fits:
        shards.append(packed_side(w_table, w_in, w_out, gains, sizes))
        latents, logdet, patch_grad, sums = staged(
            patches, seg_lengths, class_labels, cotangent, shards, sizes
        )
        small = small_updates(sums[4], [groups[i] for i in (0, 1, 6, 7)], sizes)
        updates = [None] * 8
        for i, where_at in enumerate((0, 1, 6, 7)):
            updates[where_at] = small[3 * i : 3 * i + 3]
        for i, where_at in enumerate((2, 3, 4, 5)):
            updates[where_at] = adam_step(
                *groups[where_at], sums[i].astype(jnp.float32), RATES[where_at]
            )
        results = (latents, logdet, patch_grad)
    else:
        small = [masters[i].astype(jnp.bfloat16) for i in (1, 0, 6, 7)]
        shards.append(pack_side(*small))
        share = max(1, held // seq_count)
        copies = seq_count * share // held
        first_row = (lax.axis_index("seq") // copies) * share
        pieces = jnp.concatenate([patches.astype(jnp.float32), cotangent], 2)
        pieces = lax.all_gather(pieces, "seq", axis=1, tiled=True)
        pieces = lax.dynamic_slice_in_dim(pieces, first_row, share, 0)
        seg_ids, labels = row_facts(
            lax.dynamic_slice_in_dim(seg_lengths, first_row, share, 0),
            lax.dynamic_slice_in_dim(class_labels, first_row, share, 0),
            length,
        )
        mine = (pieces[..., :channels], pieces[..., channels:], seg_ids, labels)
        outcome, patch_grad, sums = unstaged(mine, shards, sizes)
        results = lax.all_gather(jnp.concatenate([outcome, patch_grad], 2), "seq", axis=0)
        results = results[::copies].reshape((held,) + results.shape[2:])
        results = lax.dynamic_slice_in_dim(results, lax.axis_index("seq") * group, group, 1)
        results = (
            results[..., :channels],
            results[..., channels],
            results[..., channels + 1 :],
        )
        sums = [total.astype(jnp.float32) / copies for total in sums]
        table, first, last, gain = split_side(sums[4], *sizes)
        grads = (first, table, sums[0], sums[1], sums[2], sums[3], last, gain)
        updates = [adam_step(*item) for item in zip(masters, firsts, seconds, grads, RATES)]
    return results + tuple(part for update in updates for part in update)


def solution(mesh):
    tokens = P("rows", "seq", None)
    row = P("rows", None)
    last, middle = P(None, None, "rows"), P(None, "rows", None)
    weights = (last,) * 6 + (middle,) * 15 + (last,) * 3
    return jax.shard_map(
        body,
        mesh=mesh,
        in_specs=(tokens, row, row, tokens) + weights,
        out_specs=(tokens, P("rows", "seq"), tokens) + weights,
        check_vma=False,
    )
```
